32 devices in a mesh: seq: 16 (over z, y, x), tp: 2 (over core).
Axes of the slice: x: 2, y: 2, z: 4, core: 2. Of those that a mesh axis runs over, the one named last changes fastest.
Arguments:
- layer_input: bfloat16 [4096, 768], P('seq'), may hold values from -6 to 6
- mixer_gain: float32 [768], replicated, may hold values from 0.1 to 1.9
- in_proj: bfloat16 [192, 3, 768], replicated, may hold values from -0.4375 to 0.4375
- short_taps: float32 [3, 3, 768], replicated, may hold values from -3 to 3
- filter_w1: float32 [5, 128], replicated, may hold values from -2.5 to 2.5
- filter_b1: float32 [128], replicated, may hold values from -3.140625 to 3.140625
- filter_w2: float32 [128, 128], replicated, may hold values from -0.5 to 0.5
- filter_w3: float32 [128, 768], P(None, 'seq'), may hold values from -0.015625 to 0.015625
- filter_decay: float32 [768], P('seq'), may hold values from 0.5 to 128
- out_proj: bfloat16 [192, 768], replicated, may hold values from -0.4375 to 0.4375
- glu_gain: float32 [768], replicated, may hold values from 0.1 to 1.9
- glu_in: bfloat16 [4, 192, 2, 768], P(None, None, None, 'tp'), may hold values from -0.4375 to 0.4375
- glu_out: bfloat16 [768, 768], P('tp'), may hold values from -0.21875 to 0.21875
- out_grad: bfloat16 [4096, 768], P(('seq', 'tp')), may hold values from -6 to 6
Outputs:
- layer_output: bfloat16 [4096, 768], P(('seq', 'tp'))
- input_grad: bfloat16 [4096, 768], P('seq')
- mixer_gain_grad: float32 [768], replicated
- in_proj_grad: float32 [192, 3, 768], replicated
- short_taps_grad: float32 [3, 3, 768], replicated
- filter_w1_grad: float32 [5, 128], replicated
- filter_b1_grad: float32 [128], replicated
- filter_w2_grad: float32 [128, 128], replicated
- filter_w3_grad: float32 [128, 768], P(None, 'seq')
- out_proj_grad: float32 [192, 768], replicated
- glu_gain_grad: float32 [768], replicated
- glu_in_grad: float32 [4, 192, 2, 768], P(None, None, None, 'tp')
- glu_out_grad: float32 [768, 768], P('tp')
The draws below stay inside these ranges and needn't reach their ends.
All inputs are finite; a program needn't handle non-finite values.
Results may differ from the reference program's by a relative error of at most 0.012.
Values may be sent and summed in bfloat16 or wider, within the bound.
No kernel may reach another device: no remote copies, remote signals or barrier semaphores. Data moves between devices by JAX's collectives and lax.ppermute only.
A program may use at most 128 MiB of HBM per device.

```python
import math
import jax
import jax.numpy as jnp
from jax import lax

D = 768
NBLK = 4
ORDER = 128
EMB = 5
TOKENS = 4096
SEQ_LEN = 4096
SEQS = 1
BW = 192
FFB = 768


def shard_levels(stream_key, extent, cuts, low, largest):
    level = 1.0
    for dim, shards_of in cuts:
        heights = jax.random.uniform(jax.random.fold_in(jax.random.fold_in(stream_key, 6), dim), (shards_of,), jnp.float32, low / len(cuts), largest / len(cuts))
        level = level * jnp.repeat(jnp.exp(heights), extent[dim] // shards_of).reshape((-1,) + (1,) * (len(extent) - 1 - dim))
    return level


def centred(rng, dims, scale, limit, shards=(), kind=jnp.bfloat16):
    drawn = jax.random.normal(rng, dims, jnp.float32) * scale
    if len(shards) > 0:
        drawn = shard_levels(rng, dims, shards, -0.22, 0.18) * drawn
    return jnp.clip(drawn, min=-limit, max=limit).astype(kind)


def setup_inputs(seed: int = 0) -> dict:
    streams_of = jax.random.split(jax.random.key(seed), 15)
    return {
        "layer_input": centred(streams_of[0], (TOKENS, D), 1.0, 6.0, ((0, 16),)),
        "mixer_gain": jnp.clip(1.0 + 0.18 * jax.random.normal(streams_of[1], (D,), jnp.float32), 0.1, 1.9),
        "in_proj": centred(streams_of[2], (BW, 3, D), BW ** -0.5, 0.4375),
        "short_taps": centred(streams_of[3], (3, 3, D), 0.6, 3.0, (), jnp.float32),
        "filter_w1": centred(streams_of[4], (EMB, ORDER), EMB ** -0.5, 2.5, (), jnp.float32),
        "filter_b1": jnp.clip(jax.random.uniform(streams_of[5], (ORDER,), jnp.float32, -3.140625, 3.140625), -3.140625, 3.140625),
        "filter_w2": centred(streams_of[6], (ORDER, ORDER), ORDER ** -0.5, 0.5, (), jnp.float32),
        "filter_w3": centred(streams_of[7], (ORDER, D), (ORDER * SEQ_LEN // 4) ** -0.5, 0.015625, ((1, 16),), jnp.float32),
        "filter_decay": jnp.clip(jnp.exp(math.log(128.0) - 5.5451774 * jax.random.uniform(streams_of[8], (D,), jnp.float32) ** shard_levels(streams_of[8], (D,), ((0, 16),), -0.2, 0.2)), 0.5, 128.0),
        "out_proj": centred(streams_of[9], (BW, D), BW ** -0.5, 0.4375),
        "glu_gain": jnp.clip(1.0 + 0.18 * jax.random.normal(streams_of[10], (D,), jnp.float32), 0.1, 1.9),
        "glu_in": centred(streams_of[11], (NBLK, BW, 2, FFB), BW ** -0.5, 0.4375, ((3, 2),)),
        "glu_out": centred(streams_of[12], (FFB, D), FFB ** -0.5, 0.21875, ((0, 2),)),
        "out_grad": centred(streams_of[13], (TOKENS, D), 1.0, 6.0, ((0, 32),)),
    }


@jax.custom_vjp
def low(v):
    return lax.optimization_barrier(v.astype(jnp.bfloat16)).astype(jnp.float32)

@jax.custom_vjp
def low_back(v):
    return v

def low_keep(v):
    return (low(v), None)

def low_pass(kept, grad):
    return (grad,)

def back_keep(v):
    return (v, None)

def back_low(kept, grad):
    return (low(grad),)
low.defvjp(low_keep, low_pass)
low_back.defvjp(back_keep, back_low)
EXACT_PRODUCT = lax.Precision.HIGHEST
EPSILON = 1e-05

def layer_normed(values, gain):
    centered = values - lax.optimization_barrier(jnp.mean(values, axis=-1, keepdims=True))
    variance = lax.optimization_barrier(jnp.mean(centered * centered, axis=-1, keepdims=True))
    return centered * lax.rsqrt(variance + EPSILON) * gain

def gated_units(gate_part, up_part):
    return jax.nn.gelu(gate_part, approximate=False) * up_part

def filter_taps(weight_first, bias_first, weight_second, weight_third, decay_rates, seq_length):
    period = 2 * seq_length
    step_index = jnp.arange(period, dtype=jnp.int32)
    lag_steps = jnp.where(step_index < seq_length, step_index, step_index - period).astype(jnp.float32)
    position = lag_steps / seq_length
    columns = [position]
    band_count = (EMB - 1) // 2
    for band_index in range(1, band_count + 1):
        columns.append(jnp.cos(2.0 * math.pi * band_index * position))
    for band_index in range(1, band_count + 1):
        columns.append(jnp.sin(2.0 * math.pi * band_index * position))
    features = jnp.stack(columns, axis=1)
    hidden_first = jnp.sin(jnp.dot(features, weight_first, precision=EXACT_PRODUCT) + bias_first)
    hidden_second = jnp.sin(jnp.dot(hidden_first, weight_second, precision=EXACT_PRODUCT))
    shaped = jnp.dot(hidden_second, weight_third, precision=EXACT_PRODUCT)
    return shaped * jnp.exp(-jnp.abs(lag_steps)[:, None] * decay_rates[None, :] / seq_length)

def forward(input_rows, mixer_gain, in_proj, short_taps, filter_w1, filter_b1, filter_w2, filter_w3, out_proj, glu_gain, glu_in, glu_out, filter_decay):
    period = 2 * SEQ_LEN
    lag_filter = filter_taps(filter_w1, filter_b1, filter_w2, filter_w3, filter_decay, SEQ_LEN)
    filter_spec = jnp.fft.rfft(lag_filter, axis=0)
    in_blocks = in_proj.reshape(BW, 3, NBLK, BW)
    out_blocks = out_proj.reshape(BW, NBLK, BW)
    down_blocks = glu_out.reshape(FFB, NBLK, BW)

    def one_sequence(sequence_rows):
        normed_one = low(layer_normed(sequence_rows, mixer_gain))
        projected = jnp.einsum('tbi,isbo->tsbo', normed_one.reshape(SEQ_LEN, NBLK, BW), in_blocks, precision=EXACT_PRODUCT).reshape(SEQ_LEN, 3, D)
        projected = low_back(low(projected))
        padded = jnp.concatenate([jnp.zeros((2, 3, D), jnp.float32), projected], axis=0)
        short_mixed = short_taps[0] * projected + short_taps[1] * padded[1:SEQ_LEN + 1] + short_taps[2] * padded[:SEQ_LEN]
        conv_input = low_back(low(short_mixed[:, 0] * short_mixed[:, 1]))
        spectrum = jnp.fft.rfft(conv_input, n=period, axis=0)
        conv_out = low_back(low(jnp.fft.irfft(spectrum * filter_spec, n=period, axis=0)[:SEQ_LEN]))
        gated_rows = low(short_mixed[:, 2] * conv_out)
        branch = low_back(jnp.einsum('tbi,ibo->tbo', gated_rows.reshape(SEQ_LEN, NBLK, BW), out_blocks, precision=EXACT_PRODUCT).reshape(SEQ_LEN, D))
        middle = sequence_rows + branch
        normed_two = low(layer_normed(middle, glu_gain))
        gate_up = low_back(jnp.einsum('tbi,bisf->tsbf', normed_two.reshape(SEQ_LEN, NBLK, BW), glu_in, precision=EXACT_PRODUCT))
        hidden = low(gated_units(gate_up[:, 0], gate_up[:, 1]))
        down_out = jnp.einsum('tbf,fbo->tbo', hidden, down_blocks, precision=EXACT_PRODUCT).reshape(SEQ_LEN, D)
        return middle + down_out
    stacked = input_rows.reshape(SEQS, SEQ_LEN, D)
    return lax.map(jax.checkpoint(one_sequence), stacked).reshape(TOKENS, D)

def reference(layer_input, mixer_gain, in_proj, short_taps, filter_w1, filter_b1, filter_w2, filter_w3, filter_decay, out_proj, glu_gain, glu_in, glu_out, out_grad):

    def whole_layer(input_rows, gain_one, in_weights, short_weights, weight_first, bias_first, weight_second, weight_third, out_weights, gain_two, glu_first, glu_second):
        return forward(input_rows, gain_one, in_weights, short_weights, weight_first, bias_first, weight_second, weight_third, out_weights, gain_two, glu_first, glu_second, filter_decay)
    result, pullback = jax.vjp(whole_layer, layer_input.astype(jnp.float32), mixer_gain, in_proj.astype(jnp.float32), short_taps, filter_w1, filter_b1, filter_w2, filter_w3, out_proj.astype(jnp.float32), glu_gain, glu_in.astype(jnp.float32), glu_out.astype(jnp.float32))
    gradients = pullback(out_grad.astype(jnp.float32))
    return (result.astype(jnp.bfloat16), gradients[0].astype(jnp.bfloat16), gradients[1], gradients[2], gradients[3], gradients[4], gradients[5], gradients[6], gradients[7], gradients[8], gradients[9], gradients[10], gradients[11])
```

```python
import math
import functools

import jax
import jax.numpy as jnp
import ml_dtypes
import numpy as np
from jax import lax
from jax.experimental import pallas as pl
from jax.experimental.pallas import tpu as pltpu
from jax.sharding import PartitionSpec as P

MIN_LEN = 8192
EPSILON = 1e-05
LANES = 128
GROUP = 8
VMEM_BYTES = 60 * 1024 * 1024
BF = jnp.bfloat16
F32 = jnp.float32

PI_HIGH = 3.140625
PI_LOW = 9.67653589793e-4
SIN_C = (1.0, -0.16666647791862488, 0.00833289884030819, -0.0001980081869987771, 2.590327312645968e-06)
COS_C = (0.9999999403953552, -0.4999990463256836, 0.041663575917482376, -0.0013853635173290968, 2.315232813998591e-05)


def vmem_specs(count):
    return [pl.BlockSpec(memory_space=pltpu.VMEM)] * count


def params(flops=0):
    return pltpu.CompilerParams(vmem_limit_bytes=VMEM_BYTES)


def cost(flops, bytes_accessed=0, transcendentals=0):
    return pl.CostEstimate(flops=flops, bytes_accessed=bytes_accessed, transcendentals=transcendentals)


def split_np(table):
    high = np.asarray(table, np.float32).astype(ml_dtypes.bfloat16)
    low = (np.asarray(table, np.float64) - high.astype(np.float64)).astype(ml_dtypes.bfloat16)
    return high, low


def split3_np(table):
    table = np.asarray(table, np.float64)
    high = table.astype(np.float32).astype(ml_dtypes.bfloat16)
    rest = table - high.astype(np.float64)
    mid = rest.astype(np.float32).astype(ml_dtypes.bfloat16)
    low = (rest - mid.astype(np.float64)).astype(np.float32).astype(ml_dtypes.bfloat16)
    return high, mid, low


@functools.lru_cache(maxsize=None)
def transform_tables(seq_length):
    period = 2 * seq_length
    first = period // LANES
    kept = first // 2 + 1
    padded = -(-kept // 8) * 8
    k = np.arange(padded)
    live = (k < kept).astype(np.float64)
    n = np.arange(first)
    angle = 2 * np.pi / first * ((k[:, None] * n[None, :]) % first)
    eye = np.eye(GROUP)
    stage = np.zeros((GROUP, 2, padded, first, GROUP))
    stage[:, 0] = np.einsum("kn,cd->cknd", np.cos(angle) * live[:, None], eye)
    stage[:, 1] = np.einsum("kn,cd->cknd", -np.sin(angle) * live[:, None], eye)
    forward = stage.reshape(GROUP * 2 * padded, first * GROUP)
    backward = forward.T
    m = np.arange(LANES)
    turn = 2 * np.pi / period * ((k[:, None] * m[None, :]) % period)
    weight = np.where((k == 0) | (k == first // 2), 1.0, 2.0) * live / period
    twiddle = np.stack(
        [np.cos(turn), np.sin(turn), np.cos(turn) * weight[:, None], np.sin(turn) * weight[:, None]]
    ).astype(np.float32)
    inner = 2 * np.pi / LANES * ((m[:, None] * m[None, :]) % LANES)
    c, s = np.cos(inner), np.sin(inner)
    second = np.block([[c, -s], [s, c]])
    return {
        "forward": split_np(forward),
        "backward": split_np(backward),
        "twiddle": twiddle,
        "second": split_np(second),
        "inverse": split_np(second.T),
        "first": first,
        "padded": padded,
    }


@functools.lru_cache(maxsize=None)
def feature_table(seq_length):
    period = 2 * seq_length
    index = np.arange(period)
    lag = np.where(index < seq_length, index, index - period)
    q = lag / seq_length
    rows = [q, np.cos(2 * np.pi * q), np.cos(4 * np.pi * q), np.sin(2 * np.pi * q), np.sin(4 * np.pi * q)]
    rows.append(np.ones_like(q))
    rows += [np.zeros_like(q)] * 2
    high, mid, low = split3_np(np.stack(rows))
    return np.concatenate([high, high, mid, high, mid, low], axis=0)


def split(values):
    high = values.astype(BF)
    low = (values - high.astype(F32)).astype(BF)
    return high, low


def first_weights(rows):
    high = rows.astype(BF).astype(F32)
    mid = (rows - high).astype(BF).astype(F32)
    low = rows - high - mid
    return jnp.concatenate([high, mid, high, low, mid, high], axis=0).astype(BF)


def mm(a, b):
    return jnp.dot(a, b, preferred_element_type=F32)


def mm_nt(a, b):
    return lax.dot_general(a, b, (((1,), (1,)), ((), ())), preferred_element_type=F32)


def mm_tn(a, b):
    return lax.dot_general(a, b, (((0,), (0,)), ((), ())), preferred_element_type=F32)


def mm3(a, b):
    ah, al = a
    bh, bl = b
    return mm(ah, bh) + (mm(al, bh) + mm(ah, bl))


def mm3_tn(a, b):
    ah, al = a
    bh, bl = b
    return mm_tn(ah, bh) + (mm_tn(al, bh) + mm_tn(ah, bl))


def sine_cosine(x):
    n = jnp.round(x * (1.0 / math.pi))
    r = (x - n * PI_HIGH) - n * PI_LOW
    half = n * 0.5
    sign = 1.0 - 4.0 * (half - jnp.floor(half))
    r2 = r * r
    s = SIN_C[4]
    for c in SIN_C[3::-1]:
        s = s * r2 + c
    k = COS_C[4]
    for c in COS_C[3::-1]:
        k = k * r2 + c
    return s * (r * sign), k * sign


def lag_decay(decay, start, width, seq_length):
    lane = lax.broadcasted_iota(jnp.int32, decay.shape[:1] + (width,), 1) + start
    lag = jnp.where(lane < seq_length, lane, 2 * seq_length - lane).astype(F32)
    return jnp.exp(lag * (decay[:, :1] * (-1.0 / seq_length)))


def filter_forward_kernel(seq_length, feat_ref, w1_ref, w2_ref, w3_ref, decay_ref, lag_ref, a_ref, ac_ref, b_ref, bc_ref):
    width = feat_ref.shape[1]
    start = pl.program_id(0) * width
    pre = mm_tn(first_weights(w1_ref[...]), feat_ref[...])
    s1, c1 = sine_cosine(pre)
    a_ref[...] = s1.astype(BF)
    ac_ref[...] = c1.astype(BF)
    pre2 = mm3_tn(split(w2_ref[...]), split(s1))
    s2, c2 = sine_cosine(pre2)
    b_ref[...] = s2.astype(BF)
    bc_ref[...] = c2.astype(BF)
    shaped = mm3(split(w3_ref[...]), split(s2))
    lag_ref[...] = shaped * lag_decay(decay_ref[...], start, width, seq_length)


def filter_forward(features, w1b, w2, w3t, decay, seq_length):
    hidden = w2.shape[0]
    channels = w3t.shape[0]
    period = features.shape[1]
    width = 1024
    whole = lambda a: pl.BlockSpec(a.shape, lambda i: (0, 0))
    lanes = lambda rows: pl.BlockSpec((rows, width), lambda i: (0, i))
    return pl.pallas_call(
        functools.partial(filter_forward_kernel, seq_length),
        grid=(period // width,),
        in_specs=[lanes(features.shape[0]), whole(w1b), whole(w2), whole(w3t), whole(decay)],
        out_specs=[lanes(channels)] + [lanes(hidden)] * 4,
        out_shape=[jax.ShapeDtypeStruct((channels, period), F32)]
        + [jax.ShapeDtypeStruct((hidden, period), BF)] * 4,
        compiler_params=params(),
        cost_estimate=cost(2 * period * hidden * (hidden * 3 + 48 + 72), 4 * period * hidden * 2, 0),
        name="filter_forward",
    )(features, w1b, w2, w3t, decay)


def filter_backward_kernel(seq_length, grad_ref, feat_ref, w2_ref, w3_ref, decay_ref, a_ref, ac_ref, b_ref, bc_ref, g1_ref, g2_ref, g3_ref):
    width = grad_ref.shape[1]
    step = pl.program_id(0)

    @pl.when(step == 0)
    def _():
        g1_ref[...] = jnp.zeros_like(g1_ref)
        g2_ref[...] = jnp.zeros_like(g2_ref)
        g3_ref[...] = jnp.zeros_like(g3_ref)

    weighted = grad_ref[...] * lag_decay(decay_ref[...], step * width, width, seq_length)
    wh, wl = split(weighted)
    second = b_ref[...]
    g3_ref[...] += mm_nt(wh, second) + mm_nt(wl, second)
    pre2 = mm3_tn(split(w3_ref[...]), (wh, wl)) * bc_ref[...].astype(F32)
    ph, plow = split(pre2)
    first = a_ref[...]
    g2_ref[...] += mm_nt(first, ph) + mm_nt(first, plow)
    pre1 = mm3(split(w2_ref[...]), (ph, plow)) * ac_ref[...].astype(F32)
    qh, ql = split(pre1)
    feat = feat_ref[...]
    g1_ref[...] += mm_nt(feat, qh) + mm_nt(feat, ql)


def filter_backward(grad, features, w2, w3t, decay, saved, seq_length):
    hidden = w2.shape[0]
    channels, period = grad.shape
    width = 1024
    whole = lambda a: pl.BlockSpec(a.shape, lambda i: (0, 0))
    lanes = lambda rows: pl.BlockSpec((rows, width), lambda i: (0, i))
    out = lambda r, c: pl.BlockSpec((r, c), lambda i: (0, 0))
    return pl.pallas_call(
        functools.partial(filter_backward_kernel, seq_length),
        grid=(period // width,),
        in_specs=[lanes(channels), lanes(8), whole(w2), whole(w3t), whole(decay)] + [lanes(hidden)] * 4,
        out_specs=[out(8, hidden), out(hidden, hidden), out(channels, hidden)],
        out_shape=[
            jax.ShapeDtypeStruct((8, hidden), F32),
            jax.ShapeDtypeStruct((hidden, hidden), F32),
            jax.ShapeDtypeStruct((channels, hidden), F32),
        ],
        compiler_params=params(),
        cost_estimate=cost(2 * period * hidden * (hidden * 5 + 200), 4 * period * hidden * 2, 0),
        name="filter_backward",
    )(grad, features, w2, w3t, decay, *saved)


def spectrum_of(x_pair, fwd, twiddle_ref, second, padded, columns):
    if x_pair[1] is None:
        a = mm(fwd[0], x_pair[0]) + mm(fwd[1], x_pair[0])
    else:
        a = mm3(fwd, x_pair)
    tc, ts = twiddle_ref[0], twiddle_ref[1]
    parts = []
    for col in range(columns):
        lanes = slice(col * LANES, (col + 1) * LANES)
        for c in range(GROUP):
            base = c * 2 * padded
            re = a[base : base + padded, lanes]
            im = a[base + padded : base + 2 * padded, lanes]
            parts.append(jnp.concatenate([re * tc + im * ts, im * tc - re * ts], axis=1))
    return mm3(split(jnp.concatenate(parts, axis=0)), second)


def signal_of(spec, inverse, twiddle_ref, back, padded, columns):
    b = mm3(split(spec), inverse)
    tc, ts = twiddle_ref[2], twiddle_ref[3]
    cols = []
    for col in range(columns):
        parts = []
        for c in range(GROUP):
            base = (col * GROUP + c) * padded
            re = b[base : base + padded, :LANES]
            im = b[base : base + padded, LANES:]
            parts.append(re * tc - im * ts)
            parts.append(im * tc + re * ts)
        cols.append(jnp.concatenate(parts, axis=0))
    z = jnp.concatenate(cols, axis=1)
    return mm3(back, split(z))


def gathered(x_ref, seqs, rows, groups):
    cols = []
    for q in range(seqs):
        for g in range(groups):
            block = x_ref[q * rows : (q + 1) * rows, g * GROUP : (g + 1) * GROUP, :].astype(F32)
            cols.append(block.reshape(rows * GROUP, LANES))
    return jnp.concatenate(cols, axis=1)


def scattered(y_ref, y, seqs, rows, groups):
    for q in range(seqs):
        for g in range(groups):
            col = q * groups + g
            block = y[:, col * LANES : (col + 1) * LANES].reshape(rows, GROUP, LANES)
            y_ref[q * rows : (q + 1) * rows, g * GROUP : (g + 1) * GROUP, :] = block.astype(y_ref.dtype)


def product(a, b, conjugate):
    ar, ai = a[:, :LANES], a[:, LANES:]
    br, bi = b[:, :LANES], b[:, LANES:]
    if conjugate:
        return jnp.concatenate([ar * br + ai * bi, ai * br - ar * bi], axis=1)
    return jnp.concatenate([ar * br - ai * bi, ar * bi + ai * br], axis=1)


def filter_spectrum_kernel(padded, lag_ref, fh, fl, tw, sh, sl, out_ref):
    groups = lag_ref.shape[0] // GROUP
    first = lag_ref.shape[1] // LANES
    cols = []
    for g in range(groups):
        rows = [lag_ref[g * GROUP : (g + 1) * GROUP, n * LANES : (n + 1) * LANES] for n in range(first)]
        cols.append(jnp.concatenate(rows, axis=0))
    x = jnp.concatenate(cols, axis=1)
    out_ref[...] = spectrum_of(split(x), (fh[...], fl[...]), tw, (sh[...], sl[...]), padded, groups)


def conv_forward_kernel(padded, seqs, x_ref, h_ref, fh, fl, tw, sh, sl, ih, il, bh, bl, y_ref, spec_ref):
    rows = x_ref.shape[0] // seqs
    groups = x_ref.shape[1] // GROUP
    used = rows * GROUP
    x = gathered(x_ref, seqs, rows, groups).astype(BF)
    spec = spectrum_of((x, None), (fh[:, :used], fl[:, :used]), tw, (sh[...], sl[...]), padded, seqs * groups)
    spec_ref[...] = spec
    h = h_ref[...]
    prod = product(spec, jnp.concatenate([h] * seqs, axis=0), False)
    y = signal_of(prod, (ih[...], il[...]), tw, (bh[:used, :], bl[:used, :]), padded, seqs * groups)
    scattered(y_ref, y, seqs, rows, groups)


def conv_backward_kernel(padded, seqs, x_ref, h_ref, fh, fl, tw, sh, sl, ih, il, bh, bl, y_ref, spec_ref):
    rows = x_ref.shape[0] // seqs
    groups = x_ref.shape[1] // GROUP
    used = rows * GROUP
    x = gathered(x_ref, seqs, rows, groups).astype(BF)
    spec = spectrum_of((x, None), (fh[:, :used], fl[:, :used]), tw, (sh[...], sl[...]), padded, seqs * groups)
    spec_ref[...] = spec
    h = h_ref[...]
    prod = product(spec, jnp.concatenate([h] * seqs, axis=0), True)
    y = signal_of(prod, (ih[...], il[...]), tw, (bh[:used, :], bl[:used, :]), padded, seqs * groups)
    scattered(y_ref, y, seqs, rows, groups)


def filter_grad_kernel(padded, seqs, spec_ref, saved_ref, tw, ih, il, bh, bl, out_ref):
    groups = out_ref.shape[0] // GROUP
    first = out_ref.shape[1] // LANES
    height = groups * GROUP * padded
    total = None
    for q in range(seqs):
        rows = slice(q * height, (q + 1) * height)
        part = product(spec_ref[rows, :], saved_ref[rows, :], True)
        total = part if total is None else total + part
    y = signal_of(total, (ih[...], il[...]), tw, (bh[...], bl[...]), padded, groups)
    for g in range(groups):
        for n in range(first):
            out_ref[g * GROUP : (g + 1) * GROUP, n * LANES : (n + 1) * LANES] = y[
                n * GROUP : (n + 1) * GROUP, g * LANES : (g + 1) * LANES
            ]


def filter_spectrum(lag, tables):
    padded = tables["padded"]
    return pl.pallas_call(
        functools.partial(filter_spectrum_kernel, padded),
        in_specs=vmem_specs(6),
        out_specs=vmem_specs(1)[0],
        out_shape=jax.ShapeDtypeStruct((lag.shape[0] * padded, 2 * LANES), F32),
        compiler_params=params(),
        cost_estimate=cost(2 * 10**9, 4 * 10**6),
        name="filter_spectrum",
    )(lag, *tables["forward"], tables["twiddle"], *tables["second"])


def conv_call(kernel, name, x, spectrum, tables, seqs):
    padded = tables["padded"]
    rows = seqs * x.shape[1] * padded
    return pl.pallas_call(
        functools.partial(kernel, padded, seqs),
        in_specs=vmem_specs(11),
        out_specs=vmem_specs(2),
        out_shape=[
            jax.ShapeDtypeStruct(x.shape, BF),
            jax.ShapeDtypeStruct((rows, 2 * LANES), F32),
        ],
        compiler_params=params(),
        cost_estimate=cost(4 * 10**9, 6 * 10**6),
        name=name,
    )(x, spectrum, *tables["forward"], tables["twiddle"], *tables["second"], *tables["inverse"], *tables["backward"])


def filter_grad_of(spec, saved, channels, seq_length, tables, seqs):
    padded = tables["padded"]
    return pl.pallas_call(
        functools.partial(filter_grad_kernel, padded, seqs),
        in_specs=vmem_specs(7),
        out_specs=vmem_specs(1)[0],
        out_shape=jax.ShapeDtypeStruct((channels, 2 * seq_length), F32),
        compiler_params=params(),
        cost_estimate=cost(3 * 10**9, 6 * 10**6),
        name="filter_grad",
    )(spec, saved, tables["twiddle"], *tables["inverse"], *tables["backward"])


def erf_parts(g):
    x = jnp.abs(g) * (1.0 / math.sqrt(2.0))
    t = 1.0 / (1.0 + 0.3275911 * x)
    e = jnp.exp(-x * x)
    poly = t * (0.254829592 + t * (-0.284496736 + t * (1.421413741 + t * (-1.453152027 + t * 1.061405429))))
    tail = 0.5 * poly * e
    return jnp.where(g < 0, tail, 1.0 - tail), e


def norm_stats(v):
    centered = v - jnp.mean(v, axis=-1, keepdims=True)
    variance = jnp.mean(centered * centered, axis=-1, keepdims=True)
    r = lax.rsqrt(variance + EPSILON)
    return centered * r, r


def norm_backward(w, gain, xhat, r):
    a = w * gain
    return r * (a - jnp.mean(a, axis=-1, keepdims=True) - xhat * jnp.mean(a * xhat, axis=-1, keepdims=True))


def column(j, width):
    return slice(j * width, (j + 1) * width)


def mixer_in_kernel(x_ref, halo_ref, gain_ref, w_ref, taps_ref, conv_ref, n1_ref, proj_ref, sm2_ref):
    rows = x_ref.shape[0]
    width = w_ref.shape[1]
    blocks = w_ref.shape[2] // width
    lead = halo_ref.shape[0]
    x = jnp.concatenate([halo_ref[...].astype(F32), x_ref[...].astype(F32)], axis=0)
    xhat, _ = norm_stats(x)
    n1 = (xhat * gain_ref[...]).astype(BF)
    n1_ref[...] = n1[lead:]
    mixed = []
    for p in range(3):
        proj = jnp.concatenate(
            [mm(n1[:, column(j, width)], w_ref[p, :, column(j, width)]) for j in range(blocks)], axis=1
        ).astype(BF)
        proj_ref[p] = proj
        proj = proj.astype(F32)
        mixed.append(
            taps_ref[0, p : p + 1, :] * proj[lead:]
            + taps_ref[1, p : p + 1, :] * proj[lead - 1 : lead - 1 + rows]
            + taps_ref[2, p : p + 1, :] * proj[lead - 2 : lead - 2 + rows]
        )
    sm2_ref[...] = mixed[2]
    conv_ref[...] = (mixed[0] * mixed[1]).T.astype(BF)


def mixer_in(x, halo, gain, w, taps):
    rows, width = x.shape
    lead = halo.shape[0]
    return pl.pallas_call(
        mixer_in_kernel,
        in_specs=vmem_specs(5),
        out_specs=vmem_specs(4),
        out_shape=[
            jax.ShapeDtypeStruct((width, rows), BF),
            jax.ShapeDtypeStruct((rows, width), BF),
            jax.ShapeDtypeStruct((3, lead + rows, width), BF),
            jax.ShapeDtypeStruct((rows, width), F32),
        ],
        compiler_params=params(),
        cost_estimate=cost(3 * 10**9, 4 * 10**6),
        name="mixer_in",
    )(x, halo, gain, w, taps)


def glu_block(x, og, w_pairs, d_pairs):
    down = None
    back = None
    kept = []
    for (wg, wu), wd in zip(w_pairs, d_pairs):
        gate = mm(x, wg)
        up = mm(x, wu)
        phi, e = erf_parts(gate)
        act = gate * phi
        hidden = (act * up).astype(BF)
        hg = mm_nt(og, wd)
        slope = phi + gate * (e * (1.0 / math.sqrt(2.0 * math.pi)))
        gg = (hg * up * slope).astype(BF)
        ug = (hg * act).astype(BF)
        kept.append((hidden, gg, ug))
        if x is not None:
            down_part = mm(hidden, wd)
            back_part = mm_nt(gg, wg) + mm_nt(ug, wu)
            down = down_part if down is None else down + down_part
            back = back_part if back is None else back + back_part
    return down, back, kept


def middle_kernel(conv_ref, sm2_ref, x_ref, og_ref, gain_ref, wo_ref, ga_ref, gb_ref, da_ref, db_ref,
                  cg_ref, third_ref, mid_ref, out_ref, n2_ref, wog_ref, gg_ref):
    width = wo_ref.shape[0]
    blocks = wo_ref.shape[1] // width
    conv = conv_ref[...].astype(F32).T
    sm2 = sm2_ref[...]
    gated = (sm2 * conv).astype(BF)
    branch = jnp.concatenate(
        [mm(gated[:, column(j, width)], wo_ref[:, column(j, width)]) for j in range(blocks)], axis=1
    )
    middle = x_ref[...].astype(F32) + branch
    xhat, r = norm_stats(middle)
    n2 = (xhat * gain_ref[...]).astype(BF)
    n2_ref[...] = n2.astype(F32).T.astype(BF)
    og = og_ref[...]
    downs, backs = [], []
    for j in range(blocks):
        down, back, _ = glu_block(
            n2[:, column(j, width)],
            og[:, column(j, width)],
            [(ga_ref[j, 0], ga_ref[j, 1]), (gb_ref[j, 0], gb_ref[j, 1])],
            [da_ref[j], db_ref[j]],
        )
        downs.append(down)
        backs.append(back)
    out_ref[...] = (middle + jnp.concatenate(downs, axis=1)).astype(BF)
    n2_grad = jnp.concatenate(backs, axis=1)
    gg_ref[...] = jnp.sum(n2_grad * xhat, axis=0, keepdims=True)
    mid_grad = og.astype(F32) + norm_backward(n2_grad, gain_ref[...], xhat, r)
    mid_ref[...] = mid_grad
    bg = mid_grad.astype(BF)
    gated_grad = jnp.concatenate(
        [mm_nt(bg[:, column(j, width)], wo_ref[:, column(j, width)]) for j in range(blocks)], axis=1
    )
    third_ref[...] = gated_grad * conv
    cg_ref[...] = (gated_grad * sm2).T.astype(BF)
    wog_ref[...] = jnp.concatenate(
        [mm_tn(gated[:, column(j, width)], bg[:, column(j, width)]) for j in range(blocks)], axis=1
    )


def middle_part(conv, sm2, x, og, gain, wo, ga, gb, da, db):
    rows, width = x.shape
    return pl.pallas_call(
        middle_kernel,
        in_specs=vmem_specs(10),
        out_specs=vmem_specs(7),
        out_shape=[
            jax.ShapeDtypeStruct((width, rows), BF),
            jax.ShapeDtypeStruct((rows, width), F32),
            jax.ShapeDtypeStruct((rows, width), F32),
            jax.ShapeDtypeStruct((rows, width), BF),
            jax.ShapeDtypeStruct((width, rows), BF),
            jax.ShapeDtypeStruct(wo.shape, F32),
            jax.ShapeDtypeStruct((1, width), F32),
        ],
        compiler_params=params(),
        cost_estimate=cost(9 * 10**9, 6 * 10**6),
        name="middle_part",
    )(conv, sm2, x, og, gain, wo, ga, gb, da, db)


def glu_grad_kernel(per_plane, x_ref, og_ref, ga_ref, gb_ref, da_ref, db_ref, own_ref, other_ref):
    j = lax.div(lax.axis_index("seq"), per_plane)
    parts = x_ref.shape[0]
    xt = jnp.concatenate([x_ref[k].astype(F32) for k in range(parts)], axis=1)
    ot = jnp.concatenate([og_ref[k].astype(F32) for k in range(parts)], axis=1)
    x = xt.T.astype(BF)
    og = ot.T.astype(BF)
    xt = xt.astype(BF)
    ot = ot.astype(BF)
    width = xt.shape[0]
    for g_ref, d_ref, out_ref in ((ga_ref, da_ref, own_ref), (gb_ref, db_ref, other_ref)):
        wg, wu, wd = g_ref[j, 0], g_ref[j, 1], d_ref[j]
        gate = mm(x, wg)
        up = mm(x, wu)
        phi, e = erf_parts(gate)
        act = gate * phi
        hidden = (act * up).astype(BF)
        hg = mm_nt(og, wd)
        slope = phi + gate * (e * (1.0 / math.sqrt(2.0 * math.pi)))
        out_ref[0:width, :] = mm(xt, (hg * up * slope).astype(BF)).astype(out_ref.dtype)
        out_ref[width : 2 * width, :] = mm(xt, (hg * act).astype(BF)).astype(out_ref.dtype)
        out_ref[2 * width :, :] = mm(ot, hidden).astype(out_ref.dtype)


def glu_grads(x, og, ga, gb, da, db, per_plane):
    width = x.shape[1]
    half = ga.shape[3]
    return pl.pallas_call(
        functools.partial(glu_grad_kernel, per_plane),
        in_specs=vmem_specs(6),
        out_specs=vmem_specs(2),
        out_shape=[
            jax.ShapeDtypeStruct((3 * width, half), F32),
            jax.ShapeDtypeStruct((3 * width, half), BF),
        ],
        compiler_params=params(),
        cost_estimate=cost(9 * 10**9, 4 * 10**6),
        name="glu_grads",
    )(x, og, ga, gb, da, db)


def short_mix(proj_ref, taps_ref, p, rows):
    lead = proj_ref.shape[1] - rows
    proj = proj_ref[p].astype(F32)
    return (
        taps_ref[0, p : p + 1, :] * proj[lead:]
        + taps_ref[1, p : p + 1, :] * proj[lead - 1 : lead - 1 + rows]
        + taps_ref[2, p : p + 1, :] * proj[lead - 2 : lead - 2 + rows]
    )


def short_grad_kernel(icg_ref, third_ref, proj_ref, taps_ref, grad_ref, halo_ref):
    rows = third_ref.shape[0]
    icg = icg_ref[...].astype(F32).T
    g0 = icg * short_mix(proj_ref, taps_ref, 1, rows)
    g1 = icg * short_mix(proj_ref, taps_ref, 0, rows)
    grad_ref[0] = g0
    grad_ref[1] = g1
    halo_ref[0] = g0[:8]
    halo_ref[1] = g1[:8]
    halo_ref[2] = third_ref[0:8, :]


def short_grads(icg, third, proj, taps):
    rows, width = third.shape
    return pl.pallas_call(
        short_grad_kernel,
        in_specs=vmem_specs(4),
        out_specs=vmem_specs(2),
        out_shape=[jax.ShapeDtypeStruct((2, rows, width), F32), jax.ShapeDtypeStruct((3, 8, width), F32)],
        compiler_params=params(),
        cost_estimate=cost(10**9, 2 * 10**6),
        name="short_grads",
    )(icg, third, proj, taps)


def mixer_back_kernel(grad_ref, third_ref, halo_ref, proj_ref, n1_ref, mid_ref, x_ref, gain_ref, w_ref, taps_ref,
                      wog_ref, gg_ref, f1_ref, f2_ref, in_ref, own_ref, other_ref, pack_ref):
    rows, model = third_ref.shape
    width = w_ref.shape[1]
    blocks = model // width
    lead = proj_ref.shape[1] - rows
    n1 = n1_ref[...]
    pack_ref[...] = jnp.zeros_like(pack_ref)
    sums = []
    back = [None] * blocks
    for p in range(3):
        g = third_ref[...] if p == 2 else grad_ref[p]
        ext = jnp.concatenate([g, halo_ref[p]], axis=0)
        proj = proj_ref[p].astype(F32)
        for k in range(3):
            sums.append(jnp.sum(g * proj[lead - k : lead - k + rows], axis=0, keepdims=True))
        pg = (
            taps_ref[0, p : p + 1, :] * g
            + taps_ref[1, p : p + 1, :] * ext[1 : rows + 1]
            + taps_ref[2, p : p + 1, :] * ext[2 : rows + 2]
        ).astype(BF)
        pack_ref[p * width : (p + 1) * width, :model] = jnp.concatenate(
            [mm_tn(n1[:, column(j, width)], pg[:, column(j, width)]) for j in range(blocks)], axis=1
        )
        for j in range(blocks):
            part = mm_nt(pg[:, column(j, width)], w_ref[p, :, column(j, width)])
            back[j] = part if back[j] is None else back[j] + part
    n1_grad = jnp.concatenate(back, axis=1)
    xhat, r = norm_stats(x_ref[...].astype(F32))
    sums.append(jnp.sum(n1_grad * xhat, axis=0, keepdims=True))
    sums.append(gg_ref[...])
    in_ref[...] = (mid_ref[...] + norm_backward(n1_grad, gain_ref[...], xhat, r)).astype(BF)
    pack_ref[3 * width : 4 * width, :model] = wog_ref[...]
    pieces = model // LANES
    hidden = f2_ref.shape[0]
    small = jnp.concatenate(sums, axis=0)
    for c in range(pieces):
        pack_ref[c * 16 : c * 16 + len(sums), model:] = small[:, c * LANES : (c + 1) * LANES]
    base = pieces * 16
    pack_ref[base : base + hidden, model:] = f2_ref[...]
    pack_ref[base + hidden : base + hidden + 8, model:] = f1_ref[...]
    half = own_ref.shape[0]
    me = lax.axis_index("tp")
    own_ref[...] = pack_ref[pl.ds(me * half, half), :]
    other_ref[...] = pack_ref[pl.ds((1 - me) * half, half), :].astype(BF)


def mixer_back(grad, third, halo, proj, n1, mid, x, gain, w, taps, wog, gg, f1, f2):
    rows, model = x.shape
    half = 2 * w.shape[1]
    return pl.pallas_call(
        mixer_back_kernel,
        in_specs=vmem_specs(14),
        out_specs=vmem_specs(3),
        out_shape=[
            jax.ShapeDtypeStruct((rows, model), BF),
            jax.ShapeDtypeStruct((half, model + LANES), F32),
            jax.ShapeDtypeStruct((half, model + LANES), BF),
        ],
        scratch_shapes=[pltpu.VMEM((2 * half, model + LANES), F32)],
        compiler_params=params(),
        cost_estimate=cost(4 * 10**9, 6 * 10**6),
        name="mixer_back",
    )(grad, third, halo, proj, n1, mid, x, gain, w, taps, wog, gg, f1, f2)


def permuted(x, axes, count, by):
    pairs = [(i, i + by) for i in range(count) if 0 <= i + by < count]
    return lax.ppermute(x, axes, pairs)


def swapped(x):
    return lax.ppermute(x, "tp", [(0, 1), (1, 0)])


def exchanged(x, axes, groups=None):
    return lax.all_to_all(x, axes, 0, 0, axis_index_groups=groups, tiled=True)


def gathered_all(x, count):
    return exchanged(jnp.broadcast_to(x[None], (count,) + x.shape), "seq")


def local(
    layer_input,
    mixer_gain,
    in_proj,
    short_taps,
    filter_w1,
    filter_b1,
    filter_w2,
    filter_w3,
    filter_decay,
    out_proj,
    glu_gain,
    glu_in,
    glu_out,
    out_grad,
):
    tok_rows, model = layer_input.shape
    width = in_proj.shape[0]
    blocks = model // width
    half = glu_out.shape[0]
    seq_devices = lax.axis_size("seq")
    tp_devices = lax.axis_size("tp")
    devices = seq_devices * tp_devices
    both = ("seq", "tp")
    rows = tok_rows // tp_devices
    seq_length = min(MIN_LEN, tok_rows * seq_devices)
    seqs = tok_rows * seq_devices // seq_length
    per_plane = seq_devices // blocks
    chans = model // devices
    chans_padded = -(-chans // GROUP) * GROUP
    tp_index = lax.axis_index("tp")
    linear = lax.axis_index("seq") * tp_devices + tp_index
    at_start = linear * rows % seq_length == 0
    at_end = (linear + 1) * rows % seq_length == 0
    tables = transform_tables(seq_length)
    features = feature_table(seq_length)
    across = [[r + g * per_plane for g in range(blocks)] for r in range(per_plane)]
    within = [[g * per_plane + r for r in range(per_plane)] for g in range(blocks)]

    own_rows = lax.dynamic_slice_in_dim(layer_input, tp_index * rows, rows, 0)
    halo = permuted(own_rows[rows - 16 :], both, devices, 1)
    halo = jnp.where(at_start, jnp.zeros_like(halo), halo)

    hidden = filter_w2.shape[0]
    w1b = jnp.concatenate([filter_w1, filter_b1[None], jnp.zeros((2, hidden), F32)], axis=0)
    pad = ((0, chans_padded - chans), (0, 0))
    w3t = jnp.pad(lax.dynamic_slice_in_dim(filter_w3.T, tp_index * chans, chans, 0), pad)
    decay = lax.dynamic_slice_in_dim(filter_decay, tp_index * chans, chans, 0)
    decay = jnp.pad(jnp.broadcast_to(decay[:, None], (chans, LANES)), pad)
    lag, *saved = filter_forward(features, w1b, filter_w2, w3t, decay, seq_length)
    spectrum = filter_spectrum(lag, tables)

    w_in = in_proj.transpose(1, 0, 2)
    conv_rows, n1, proj, sm2 = mixer_in(own_rows, halo, mixer_gain[None], w_in, short_taps)

    def to_channels(x):
        out = exchanged(x.reshape(devices, chans, rows), both)
        return jnp.pad(out, ((0, 0), (0, chans_padded - chans), (0, 0)))

    def to_tokens(x):
        return exchanged(x[:, :chans], both).reshape(model, rows)

    conv_out, signal_spec = conv_call(
        conv_forward_kernel, "conv_forward", to_channels(conv_rows), spectrum, tables, seqs
    )
    conv_tokens = to_tokens(conv_out)

    glu_own = glu_in.transpose(0, 2, 1, 3)
    down_own = glu_out.reshape(half, blocks, width).transpose(1, 0, 2)
    glu_other = swapped(glu_own)
    down_other = swapped(down_own)
    og_plane = exchanged(out_grad.T.reshape(blocks, width, rows), "seq", across)
    conv_grad, third, mid, layer_output, n2, out_grad_w, gain_two = middle_part(
        conv_tokens, sm2, own_rows, out_grad, glu_gain[None], out_proj, glu_own, glu_other, down_own, down_other
    )
    conv_grad_channels = to_channels(conv_grad)
    n2_plane = exchanged(n2.reshape(blocks, width, rows), "seq", across)

    g_own, g_other = glu_grads(n2_plane, og_plane, glu_own, glu_other, down_own, down_other, per_plane)
    glu_sum = (g_own + swapped(g_other).astype(F32)).astype(BF)
    glu_part = exchanged(glu_sum.reshape(per_plane, -1, half), "seq", within)
    glu_part = jnp.sum(glu_part.astype(F32), axis=0).astype(BF)

    input_conv_grad, grad_spec = conv_call(
        conv_backward_kernel, "conv_backward", conv_grad_channels, spectrum, tables, seqs
    )
    icg = to_tokens(input_conv_grad)
    filter_grad = filter_grad_of(grad_spec, signal_spec, chans_padded, seq_length, tables, seqs)
    g1, g2, g3 = filter_backward(filter_grad, features, filter_w2, w3t, decay, saved, seq_length)

    glu_all = gathered_all(glu_part, seq_devices).reshape(blocks, 3, width, half)

    grad01, edge = short_grads(icg, third, proj, short_taps)
    edge = permuted(edge, both, devices, -1)
    edge = jnp.where(at_end, jnp.zeros_like(edge), edge)
    input_half, own, other = mixer_back(
        grad01, third, edge, proj, n1, mid, own_rows, mixer_gain[None], w_in, short_taps, out_grad_w, gain_two, g1, g2
    )
    total = (own + swapped(other).astype(F32)).astype(BF)
    part = exchanged(total, "seq").reshape(seq_devices, -1, model + LANES)
    part = jnp.sum(part.astype(F32), axis=0).astype(BF)
    mine = gathered_all(part, seq_devices).reshape(2 * width, model + LANES)
    theirs = swapped(mine)
    first = jnp.where(tp_index == 0, mine, theirs).astype(F32)
    second = jnp.where(tp_index == 0, theirs, mine).astype(F32)
    big = jnp.concatenate([first, second], axis=0)[:, :model]
    small = first[:, model:]
    pieces = model // LANES
    vectors = small[: pieces * 16].reshape(pieces, 16, LANES).transpose(1, 0, 2).reshape(16, model)
    base = pieces * 16
    tail = small[base + hidden : base + hidden + 8]
    input_other = swapped(input_half)
    input_grad = jnp.where(
        tp_index == 0,
        jnp.concatenate([input_half, input_other], axis=0),
        jnp.concatenate([input_other, input_half], axis=0),
    )
    g3 = g3[:chans]
    g3_other = swapped(g3)
    g3_full = jnp.where(
        tp_index == 0, jnp.concatenate([g3, g3_other], axis=0), jnp.concatenate([g3_other, g3], axis=0)
    ).T
    return (
        layer_output,
        input_grad,
        vectors[9],
        big[: 3 * width].reshape(3, width, model).transpose(1, 0, 2),
        vectors[:9].reshape(3, 3, model).transpose(1, 0, 2),
        tail[:5],
        tail[5],
        small[base : base + hidden],
        g3_full,
        big[3 * width :],
        vectors[10],
        glu_all[:, :2].transpose(0, 2, 1, 3).astype(F32),
        glu_all[:, 2].transpose(2, 0, 1).reshape(half, model).astype(F32),
    )


def solution(mesh):
    placed = (
        P("seq", None),
        P(),
        P(),
        P(),
        P(),
        P(),
        P(),
        P(None, "seq"),
        P("seq"),
        P(),
        P(),
        P(None, None, None, "tp"),
        P("tp", None),
        P(("seq", "tp"), None),
    )
    return jax.shard_map(
        local,
        mesh=mesh,
        in_specs=placed,
        out_specs=(
            P(("seq", "tp"), None),
            P("seq", None),
            P(),
            P(),
            P(),
            P(),
            P(),
            P(),
            P(None, "seq"),
            P(),
            P(),
            P(None, None, None, "tp"),
            P("tp", None),
        ),
        check_vma=False,
    )
```

```python
import math
import functools

import jax
import jax.numpy as jnp
import ml_dtypes
import numpy as np
from jax import lax
from jax.experimental import pallas as pl
from jax.experimental.pallas import tpu as pltpu
from jax.sharding import PartitionSpec as P

MIN_LEN = 8192
SLOW_PATH = False
EPSILON = 1e-05
LANES = 128
GROUP = 8
FILTER_LANES = 2048
VMEM_BYTES = 60 * 1024 * 1024
BF = jnp.bfloat16
F32 = jnp.float32

PI_HIGH = 3.140625
ROUNDER = 12582912.0
PI_LOW = 9.67653589793e-4
SIN_C = (1.0, -0.16666647791862488, 0.00833289884030819, -0.0001980081869987771, 2.590327312645968e-06)
COS_C = (0.9999999403953552, -0.4999990463256836, 0.041663575917482376, -0.0013853635173290968, 2.315232813998591e-05)


def vmem_specs(count):
    return [pl.BlockSpec(memory_space=pltpu.VMEM)] * count


def params(flops=0):
    return pltpu.CompilerParams(vmem_limit_bytes=VMEM_BYTES)


def cost(flops, bytes_accessed=0, transcendentals=0):
    return pl.CostEstimate(flops=flops, bytes_accessed=bytes_accessed, transcendentals=transcendentals)


def split_np(table):
    high = np.asarray(table, np.float32).astype(ml_dtypes.bfloat16)
    low = (np.asarray(table, np.float64) - high.astype(np.float64)).astype(ml_dtypes.bfloat16)
    return high, low


def split3_np(table):
    table = np.asarray(table, np.float64)
    high = table.astype(np.float32).astype(ml_dtypes.bfloat16)
    rest = table - high.astype(np.float64)
    mid = rest.astype(np.float32).astype(ml_dtypes.bfloat16)
    low = (rest - mid.astype(np.float64)).astype(np.float32).astype(ml_dtypes.bfloat16)
    return high, mid, low


@functools.lru_cache(maxsize=None)
def transform_tables(seq_length):
    period = 2 * seq_length
    first = period // LANES
    kept = first // 2 + 1
    padded = -(-kept // 8) * 8
    k = np.arange(padded)
    live = (k < kept).astype(np.float64)
    n = np.arange(first)
    angle = 2 * np.pi / first * ((k[:, None] * n[None, :]) % first)
    eye = np.eye(GROUP)
    stage = np.zeros((GROUP, 2, padded, first, GROUP))
    stage[:, 0] = np.einsum("kn,cd->cknd", np.cos(angle) * live[:, None], eye)
    stage[:, 1] = np.einsum("kn,cd->cknd", -np.sin(angle) * live[:, None], eye)
    forward = stage.reshape(GROUP * 2 * padded, first * GROUP)
    backward = forward.T
    m = np.arange(LANES)
    turn = 2 * np.pi / period * ((k[:, None] * m[None, :]) % period)
    weight = np.where((k == 0) | (k == first // 2), 1.0, 2.0) * live / period
    twiddle = np.stack(
        [np.cos(turn), np.sin(turn), np.cos(turn) * weight[:, None], np.sin(turn) * weight[:, None]]
    ).astype(np.float32)
    inner = 2 * np.pi / LANES * ((m[:, None] * m[None, :]) % LANES)
    c, s = np.cos(inner), np.sin(inner)
    second = np.block([[c, -s], [s, c]])
    return {
        "forward": split_np(forward),
        "backward": split_np(backward),
        "twiddle": twiddle,
        "second": split_np(second),
        "inverse": split_np(second.T),
        "first": first,
        "padded": padded,
    }


@functools.lru_cache(maxsize=None)
def feature_table(seq_length):
    period = 2 * seq_length
    index = np.arange(period)
    lag = np.where(index < seq_length, index, index - period)
    q = lag / seq_length
    rows = [q, np.cos(2 * np.pi * q), np.cos(4 * np.pi * q), np.sin(2 * np.pi * q), np.sin(4 * np.pi * q)]
    rows.append(np.ones_like(q))
    rows += [np.zeros_like(q)] * 2
    high, mid, low = split3_np(np.stack(rows))
    return np.concatenate([high, high, mid, high, mid, low], axis=0)


def split(values):
    high = values.astype(BF)
    low = (values - high.astype(F32)).astype(BF)
    return high, low


def first_weights(rows):
    high = rows.astype(BF).astype(F32)
    mid = (rows - high).astype(BF).astype(F32)
    low = rows - high - mid
    return jnp.concatenate([high, mid, high, low, mid, high], axis=0).astype(BF)


def mm(a, b):
    return jnp.dot(a, b, preferred_element_type=F32)


def mm_nt(a, b):
    return lax.dot_general(a, b, (((1,), (1,)), ((), ())), preferred_element_type=F32)


def mm_tn(a, b):
    return lax.dot_general(a, b, (((0,), (0,)), ((), ())), preferred_element_type=F32)


def mm3(a, b):
    ah, al = a
    bh, bl = b
    return mm(ah, bh) + (mm(al, bh) + mm(ah, bl))


def mm3_tn(a, b):
    ah, al = a
    bh, bl = b
    return mm_tn(ah, bh) + (mm_tn(al, bh) + mm_tn(ah, bl))


def sine_cosine(x):
    n = (x * (0.5 / math.pi) + ROUNDER) - ROUNDER
    t = (x * 0.5 - n * PI_HIGH) - n * PI_LOW
    t2 = t * t
    s = SIN_C[4]
    for c in SIN_C[3::-1]:
        s = s * t2 + c
    s = s * t
    k = COS_C[4]
    for c in COS_C[3::-1]:
        k = k * t2 + c
    twice = s + s
    return twice * k, 1.0 - twice * s


def lag_decay(decay, start, width, seq_length):
    lane = lax.broadcasted_iota(jnp.int32, decay.shape[:1] + (width,), 1) + start
    lag = jnp.where(lane < seq_length, lane, 2 * seq_length - lane).astype(F32)
    return jnp.exp(lag * (decay[:, :1] * (-1.0 / seq_length)))


def stacked_weights(w):
    high, low = split(w)
    zero = jnp.zeros_like(high)
    return jnp.concatenate(
        [jnp.concatenate([high, high], axis=1), jnp.concatenate([low, zero], axis=1)], axis=0
    )


def stacked_product(weights, values):
    out = mm(weights, jnp.concatenate(split(values), axis=0))
    rows = out.shape[0] // 2
    return out[:rows] + out[rows:]


def filter_forward_kernel(feat_ref, w1_ref, w2_ref, w3_ref, decay_ref, own_ref, other_ref, a_ref, ac_ref, b_ref, bc_ref):
    length = own_ref.shape[1]
    channels = own_ref.shape[0]
    width = min(FILTER_LANES, length)
    begin = lax.axis_index("tp") * length
    w1 = first_weights(w1_ref[...])
    w2 = stacked_weights(w2_ref[...].T)
    w3 = stacked_weights(w3_ref[...])
    decay = decay_ref[...]
    for lo in range(0, length, width):
        lanes = slice(lo, lo + width)
        start = pl.multiple_of(begin + lo, LANES)
        s1, c1 = sine_cosine(mm_tn(w1, feat_ref[:, pl.ds(start, width)]))
        a_ref[:, lanes] = s1.astype(BF)
        ac_ref[:, lanes] = c1.astype(BF)
        s2, c2 = sine_cosine(stacked_product(w2, s1))
        b_ref[:, lanes] = s2.astype(BF)
        bc_ref[:, lanes] = c2.astype(BF)
        lag = stacked_product(w3, s2) * lag_decay(decay, start, width, length)
        own_ref[:, lanes] = lag[:channels]
        other_ref[:, lanes] = lag[channels:]


def filter_forward(features, w1b, w2, w3t, decay):
    hidden = w2.shape[0]
    channels = w3t.shape[0] // 2
    length = features.shape[1] // 2
    return pl.pallas_call(
        filter_forward_kernel,
        in_specs=vmem_specs(5),
        out_specs=vmem_specs(6),
        out_shape=[jax.ShapeDtypeStruct((channels, length), F32)] * 2
        + [jax.ShapeDtypeStruct((hidden, length), BF)] * 4,
        compiler_params=params(),
        cost_estimate=cost(8 * 10**9, 8 * 10**6),
        name="filter_forward",
    )(features, w1b, w2, w3t, decay)


def filter_backward_kernel(own_ref, other_ref, feat_ref, w2_ref, w3_ref, decay_ref, a_ref, ac_ref, b_ref, bc_ref, g1_ref, g2_ref, g3_ref):
    length = own_ref.shape[1]
    width = min(FILTER_LANES, length)
    begin = lax.axis_index("tp") * length
    w2 = stacked_weights(w2_ref[...])
    w3 = split(w3_ref[...])
    decay = decay_ref[...]
    g1 = g2 = g3 = 0.0
    for lo in range(0, length, width):
        lanes = slice(lo, lo + width)
        start = pl.multiple_of(begin + lo, LANES)
        grad = jnp.concatenate([own_ref[:, lanes], other_ref[:, lanes]], axis=0)
        wh, wl = split(grad * lag_decay(decay, start, width, length))
        second = b_ref[:, lanes]
        g3 += mm_nt(wh, second) + mm_nt(wl, second)
        pre2 = mm3_tn(w3, (wh, wl)) * bc_ref[:, lanes].astype(F32)
        ph = pre2.astype(BF)
        g2 += mm_nt(a_ref[:, lanes], ph)
        pre1 = stacked_product(w2, pre2) * ac_ref[:, lanes].astype(F32)
        g1 += mm_nt(feat_ref[:8, pl.ds(start, width)], pre1.astype(BF))
    g1_ref[...] = g1
    g2_ref[...] = g2
    g3_ref[...] = g3


def filter_backward(own, other, features, w2, w3t, decay, saved):
    hidden = w2.shape[0]
    return pl.pallas_call(
        filter_backward_kernel,
        in_specs=vmem_specs(10),
        out_specs=vmem_specs(3),
        out_shape=[
            jax.ShapeDtypeStruct((8, hidden), F32),
            jax.ShapeDtypeStruct((hidden, hidden), F32),
            jax.ShapeDtypeStruct((w3t.shape[0], hidden), F32),
        ],
        compiler_params=params(),
        cost_estimate=cost(8 * 10**9, 8 * 10**6),
        name="filter_backward",
    )(own, other, features, w2, w3t, decay, *saved)


def inner_spectrum(a, twiddle_ref, second, padded, columns):
    tc, ts = twiddle_ref[0], twiddle_ref[1]
    parts = []
    for col in range(columns):
        lanes = slice(col * LANES, (col + 1) * LANES)
        for c in range(GROUP):
            base = c * 2 * padded
            re = a[base : base + padded, lanes]
            im = a[base + padded : base + 2 * padded, lanes]
            parts.append(jnp.concatenate([re * tc + im * ts, im * tc - re * ts], axis=1))
    return mm3(split(jnp.concatenate(parts, axis=0)), second)


def signal_of(spec, inverse, twiddle_ref, back, padded, columns):
    b = mm3(split(spec), inverse)
    tc, ts = twiddle_ref[2], twiddle_ref[3]
    cols = []
    for col in range(columns):
        parts = []
        for c in range(GROUP):
            base = (col * GROUP + c) * padded
            re = b[base : base + padded, :LANES]
            im = b[base : base + padded, LANES:]
            parts.append(re * tc - im * ts)
            parts.append(im * tc + re * ts)
        cols.append(jnp.concatenate(parts, axis=0))
    z = split(jnp.concatenate(cols, axis=1))
    return [mm3(rows, z) for rows in back]


def gathered(x, seqs, rows, groups):
    cols = []
    for q in range(seqs):
        for g in range(groups):
            block = x[q * rows : (q + 1) * rows, g * GROUP : (g + 1) * GROUP, :]
            cols.append(block.reshape(rows * GROUP, LANES))
    return jnp.concatenate(cols, axis=1)


def scattered(y, seqs, rows, groups):
    out = []
    for q in range(seqs):
        cols = [
            y[:, (q * groups + g) * LANES : (q * groups + g + 1) * LANES].reshape(rows, GROUP, LANES)
            for g in range(groups)
        ]
        out.append(jnp.concatenate(cols, axis=1))
    return jnp.concatenate(out, axis=0)


def product(a, b, conjugate):
    ar, ai = a[:, :LANES], a[:, LANES:]
    br, bi = b[:, :LANES], b[:, LANES:]
    if conjugate:
        return jnp.concatenate([ar * br + ai * bi, ai * br - ar * bi], axis=1)
    return jnp.concatenate([ar * br - ai * bi, ar * bi + ai * br], axis=1)


def filter_spectrum_kernel(padded, own_ref, other_ref, fh, fl, tw, sh, sl, out_ref):
    groups = own_ref.shape[0] // GROUP
    rows = own_ref.shape[1] // LANES
    used = rows * GROUP
    me = lax.axis_index("tp")
    total = None
    for lag_ref, half in ((own_ref, me), (other_ref, 1 - me)):
        cols = []
        for g in range(groups):
            tiles = [lag_ref[g * GROUP : (g + 1) * GROUP, n * LANES : (n + 1) * LANES] for n in range(rows)]
            cols.append(jnp.concatenate(tiles, axis=0))
        begin = pl.multiple_of(half * used, LANES)
        table = (fh[:, pl.ds(begin, used)], fl[:, pl.ds(begin, used)])
        part = mm3(table, split(jnp.concatenate(cols, axis=1)))
        total = part if total is None else total + part
    out_ref[...] = inner_spectrum(total, tw, (sh[...], sl[...]), padded, groups)


def signal_spectrum(x, seqs, fh, fl, tw, sh, sl, padded):
    rows = x.shape[0] // seqs
    groups = x.shape[1] // GROUP
    used = rows * GROUP
    flat = gathered(x, seqs, rows, groups).astype(BF)
    a = mm(fh[:, :used], flat) + mm(fl[:, :used], flat)
    return inner_spectrum(a, tw, (sh[...], sl[...]), padded, seqs * groups)


def filtered(spec, h_ref, seqs, conjugate, tw, ih, il, bh, bl, padded, shape):
    rows = shape[0] // seqs
    groups = shape[1] // GROUP
    used = rows * GROUP
    prod = product(spec, jnp.concatenate([h_ref[...]] * seqs, axis=0), conjugate)
    (y,) = signal_of(prod, (ih[...], il[...]), tw, [(bh[:used, :], bl[:used, :])], padded, seqs * groups)
    return scattered(y, seqs, rows, groups)


def conv_forward_kernel(padded, seqs, x_ref, h_ref, fh, fl, tw, sh, sl, ih, il, bh, bl, y_ref, spec_ref):
    x = x_ref[...].astype(F32)
    spec = signal_spectrum(x, seqs, fh, fl, tw, sh, sl, padded)
    spec_ref[...] = spec
    y_ref[...] = filtered(spec, h_ref, seqs, False, tw, ih, il, bh, bl, padded, x.shape).astype(BF)


def conv_backward_kernel(padded, seqs, g_ref, sm_ref, p_ref, y_ref, taps_ref, h_ref, fh, fl, tw, sh, sl, ih, il, bh, bl,
                         pg_ref, spec_ref, st_ref, icg_ref):
    count, chans, _ = g_ref.shape
    gated = g_ref[...].astype(F32)
    conv_grad = gated * sm_ref[:, 2 * chans :, :]
    spec = signal_spectrum(conv_grad, seqs, fh, fl, tw, sh, sl, padded)
    spec_ref[...] = spec
    icg = filtered(spec, h_ref, seqs, True, tw, ih, il, bh, bl, padded, g_ref.shape)
    icg_ref[...] = icg.astype(BF).astype(F32)
    per_seq = count // seqs
    taps = [jnp.broadcast_to(taps_ref[:, k : k + 1], (3 * chans, LANES)) for k in range(3)]
    lane = lax.broadcasted_iota(jnp.int32, (3 * chans, LANES), 1)

    def step(i, carry):
        next1, next2, acc0, acc1, acc2 = carry
        n = count - 1 - i
        keep = jnp.where(lax.rem(n + 1, per_seq) == 0, 0.0, 1.0)
        sm = sm_ref[n]
        back = icg_ref[n]
        sg = jnp.concatenate(
            [back * sm[chans : 2 * chans], back * sm[:chans], g_ref[n].astype(F32) * y_ref[n].astype(F32)], axis=0
        )
        r1 = pltpu.roll(sg, LANES - 1, 1)
        r2 = pltpu.roll(sg, LANES - 2, 1)
        s1 = jnp.where(lane < LANES - 1, r1, next1 * keep)
        s2 = jnp.where(lane < LANES - 2, r2, next2 * keep)
        pg_ref[n] = (taps[0] * sg + taps[1] * s1 + taps[2] * s2).astype(BF)
        p = p_ref[n]
        return r1, r2, acc0 + sg * p, acc1 + s1 * p, acc2 + s2 * p

    zero = jnp.zeros((3 * chans, LANES), F32)
    _, _, acc0, acc1, acc2 = lax.fori_loop(0, count, step, (zero,) * 5, unroll=4)
    out = zero
    for k, acc in enumerate((acc0, acc1, acc2)):
        out = jnp.where(lane == k, jnp.sum(acc, axis=1, keepdims=True), out)
    st_ref[...] = out


def filter_grad_kernel(padded, seqs, spec_ref, saved_ref, tw, ih, il, bh, bl, own_ref, other_ref):
    groups = own_ref.shape[0] // GROUP
    rows = own_ref.shape[1] // LANES
    used = rows * GROUP
    height = groups * GROUP * padded
    total = None
    for q in range(seqs):
        part = product(spec_ref[q * height : (q + 1) * height, :], saved_ref[q * height : (q + 1) * height, :], True)
        total = part if total is None else total + part
    me = lax.axis_index("tp")
    halves = []
    for half in (me, 1 - me):
        begin = pl.multiple_of(half * used, LANES)
        halves.append((bh[pl.ds(begin, used), :], bl[pl.ds(begin, used), :]))
    for out_ref, y in zip((own_ref, other_ref), signal_of(total, (ih[...], il[...]), tw, halves, padded, groups)):
        for g in range(groups):
            for n in range(rows):
                out_ref[g * GROUP : (g + 1) * GROUP, n * LANES : (n + 1) * LANES] = y[
                    n * GROUP : (n + 1) * GROUP, g * LANES : (g + 1) * LANES
                ]


def filter_spectrum(own, other, tables):
    padded = tables["padded"]
    return pl.pallas_call(
        functools.partial(filter_spectrum_kernel, padded),
        in_specs=vmem_specs(7),
        out_specs=vmem_specs(1)[0],
        out_shape=jax.ShapeDtypeStruct((own.shape[0] * padded, 2 * LANES), F32),
        compiler_params=params(),
        cost_estimate=cost(4 * 10**9, 4 * 10**6),
        name="filter_spectrum",
    )(own, other, *tables["forward"], tables["twiddle"], *tables["second"])


def transforms(tables):
    return (*tables["forward"], tables["twiddle"], *tables["second"], *tables["inverse"], *tables["backward"])


def conv_forward(x, spectrum, tables, seqs):
    padded = tables["padded"]
    return pl.pallas_call(
        functools.partial(conv_forward_kernel, padded, seqs),
        in_specs=vmem_specs(11),
        out_specs=vmem_specs(2),
        out_shape=[
            jax.ShapeDtypeStruct(x.shape, BF),
            jax.ShapeDtypeStruct((seqs * x.shape[1] * padded, 2 * LANES), F32),
        ],
        compiler_params=params(),
        cost_estimate=cost(5 * 10**9, 6 * 10**6),
        name="conv_forward",
    )(x, spectrum, *transforms(tables))


def conv_backward(gated, mixed, proj, conv_out, taps, spectrum, tables, seqs):
    padded = tables["padded"]
    count, chans, _ = gated.shape
    return pl.pallas_call(
        functools.partial(conv_backward_kernel, padded, seqs),
        in_specs=vmem_specs(15),
        out_specs=vmem_specs(3),
        out_shape=[
            jax.ShapeDtypeStruct((count, 3 * chans, LANES), BF),
            jax.ShapeDtypeStruct((seqs * chans * padded, 2 * LANES), F32),
            jax.ShapeDtypeStruct((3 * chans, LANES), F32),
        ],
        scratch_shapes=[pltpu.VMEM(gated.shape, F32)],
        compiler_params=params(),
        cost_estimate=cost(7 * 10**9, 9 * 10**6),
        name="conv_backward",
    )(gated, mixed, proj, conv_out, taps, spectrum, *transforms(tables))


def filter_grad_of(spec, saved, channels, seq_length, tables, seqs):
    padded = tables["padded"]
    return pl.pallas_call(
        functools.partial(filter_grad_kernel, padded, seqs),
        in_specs=vmem_specs(7),
        out_specs=vmem_specs(2),
        out_shape=[jax.ShapeDtypeStruct((channels, seq_length), F32)] * 2,
        compiler_params=params(),
        cost_estimate=cost(5 * 10**9, 6 * 10**6),
        name="filter_grad",
    )(spec, saved, tables["twiddle"], *tables["inverse"], *tables["backward"])


def source_of(place, turn, group):
    per_plane, relative = place
    seq = lax.axis_index("seq")
    plane = lax.div(seq, per_plane)
    inside = lax.rem(seq, per_plane)
    half, index = turn
    inner = lax.bitwise_xor(inside, index) if relative else index
    return (lax.bitwise_xor(plane, group) * per_plane + inner) * 2 + lax.bitwise_xor(lax.axis_index("tp"), half)


def channel_mixer_kernel(place, turns, seqs, wc_ref, taps_ref, *refs):
    tiles, (p_ref, sm_ref) = refs[:-2], refs[-2:]
    count, rows3, _ = p_ref.shape
    wc = wc_ref[...]
    for ref, turn_list in zip(tiles, turns):
        for q, turn in enumerate(turn_list):
            x = jnp.concatenate([ref[4 * q + z] for z in range(4)], axis=1)
            p = mm(wc, x).astype(BF).astype(F32)
            for z in range(4):
                p_ref[source_of(place, turn, z)] = p[:, z * LANES : (z + 1) * LANES]
    per_seq = count // seqs
    taps = [jnp.broadcast_to(taps_ref[:, k : k + 1], (rows3, LANES)) for k in range(3)]
    lane = lax.broadcasted_iota(jnp.int32, (rows3, LANES), 1)

    def step(n, carry):
        last1, last2 = carry
        keep = jnp.where(lax.rem(n, per_seq) == 0, 0.0, 1.0)
        p = p_ref[n]
        r1 = pltpu.roll(p, 1, 1)
        r2 = pltpu.roll(p, 2, 1)
        s1 = jnp.where(lane < 1, last1 * keep, r1)
        s2 = jnp.where(lane < 2, last2 * keep, r2)
        sm_ref[n] = taps[0] * p + taps[1] * s1 + taps[2] * s2
        return r1, r2

    zero = jnp.zeros((rows3, LANES), F32)
    lax.fori_loop(0, count, step, (zero, zero), unroll=4)


def channel_mixer(tiles, turns, place, wc, taps, count, seqs):
    return pl.pallas_call(
        functools.partial(channel_mixer_kernel, place, turns, seqs),
        in_specs=vmem_specs(2 + len(tiles)),
        out_specs=vmem_specs(2),
        out_shape=[jax.ShapeDtypeStruct((count, wc.shape[0], LANES), F32)] * 2,
        compiler_params=params(),
        cost_estimate=cost(3 * 10**9, 6 * 10**6),
        name="channel_mixer",
    )(wc, taps, *tiles)


def in_grad_kernel(place, turns, pg_ref, st_ref, *refs):
    tiles, (out_ref, keep_ref) = refs[:-2], refs[-2:]
    total = None
    for ref, turn_list in zip(tiles, turns):
        for q, turn in enumerate(turn_list):
            x = jnp.concatenate([ref[4 * q + z] for z in range(4)], axis=1)
            g = jnp.concatenate([pg_ref[source_of(place, turn, z)] for z in range(4)], axis=1)
            part = mm_nt(g, x)
            total = part if total is None else total + part
    width = total.shape[1]
    keep_ref[...] = jnp.zeros_like(keep_ref)
    keep_ref[:, :width] = total
    keep_ref[:, width : width + 3] = st_ref[:, :3]
    out_ref[...] = keep_ref[...].astype(BF)


def in_grads(tiles, turns, place, pg, st):
    rows3 = pg.shape[1]
    return pl.pallas_call(
        functools.partial(in_grad_kernel, place, turns),
        in_specs=vmem_specs(2 + len(tiles)),
        out_specs=vmem_specs(1)[0],
        out_shape=jax.ShapeDtypeStruct((rows3, 2 * LANES), BF),
        scratch_shapes=[pltpu.VMEM((rows3, 2 * LANES), F32)],
        compiler_params=params(),
        cost_estimate=cost(3 * 10**9, 4 * 10**6),
        name="in_grads",
    )(pg, st, *tiles)


def erf_parts(g):
    x = jnp.abs(g) * (1.0 / math.sqrt(2.0))
    t = 1.0 / (1.0 + 0.3275911 * x)
    e = jnp.exp(-x * x)
    poly = t * (0.254829592 + t * (-0.284496736 + t * (1.421413741 + t * (-1.453152027 + t * 1.061405429))))
    tail = 0.5 * poly * e
    return jnp.where(g < 0, tail, 1.0 - tail), e


def norm_stats(v):
    centered = v - jnp.mean(v, axis=-1, keepdims=True)
    variance = jnp.mean(centered * centered, axis=-1, keepdims=True)
    r = lax.rsqrt(variance + EPSILON)
    return centered * r, r


def norm_backward(w, gain, xhat, r):
    a = w * gain
    return r * (a - jnp.mean(a, axis=-1, keepdims=True) - xhat * jnp.mean(a * xhat, axis=-1, keepdims=True))


def column(j, width):
    return slice(j * width, (j + 1) * width)


def mixer_in_kernel(per_plane, x_ref, halo_ref, gain_ref, w_ref, taps_ref, og_ref, conv_ref, sm2_ref, z0, z1, z2, z3, keep_ref):
    rows = x_ref.shape[0]
    width = w_ref.shape[1]
    blocks = w_ref.shape[2] // width
    lead = halo_ref.shape[0]
    x = jnp.concatenate([halo_ref[...].astype(F32), x_ref[...].astype(F32)], axis=0)
    xhat, _ = norm_stats(x)
    normed = xhat * gain_ref[...]
    n1 = normed.astype(BF)
    mixed = []
    for p in range(3):
        proj = jnp.concatenate(
            [mm(n1[:, column(j, width)], w_ref[p, :, column(j, width)]) for j in range(blocks)], axis=1
        )
        proj = proj.astype(BF).astype(F32)
        mixed.append(
            taps_ref[0, p : p + 1, :] * proj[lead:]
            + taps_ref[1, p : p + 1, :] * proj[lead - 1 : lead - 1 + rows]
            + taps_ref[2, p : p + 1, :] * proj[lead - 2 : lead - 2 + rows]
        )
    sm2_ref[...] = mixed[2]
    conv_ref[...] = (mixed[0] * mixed[1]).T.astype(BF)
    nt = normed[lead:].T.astype(BF)
    ot = og_ref[...].astype(F32).T.astype(BF)
    for j in range(blocks):
        keep_ref[j, :width, :] = nt[column(j, width)]
        keep_ref[j, width:, :] = ot[column(j, width)]
    plane = lax.div(lax.axis_index("seq"), per_plane)
    for d, out in enumerate((z0, z1, z2, z3)):
        out[...] = keep_ref[lax.bitwise_xor(plane, d)]


def mixer_in(x, halo, gain, w, taps, og, per_plane):
    rows, model = x.shape
    width = w.shape[1]
    return pl.pallas_call(
        functools.partial(mixer_in_kernel, per_plane),
        in_specs=vmem_specs(6),
        out_specs=vmem_specs(6),
        out_shape=[jax.ShapeDtypeStruct((model, rows), BF), jax.ShapeDtypeStruct((rows, model), F32)]
        + [jax.ShapeDtypeStruct((2 * width, rows), BF)] * 4,
        scratch_shapes=[pltpu.VMEM((model // width, 2 * width, rows), BF)],
        compiler_params=params(),
        cost_estimate=cost(4 * 10**9, 4 * 10**6),
        name="mixer_in",
    )(x, halo, gain, w, taps, og)


def glu_block(x, og, w_pairs, d_pairs):
    down = None
    back = None
    for (wg, wu), wd in zip(w_pairs, d_pairs):
        gate = mm(x, wg)
        up = mm(x, wu)
        phi, e = erf_parts(gate)
        act = gate * phi
        hidden = (act * up).astype(BF)
        hg = mm_nt(og, wd)
        slope = phi + gate * (e * (1.0 / math.sqrt(2.0 * math.pi)))
        gg = (hg * up * slope).astype(BF)
        ug = (hg * act).astype(BF)
        down_part = mm(hidden, wd)
        back_part = mm_nt(gg, wg) + mm_nt(ug, wu)
        down = down_part if down is None else down + down_part
        back = back_part if back is None else back + back_part
    return down, back


def middle_kernel(per_plane, conv_ref, sm2_ref, x_ref, og_ref, gain_ref, wo_ref, ga_ref, gb_ref, da_ref, db_ref,
                  gg_ref, mid_ref, out_ref, z0, z1, z2, z3, keep_ref):
    width = wo_ref.shape[0]
    blocks = wo_ref.shape[1] // width
    conv = conv_ref[...].astype(F32).T
    gated = sm2_ref[...] * conv
    gated_low = gated.astype(BF)
    branch = jnp.concatenate(
        [mm(gated_low[:, column(j, width)], wo_ref[:, column(j, width)]) for j in range(blocks)], axis=1
    )
    middle = x_ref[...].astype(F32) + branch
    xhat, r = norm_stats(middle)
    normed = xhat * gain_ref[...]
    n2 = normed.astype(BF)
    og = og_ref[...]
    downs, backs = [], []
    for j in range(blocks):
        down, back = glu_block(
            n2[:, column(j, width)],
            og[:, column(j, width)],
            [(ga_ref[j, 0], ga_ref[j, 1]), (gb_ref[j, 0], gb_ref[j, 1])],
            [da_ref[j], db_ref[j]],
        )
        downs.append(down)
        backs.append(back)
    out_ref[...] = (middle + jnp.concatenate(downs, axis=1)).astype(BF)
    n2_grad = jnp.concatenate(backs, axis=1)
    mid_grad = og.astype(F32) + norm_backward(n2_grad, gain_ref[...], xhat, r)
    mid_ref[...] = mid_grad
    bg = mid_grad.astype(BF)
    gated_grad = jnp.concatenate(
        [mm_nt(bg[:, column(j, width)], wo_ref[:, column(j, width)]) for j in range(blocks)], axis=1
    )
    gg_ref[...] = gated_grad.T.astype(BF)
    turned = (normed.T.astype(BF), gated.T.astype(BF), mid_grad.T.astype(BF))
    gain_grad = jnp.sum(n2_grad * xhat, axis=0, keepdims=True)
    for j in range(blocks):
        for k, rows in enumerate(turned):
            keep_ref[j, k * width : (k + 1) * width, :] = rows[column(j, width)]
        g = gain_grad[:, column(j, width)]
        tail = jnp.concatenate(
            [g[:, :LANES], jnp.concatenate([g[:, LANES:], jnp.zeros((1, 2 * LANES - width), F32)], axis=1),
             jnp.zeros((14, LANES), F32)], axis=0
        )
        keep_ref[j, 3 * width :, :] = tail.astype(BF)
    plane = lax.div(lax.axis_index("seq"), per_plane)
    for d, out in enumerate((z0, z1, z2, z3)):
        out[...] = keep_ref[lax.bitwise_xor(plane, d)]


def middle_part(conv, sm2, x, og, gain, wo, ga, gb, da, db, per_plane):
    rows, model = x.shape
    width = wo.shape[0]
    return pl.pallas_call(
        functools.partial(middle_kernel, per_plane),
        in_specs=vmem_specs(10),
        out_specs=vmem_specs(7),
        out_shape=[
            jax.ShapeDtypeStruct((model, rows), BF),
            jax.ShapeDtypeStruct((rows, model), F32),
            jax.ShapeDtypeStruct((rows, model), BF),
        ]
        + [jax.ShapeDtypeStruct((3 * width + 16, rows), BF)] * 4,
        scratch_shapes=[pltpu.VMEM((model // width, 3 * width + 16, rows), BF)],
        compiler_params=params(),
        cost_estimate=cost(9 * 10**9, 6 * 10**6),
        name="middle_part",
    )(conv, sm2, x, og, gain, wo, ga, gb, da, db)


def glu_grad_kernel(per_plane, za, zb, zc, zd, oa, ob, oc, od, ga_ref, gb_ref, da_ref, db_ref, own_ref, other_ref, keep_ref):
    j = lax.div(lax.axis_index("seq"), per_plane)
    width = ga_ref.shape[2]
    half = ga_ref.shape[3]
    z_refs, o_refs = (za, zb, zc, zd), (oa, ob, oc, od)
    across = lambda refs, k: jnp.concatenate([ref[k * width : (k + 1) * width, :] for ref in refs], axis=1)
    xt, gt, bt, ot = across(z_refs, 0), across(z_refs, 1), across(z_refs, 2), across(o_refs, 1)
    x = xt.astype(F32).T.astype(BF)
    og = ot.astype(F32).T.astype(BF)
    weight = mm_nt(gt, bt)
    gains = sum(ref[3 * width : 3 * width + 16, :].astype(F32) for ref in z_refs)
    keep_ref[...] = jnp.zeros_like(keep_ref)
    keep_ref[: width // 2, :width] = weight[: width // 2]
    keep_ref[: width // 2, width : 2 * width] = weight[width // 2 :]
    keep_ref[width // 2 : width // 2 + 16, :LANES] = gains
    for g_ref, d_ref, out_ref in ((ga_ref, da_ref, own_ref), (gb_ref, db_ref, other_ref)):
        wg, wu, wd = g_ref[j, 0], g_ref[j, 1], d_ref[j]
        gate = mm(x, wg)
        up = mm(x, wu)
        phi, e = erf_parts(gate)
        act = gate * phi
        hidden = (act * up).astype(BF)
        hg = mm_nt(og, wd)
        slope = phi + gate * (e * (1.0 / math.sqrt(2.0 * math.pi)))
        out_ref[0:width, :] = mm(xt, (hg * up * slope).astype(BF)).astype(out_ref.dtype)
        out_ref[width : 2 * width, :] = mm(xt, (hg * act).astype(BF)).astype(out_ref.dtype)
        out_ref[2 * width : 3 * width, :] = mm(ot, hidden).astype(out_ref.dtype)
        out_ref[3 * width :, :] = keep_ref[...].astype(out_ref.dtype)


def glu_grads(z_parts, o_parts, ga, gb, da, db, per_plane):
    width, half = ga.shape[2:]
    extra = 2 * LANES // 2
    return pl.pallas_call(
        functools.partial(glu_grad_kernel, per_plane),
        in_specs=vmem_specs(12),
        out_specs=vmem_specs(2),
        out_shape=[
            jax.ShapeDtypeStruct((3 * width + extra, half), F32),
            jax.ShapeDtypeStruct((3 * width + extra, half), BF),
        ],
        scratch_shapes=[pltpu.VMEM((extra, half), F32)],
        compiler_params=params(),
        cost_estimate=cost(9 * 10**9, 4 * 10**6),
        name="glu_grads",
    )(*z_parts, *o_parts, ga, gb, da, db)


def plane_add_kernel(per_plane, own_ref, other_ref, s0, s1, s2, s3, keep_ref):
    outs = (s0, s1, s2, s3)
    rows = own_ref.shape[0] // len(outs)
    total = (own_ref[...] + other_ref[...].astype(F32)).astype(BF)
    for k in range(len(outs)):
        keep_ref[k] = total[k * rows : (k + 1) * rows]
    inside = lax.rem(lax.axis_index("seq"), per_plane)
    for d, out in enumerate(outs):
        out[...] = keep_ref[lax.bitwise_xor(inside, d)]


def plane_add(own, other, per_plane):
    rows, half = own.shape
    return pl.pallas_call(
        functools.partial(plane_add_kernel, per_plane),
        in_specs=vmem_specs(2),
        out_specs=vmem_specs(4),
        out_shape=[jax.ShapeDtypeStruct((rows // 4, half), BF)] * 4,
        scratch_shapes=[pltpu.VMEM((4, rows // 4, half), BF)],
        compiler_params=params(),
        cost_estimate=cost(10**8, 2 * 10**6),
        name="plane_add",
    )(own, other)


def glu_unpack_kernel(per_plane, width, a0, a1, a2, a3, gi_ref, go_ref, wo_ref, gain_ref, keep_ref):
    seq = lax.axis_index("seq")
    plane = lax.div(seq, per_plane)
    inside = lax.rem(seq, per_plane)
    for d, ref in enumerate((a0, a1, a2, a3)):
        for z in range(4):
            keep_ref[lax.bitwise_xor(plane, z), lax.bitwise_xor(inside, d)] = ref[z].astype(F32)
    blocks, pieces, rows, half = keep_ref.shape
    outs, wos, gains = [], [], []
    for j in range(blocks):
        block = jnp.concatenate([keep_ref[j, k] for k in range(pieces)], axis=0)
        gi_ref[j, 0] = block[:width]
        gi_ref[j, 1] = block[width : 2 * width]
        outs.append(block[2 * width : 3 * width].T)
        tail = block[3 * width :]
        wos.append(jnp.concatenate([tail[: width // 2, :width], tail[: width // 2, width : 2 * width]], axis=0))
        rows2 = tail[width // 2 : width // 2 + 8, :LANES]
        gains.append(jnp.concatenate([rows2[0:1], rows2[1:2, : width - LANES]], axis=1))
    go_ref[...] = jnp.concatenate(outs, axis=1)
    wo_ref[...] = jnp.concatenate(wos, axis=1)
    gain_ref[...] = jnp.concatenate(gains, axis=1)


def glu_unpack(arrays, per_plane, width):
    _, rows, half = arrays[0].shape
    model = 4 * width
    return pl.pallas_call(
        functools.partial(glu_unpack_kernel, per_plane, width),
        in_specs=vmem_specs(4),
        out_specs=vmem_specs(4),
        out_shape=[
            jax.ShapeDtypeStruct((4, 2, width, half), F32),
            jax.ShapeDtypeStruct((half, model), F32),
            jax.ShapeDtypeStruct((width, model), F32),
            jax.ShapeDtypeStruct((1, model), F32),
        ],
        scratch_shapes=[pltpu.VMEM((4, 4, rows, half), F32)],
        compiler_params=params(),
        cost_estimate=cost(10**8, 6 * 10**6),
        name="glu_unpack",
    )(*arrays)


def in_unpack_kernel(place, turns, w_ref, gain_ref, *refs):
    tiles, (gi_ref, st_ref, gain_out, keep_ref) = refs[:-4], refs[-4:]
    _, width, model = gi_ref.shape
    for ref, (turn,) in zip(tiles, turns):
        for z in range(4):
            keep_ref[source_of(place, turn, z)] = ref[z].astype(F32)
    count, rows3, _ = keep_ref.shape
    chans = rows3 // 3
    blocks = model // width
    per_block = count // blocks
    gains = []
    for j in range(blocks):
        acc = None
        for p in range(3):
            got = jnp.concatenate(
                [keep_ref[j * per_block + k, p * chans : (p + 1) * chans, :] for k in range(per_block)], axis=0
            )
            turned = got.T
            gi_ref[p, :, column(j, width)] = turned[:width]
            st_ref[p, :, column(j, width)] = turned[width : width + 8]
            part = turned[:width] * w_ref[p, :, column(j, width)].astype(F32)
            acc = part if acc is None else acc + part
        gains.append(jnp.sum(acc.T, axis=0, keepdims=True))
    gain_out[...] = jnp.concatenate(gains, axis=1) / gain_ref[...]


def in_unpack(tiles, turns, place, w, gain):
    rows3 = tiles[0].shape[1]
    count = 4 * len(tiles)
    _, width, model = w.shape
    return pl.pallas_call(
        functools.partial(in_unpack_kernel, place, turns),
        in_specs=vmem_specs(2 + len(tiles)),
        out_specs=vmem_specs(3),
        out_shape=[
            jax.ShapeDtypeStruct((3, width, model), F32),
            jax.ShapeDtypeStruct((3, 8, model), F32),
            jax.ShapeDtypeStruct((1, model), F32),
        ],
        scratch_shapes=[pltpu.VMEM((count, rows3, 2 * LANES), F32)],
        compiler_params=params(),
        cost_estimate=cost(10**8, 4 * 10**6),
        name="in_unpack",
    )(w, gain, *tiles)


def mixer_back_kernel(by_source, pg_ref, mid_ref, x_ref, gain_ref, w_ref, in_ref):
    rows, model = x_ref.shape
    width = w_ref.shape[1]
    blocks = model // width
    if by_source:
        pg = pg_ref[...].astype(F32)
        count, rows3, _ = pg.shape
        chans = rows3 // 3
        parts = [
            pg[:, p * chans : (p + 1) * chans, :].reshape(count * chans, rows).astype(BF) for p in range(3)
        ]
    else:
        parts = [pg_ref[p] for p in range(3)]
    grads = []
    for j in range(blocks):
        total = None
        for p in range(3):
            part = mm(w_ref[p, :, column(j, width)], parts[p][column(j, width)])
            total = part if total is None else total + part
        grads.append(total)
    n1_grad = jnp.concatenate(grads, axis=0).T
    xhat, r = norm_stats(x_ref[...].astype(F32))
    in_ref[...] = (mid_ref[...] + norm_backward(n1_grad, gain_ref[...], xhat, r)).astype(BF)


def mixer_back(pg, mid, x, gain, w, by_source):
    return pl.pallas_call(
        functools.partial(mixer_back_kernel, by_source),
        in_specs=vmem_specs(5),
        out_specs=vmem_specs(1)[0],
        out_shape=jax.ShapeDtypeStruct(x.shape, BF),
        compiler_params=params(),
        cost_estimate=cost(3 * 10**9, 4 * 10**6),
        name="mixer_back",
    )(pg, mid, x, gain, w)


def after(x, *others):
    return lax.optimization_barrier((x,) + others)[0]


def permuted(x, axes, count, by):
    pairs = [(i, i + by) for i in range(count) if 0 <= i + by < count]
    return lax.ppermute(x, axes, pairs)


def swapped(x):
    return lax.ppermute(x, "tp", [(0, 1), (1, 0)])


def crossed(x, mask):
    devices = lax.axis_size("seq")
    return lax.ppermute(x, "seq", [(i, i ^ mask) for i in range(devices)])


def exchanged(x, axes, groups=None):
    return lax.all_to_all(x, axes, 0, 0, axis_index_groups=groups, tiled=True)


def gathered_over(x, count, groups=None):
    return exchanged(jnp.broadcast_to(x[None], (count,) + x.shape), "seq", groups)


def local(
    layer_input,
    mixer_gain,
    in_proj,
    short_taps,
    filter_w1,
    filter_b1,
    filter_w2,
    filter_w3,
    filter_decay,
    out_proj,
    glu_gain,
    glu_in,
    glu_out,
    out_grad,
):
    tok_rows, model = layer_input.shape
    width = in_proj.shape[0]
    blocks = model // width
    half = glu_out.shape[0]
    seq_devices = lax.axis_size("seq")
    tp_devices = lax.axis_size("tp")
    devices = seq_devices * tp_devices
    both = ("seq", "tp")
    rows = tok_rows // tp_devices
    seq_length = min(MIN_LEN, tok_rows * seq_devices)
    seqs = tok_rows * seq_devices // seq_length
    per_plane = seq_devices // blocks
    quick = per_plane == 4 and not SLOW_PATH
    place = (per_plane, quick)
    chans = model // devices
    chans_padded = -(-chans // GROUP) * GROUP
    spare = chans_padded - chans
    hidden = filter_w2.shape[0]
    tp_index = lax.axis_index("tp")
    linear = lax.axis_index("seq") * tp_devices + tp_index
    at_start = linear * rows % seq_length == 0
    tables = transform_tables(seq_length)
    features = feature_table(seq_length)
    within = [[g * per_plane + r for r in range(per_plane)] for g in range(blocks)]

    own_rows = lax.dynamic_slice_in_dim(layer_input, tp_index * rows, rows, 0)
    halo = permuted(own_rows[rows - 16 :], both, devices, 1)
    halo = jnp.where(at_start, jnp.zeros_like(halo), halo)

    w1b = jnp.concatenate([filter_w1, filter_b1[None], jnp.zeros((2, hidden), F32)], axis=0)

    def own_then_other(x):
        a, b = x[:chans], x[chans:]
        first, second = jnp.where(tp_index == 0, a, b), jnp.where(tp_index == 0, b, a)
        pad = ((0, spare), (0, 0))
        return jnp.concatenate([jnp.pad(first, pad), jnp.pad(second, pad)], axis=0)

    w3t = own_then_other(filter_w3.T)
    decay = own_then_other(jnp.broadcast_to(filter_decay[:, None], (tp_devices * chans, LANES)))
    lag_own, lag_other, *saved = filter_forward(features, w1b, filter_w2, w3t, decay)
    lag_back = swapped(lag_other)
    spectrum = filter_spectrum(lag_own, lag_back, tables)

    w_in = in_proj.transpose(1, 0, 2)
    conv_rows, sm2, *sent = mixer_in(own_rows, halo, mixer_gain[None], w_in, short_taps, out_grad, per_plane)

    def to_channels(x):
        out = exchanged(x.reshape(devices, chans, rows), both)
        return jnp.pad(out, ((0, 0), (0, spare), (0, 0)))

    def to_tokens(x):
        return exchanged(x[:, :chans], both).reshape(model, rows)

    conv_channels = to_channels(conv_rows)
    early = [sent[0]] + [crossed(sent[d], d * per_plane) for d in range(1, blocks)]
    rows_in = jnp.stack([x[:width] for x in early])
    if quick:
        plane_tiles = [rows_in] + [crossed(rows_in, d) for d in range(1, per_plane)]
        turns = [[(0, d)] for d in range(per_plane)]
    else:
        plane_tiles = [gathered_over(rows_in, per_plane, within).reshape(per_plane * blocks, width, rows)]
        turns = [[(0, r) for r in range(per_plane)]]
    tiles = plane_tiles + [swapped(x) for x in plane_tiles]
    turns = turns + [[(1, r) for _, r in t] for t in turns]
    turns = tuple(tuple(t) for t in turns)

    conv_out, signal_spec = conv_forward(conv_channels, spectrum, tables, seqs)
    conv_tokens = to_tokens(conv_out)

    def own_channels(x):
        x = lax.dynamic_slice_in_dim(x, linear * chans, chans, 2)
        return jnp.pad(x, ((0, 0), (0, 0), (0, spare)))

    wc = own_channels(in_proj).transpose(1, 2, 0).reshape(3 * chans_padded, width)
    taps = own_channels(short_taps).transpose(1, 2, 0).reshape(3 * chans_padded, 3)
    taps = jnp.pad(taps, ((0, 0), (0, LANES - 3)))
    proj_channels, mixed_channels = channel_mixer(tiles, turns, place, wc, taps, devices, seqs)

    glu_own = glu_in.transpose(0, 2, 1, 3)
    down_own = glu_out.reshape(half, blocks, width).transpose(1, 0, 2)
    glu_other = swapped(glu_own)
    down_other = swapped(down_own)
    gated_grad, mid, layer_output, *sent = middle_part(
        conv_tokens, sm2, own_rows, out_grad, glu_gain[None], out_proj, glu_own, glu_other, down_own, down_other, per_plane
    )
    gated_channels = to_channels(gated_grad)
    late = [sent[0]] + [crossed(sent[d], d * per_plane) for d in range(1, blocks)]
    g_own, g_other = glu_grads(late, early, glu_own, glu_other, down_own, down_other, per_plane)
    g_back = swapped(g_other)
    if quick:
        pieces = plane_add(g_own, g_back, per_plane)
        sums = [pieces[0]] + [crossed(pieces[d], d) for d in range(1, per_plane)]
        piece = sum(x.astype(F32) for x in sums).astype(BF)
        piece = jnp.stack([piece] + [crossed(piece, d * per_plane) for d in range(1, blocks)])
        full = [piece] + [crossed(piece, d) for d in range(1, per_plane)]
        glu_in_grad, glu_out_grad, out_proj_grad, glu_gain_grad = glu_unpack(full, per_plane, width)
        glu_in_grad = glu_in_grad.transpose(0, 2, 1, 3)
        glu_gain_grad = glu_gain_grad[0]
    else:
        total = (g_own + g_back.astype(F32)).astype(BF)
        piece = exchanged(total, "seq", within).reshape(per_plane, -1, half)
        piece = jnp.sum(piece.astype(F32), axis=0).astype(BF)
        full = gathered_over(piece, seq_devices).reshape(blocks, -1, half).astype(F32)
        glu_in_grad = full[:, : 2 * width].reshape(blocks, 2, width, half).transpose(0, 2, 1, 3)
        glu_out_grad = full[:, 2 * width : 3 * width].transpose(2, 0, 1).reshape(half, model)
        tail = full[:, 3 * width :]
        out_proj_grad = (
            tail[:, : width // 2, : 2 * width].reshape(blocks, width // 2, 2, width).transpose(2, 1, 0, 3)
        ).reshape(width, model)
        glu_gain_grad = tail[:, width // 2 : width // 2 + 2, :LANES].reshape(blocks, 2 * LANES)[:, :width].reshape(model)

    pg, grad_spec, tap_sums = conv_backward(
        after(gated_channels, g_other), mixed_channels, proj_channels, conv_out, taps, spectrum, tables, seqs
    )
    pg_sent = pg.reshape(devices, 3, chans_padded, rows)[:, :, :chans].reshape(devices, 3 * chans, rows)
    pg_tokens = exchanged(pg_sent, both)
    if chans != chans_padded:
        pg_tokens = pg_tokens.reshape(devices, 3, chans, rows).transpose(1, 0, 2, 3).reshape(3, model, rows)
    in_piece = in_grads(tiles, turns, place, pg, after(tap_sums, pieces[0]) if quick else tap_sums)
    if quick:
        piece = jnp.stack([in_piece] + [crossed(in_piece, d * per_plane) for d in range(1, blocks)])
        full = [piece] + [crossed(piece, d) for d in range(1, per_plane)]
        full = full + [swapped(x) for x in full]
        in_proj_grad, tap_grads, mixer_gain_grad = in_unpack(full, turns, place, w_in, mixer_gain[None])
        in_proj_grad = in_proj_grad.transpose(1, 0, 2)
        short_taps_grad = tap_grads[:, :3].transpose(1, 0, 2)
        mixer_gain_grad = mixer_gain_grad[0]
    else:
        mine = gathered_over(in_piece, seq_devices)
        theirs = swapped(mine)
        pair = jnp.where(tp_index == 0, jnp.stack([mine, theirs], 1), jnp.stack([theirs, mine], 1))
        pair = pair.reshape(devices, 3, chans_padded, 2 * LANES)[:, :, :chans].astype(F32)
        pair = pair.transpose(1, 0, 2, 3).reshape(3, model, 2 * LANES)
        in_proj_grad = pair[:, :, :width].transpose(2, 0, 1)
        short_taps_grad = pair[:, :, width : width + 3].transpose(2, 0, 1)
        products = in_proj_grad * in_proj.astype(F32)
        products = jnp.sum(products.reshape(width, 3, blocks, width), axis=(1, 3))
        mixer_gain_grad = products.T.reshape(model) / mixer_gain

    fg_own, fg_other = filter_grad_of(after(grad_spec, in_piece), signal_spec, chans_padded, seq_length, tables, seqs)
    fg_back = swapped(fg_other)
    g1, g2, g3 = filter_backward(fg_own, fg_back, features, filter_w2, w3t, decay, saved)
    input_half = mixer_back(pg_tokens, mid, own_rows, mixer_gain[None], w_in, chans == chans_padded)

    total_rows = -(-(hidden + 8) // (8 * devices)) * 8 * devices
    small = jnp.concatenate([g2, g1, jnp.zeros((total_rows - hidden - 8, hidden), F32)], axis=0).astype(BF)
    small = exchanged(after(small, input_half), both).reshape(devices, -1, hidden)
    small = jnp.sum(small.astype(F32), axis=0).astype(BF)
    small = exchanged(jnp.broadcast_to(small[None], (devices,) + small.shape), both)
    small = small.reshape(total_rows, hidden).astype(F32)

    input_other = swapped(input_half)
    input_grad = jnp.where(
        tp_index == 0,
        jnp.concatenate([input_half, input_other], axis=0),
        jnp.concatenate([input_other, input_half], axis=0),
    )
    g3_back = swapped(g3)
    mine = g3[:chans] + g3_back[chans_padded : chans_padded + chans]
    theirs = g3[chans_padded : chans_padded + chans] + g3_back[:chans]
    g3_full = jnp.where(
        tp_index == 0, jnp.concatenate([mine, theirs], axis=0), jnp.concatenate([theirs, mine], axis=0)
    ).T
    return (
        layer_output,
        input_grad,
        mixer_gain_grad,
        in_proj_grad,
        short_taps_grad,
        small[hidden : hidden + 5],
        small[hidden + 5],
        small[:hidden],
        g3_full,
        out_proj_grad,
        glu_gain_grad,
        glu_in_grad,
        glu_out_grad,
    )


def solution(mesh):
    placed = (
        P("seq", None),
        P(),
        P(),
        P(),
        P(),
        P(),
        P(),
        P(None, "seq"),
        P("seq"),
        P(),
        P(),
        P(None, None, None, "tp"),
        P("tp", None),
        P(("seq", "tp"), None),
    )
    return jax.shard_map(
        local,
        mesh=mesh,
        in_specs=placed,
        out_specs=(
            P(("seq", "tp"), None),
            P("seq", None),
            P(),
            P(),
            P(),
            P(),
            P(),
            P(),
            P(None, "seq"),
            P(),
            P(),
            P(None, None, None, "tp"),
            P("tp", None),
        ),
        check_vma=False,
    )
```

```python
import math
import functools

import jax
import jax.numpy as jnp
import ml_dtypes
import numpy as np
from jax import lax
from jax.experimental import pallas as pl
from jax.experimental.pallas import tpu as pltpu
from jax.sharding import PartitionSpec as P

MIN_LEN = 8192
SLOW_PATH = False
EPSILON = 1e-05
LANES = 128
GROUP = 8
FILTER_LANES = 2048
SMALL_ROWS = 72
VMEM_BYTES = 60 * 1024 * 1024
BF = jnp.bfloat16
F32 = jnp.float32

PI_HIGH = 3.140625
ROUNDER = 12582912.0
PI_LOW = 9.67653589793e-4
SIN_C = (1.0, -0.16666647791862488, 0.00833289884030819, -0.0001980081869987771, 2.590327312645968e-06)
COS_C = (0.9999999403953552, -0.4999990463256836, 0.041663575917482376, -0.0013853635173290968, 2.315232813998591e-05)


def vmem_specs(count):
    return [pl.BlockSpec(memory_space=pltpu.VMEM)] * count


def params(flops=0):
    return pltpu.CompilerParams(vmem_limit_bytes=VMEM_BYTES)


def cost(flops, bytes_accessed=0, transcendentals=0):
    return pl.CostEstimate(flops=flops // 20, bytes_accessed=bytes_accessed // 20, transcendentals=0)


def split_np(table):
    high = np.asarray(table, np.float32).astype(ml_dtypes.bfloat16)
    low = (np.asarray(table, np.float64) - high.astype(np.float64)).astype(ml_dtypes.bfloat16)
    return high, low


def split3_np(table):
    table = np.asarray(table, np.float64)
    high = table.astype(np.float32).astype(ml_dtypes.bfloat16)
    rest = table - high.astype(np.float64)
    mid = rest.astype(np.float32).astype(ml_dtypes.bfloat16)
    low = (rest - mid.astype(np.float64)).astype(np.float32).astype(ml_dtypes.bfloat16)
    return high, mid, low


@functools.lru_cache(maxsize=None)
def transform_tables(seq_length):
    period = 2 * seq_length
    first = period // LANES
    kept = first // 2 + 1
    padded = -(-kept // 8) * 8
    k = np.arange(padded)
    live = (k < kept).astype(np.float64)
    n = np.arange(first)
    angle = 2 * np.pi / first * ((k[:, None] * n[None, :]) % first)
    eye = np.eye(GROUP)
    stage = np.zeros((GROUP, 2, padded, first, GROUP))
    stage[:, 0] = np.einsum("kn,cd->cknd", np.cos(angle) * live[:, None], eye)
    stage[:, 1] = np.einsum("kn,cd->cknd", -np.sin(angle) * live[:, None], eye)
    forward = stage.reshape(GROUP * 2 * padded, first * GROUP)
    backward = forward.T
    m = np.arange(LANES)
    turn = 2 * np.pi / period * ((k[:, None] * m[None, :]) % period)
    weight = np.where((k == 0) | (k == first // 2), 1.0, 2.0) * live / period
    twiddle = np.stack(
        [np.cos(turn), np.sin(turn), np.cos(turn) * weight[:, None], np.sin(turn) * weight[:, None]]
    ).astype(np.float32)
    inner = 2 * np.pi / LANES * ((m[:, None] * m[None, :]) % LANES)
    c, s = np.cos(inner), np.sin(inner)
    second = np.block([[c, -s], [s, c]])
    return {
        "forward": split_np(forward),
        "backward": split_np(backward),
        "twiddle": twiddle,
        "second": split_np(second),
        "inverse": split_np(second.T),
        "first": first,
        "padded": padded,
    }


@functools.lru_cache(maxsize=None)
def feature_table(seq_length):
    period = 2 * seq_length
    index = np.arange(period)
    lag = np.where(index < seq_length, index, index - period)
    q = lag / seq_length
    rows = [q, np.cos(2 * np.pi * q), np.cos(4 * np.pi * q), np.sin(2 * np.pi * q), np.sin(4 * np.pi * q)]
    rows.append(np.ones_like(q))
    rows += [np.zeros_like(q)] * 2
    high, mid, low = split3_np(np.stack(rows))
    return np.concatenate([high, high, mid, high, mid, low], axis=0)


def split(values):
    high = values.astype(BF)
    low = (values - high.astype(F32)).astype(BF)
    return high, low


def first_weights(w1_ref, b1_ref):
    hidden = w1_ref.shape[1]
    rows = jnp.concatenate([w1_ref[...], b1_ref[...].reshape(1, hidden), jnp.zeros((2, hidden), F32)], axis=0)
    high = rows.astype(BF).astype(F32)
    mid = (rows - high).astype(BF).astype(F32)
    low = rows - high - mid
    return jnp.concatenate([high, mid, high, low, mid, high], axis=0).astype(BF)


def mm(a, b):
    return jnp.dot(a, b, preferred_element_type=F32)


def mm_nt(a, b):
    return lax.dot_general(a, b, (((1,), (1,)), ((), ())), preferred_element_type=F32)


def mm_tn(a, b):
    return lax.dot_general(a, b, (((0,), (0,)), ((), ())), preferred_element_type=F32)


def mm3(a, b):
    ah, al = a
    bh, bl = b
    return mm(ah, bh) + (mm(al, bh) + mm(ah, bl))


def mm3_tn(a, b):
    ah, al = a
    bh, bl = b
    return mm_tn(ah, bh) + (mm_tn(al, bh) + mm_tn(ah, bl))


def sine_cosine(x):
    n = (x * (0.5 / math.pi) + ROUNDER) - ROUNDER
    t = (x * 0.5 - n * PI_HIGH) - n * PI_LOW
    t2 = t * t
    s = SIN_C[4]
    for c in SIN_C[3::-1]:
        s = s * t2 + c
    s = s * t
    k = COS_C[4]
    for c in COS_C[3::-1]:
        k = k * t2 + c
    twice = s + s
    return twice * k, 1.0 - twice * s


def lag_decay(decay, start, width, seq_length):
    lane = lax.broadcasted_iota(jnp.int32, decay.shape[:1] + (width,), 1) + start
    lag = jnp.where(lane < seq_length, lane, 2 * seq_length - lane).astype(F32)
    return jnp.exp(lag * (decay[:, :1] * (-1.0 / seq_length)))


def stacked_weights(w):
    high, low = split(w)
    zero = jnp.zeros_like(high)
    return jnp.concatenate(
        [jnp.concatenate([high, high], axis=1), jnp.concatenate([low, zero], axis=1)], axis=0
    )


def stacked_product(weights, values):
    out = mm(weights, jnp.concatenate(split(values), axis=0))
    rows = out.shape[0] // 2
    return out[:rows] + out[rows:]


def decay_columns(ref):
    row = jnp.broadcast_to(ref[...].reshape(1, -1), (LANES, ref.shape[0]))
    rows = row.T
    half = ref.shape[0] // 2
    a, b = rows[:half], rows[half:]
    first = lax.axis_index("tp") == 0
    return jnp.concatenate([jnp.where(first, a, b), jnp.where(first, b, a)], axis=0)


def own_first(ref):
    half = ref.shape[0] // 2
    me = lax.axis_index("tp")
    return jnp.concatenate([ref[pl.ds(me * half, half), :], ref[pl.ds((1 - me) * half, half), :]], axis=0)


def filter_forward_kernel(feat_ref, w1_ref, b1_ref, w2_ref, w3_ref, decay_ref, own_ref, other_ref, a_ref, ac_ref, b_ref, bc_ref):
    length = own_ref.shape[1]
    channels = own_ref.shape[0]
    width = min(FILTER_LANES, length)
    begin = lax.axis_index("tp") * length
    w1 = first_weights(w1_ref, b1_ref)
    w2 = stacked_weights(w2_ref[...].T)
    w3 = stacked_weights(own_first(w3_ref))
    decay = decay_columns(decay_ref)
    for lo in range(0, length, width):
        lanes = slice(lo, lo + width)
        start = pl.multiple_of(begin + lo, LANES)
        s1, c1 = sine_cosine(mm_tn(w1, feat_ref[:, pl.ds(start, width)]))
        a_ref[:, lanes] = s1.astype(BF)
        ac_ref[:, lanes] = c1.astype(BF)
        s2, c2 = sine_cosine(stacked_product(w2, s1))
        b_ref[:, lanes] = s2.astype(BF)
        bc_ref[:, lanes] = c2.astype(BF)
        lag = stacked_product(w3, s2) * lag_decay(decay, start, width, length)
        own_ref[:, lanes] = lag[:channels]
        other_ref[:, lanes] = lag[channels:]


def filter_forward(features, w1, b1, w2, w3t, decay):
    hidden = w2.shape[0]
    channels = w3t.shape[0] // 2
    length = features.shape[1] // 2
    return pl.pallas_call(
        filter_forward_kernel,
        in_specs=vmem_specs(6),
        out_specs=vmem_specs(6),
        out_shape=[jax.ShapeDtypeStruct((channels, length), F32)] * 2
        + [jax.ShapeDtypeStruct((hidden, length), BF)] * 4,
        compiler_params=params(),
        cost_estimate=cost(8 * 10**9, 8 * 10**6),
        name="filter_forward",
    )(features, w1, b1, w2, w3t, decay)


def filter_backward_kernel(own_ref, other_ref, feat_ref, w2_ref, w3_ref, decay_ref, a_ref, ac_ref, b_ref, bc_ref, piece_ref, gain_ref, out_ref, g3_ref):
    length = own_ref.shape[1]
    width = min(FILTER_LANES, length)
    begin = lax.axis_index("tp") * length
    w2 = stacked_weights(w2_ref[...])
    w3 = split(own_first(w3_ref))
    decay = decay_columns(decay_ref)
    g1 = g2 = g3 = 0.0
    for lo in range(0, length, width):
        lanes = slice(lo, lo + width)
        start = pl.multiple_of(begin + lo, LANES)
        grad = jnp.concatenate([own_ref[:, lanes], other_ref[:, lanes]], axis=0)
        wh, wl = split(grad * lag_decay(decay, start, width, length))
        second = b_ref[:, lanes]
        g3 += mm_nt(wh, second) + mm_nt(wl, second)
        pre2 = mm3_tn(w3, (wh, wl)) * bc_ref[:, lanes].astype(F32)
        ph = pre2.astype(BF)
        g2 += mm_nt(a_ref[:, lanes], ph)
        pre1 = stacked_product(w2, pre2) * ac_ref[:, lanes].astype(F32)
        g1 += mm_nt(feat_ref[:8, pl.ds(start, width)], pre1.astype(BF))
    rows3 = piece_ref.shape[0]
    more = out_ref.shape[0] - rows3
    gains = [gain_ref[k * LANES : (k + 1) * LANES].reshape(1, LANES) for k in range(gain_ref.shape[0] // LANES)]
    gains += [jnp.zeros((8 - len(gains), LANES), F32)]
    right = jnp.concatenate([g2[more:], g1] + gains, axis=0)
    small = jnp.concatenate([g2[:more], right], axis=1)
    out_ref[...] = jnp.concatenate([piece_ref[...].astype(F32), small], axis=0).astype(BF)
    g3_ref[...] = g3


def filter_backward(own, other, features, w2, w3t, decay, saved, piece, gain):
    hidden = w2.shape[0]
    return pl.pallas_call(
        filter_backward_kernel,
        in_specs=vmem_specs(12),
        out_specs=vmem_specs(2),
        out_shape=[
            jax.ShapeDtypeStruct((piece.shape[0] + SMALL_ROWS, 2 * hidden), BF),
            jax.ShapeDtypeStruct((w3t.shape[0], hidden), F32),
        ],
        compiler_params=params(),
        cost_estimate=cost(8 * 10**9, 8 * 10**6),
        name="filter_backward",
    )(own, other, features, w2, w3t, decay, *saved, piece, gain)


def inner_spectrum(a, twiddle_ref, second, padded, columns):
    tc, ts = twiddle_ref[0], twiddle_ref[1]
    parts = []
    for col in range(columns):
        lanes = slice(col * LANES, (col + 1) * LANES)
        for c in range(GROUP):
            base = c * 2 * padded
            re = a[base : base + padded, lanes]
            im = a[base + padded : base + 2 * padded, lanes]
            parts.append(jnp.concatenate([re * tc + im * ts, im * tc - re * ts], axis=1))
    return mm3(split(jnp.concatenate(parts, axis=0)), second)


def signal_of(spec, inverse, twiddle_ref, back, padded, columns):
    b = mm3(split(spec), inverse)
    tc, ts = twiddle_ref[2], twiddle_ref[3]
    cols = []
    for col in range(columns):
        parts = []
        for c in range(GROUP):
            base = (col * GROUP + c) * padded
            re = b[base : base + padded, :LANES]
            im = b[base : base + padded, LANES:]
            parts.append(re * tc - im * ts)
            parts.append(im * tc + re * ts)
        cols.append(jnp.concatenate(parts, axis=0))
    z = split(jnp.concatenate(cols, axis=1))
    return [mm3(rows, z) for rows in back]


def gathered(x, seqs, rows, groups):
    cols = []
    for q in range(seqs):
        for g in range(groups):
            block = x[q * rows : (q + 1) * rows, g * GROUP : (g + 1) * GROUP, :]
            cols.append(block.reshape(rows * GROUP, LANES))
    return jnp.concatenate(cols, axis=1)


def scattered(y, seqs, rows, groups):
    out = []
    for q in range(seqs):
        cols = [
            y[:, (q * groups + g) * LANES : (q * groups + g + 1) * LANES].reshape(rows, GROUP, LANES)
            for g in range(groups)
        ]
        out.append(jnp.concatenate(cols, axis=1))
    return jnp.concatenate(out, axis=0)


def product(a, b, conjugate):
    ar, ai = a[:, :LANES], a[:, LANES:]
    br, bi = b[:, :LANES], b[:, LANES:]
    if conjugate:
        return jnp.concatenate([ar * br + ai * bi, ai * br - ar * bi], axis=1)
    return jnp.concatenate([ar * br - ai * bi, ar * bi + ai * br], axis=1)


def filter_spectrum_kernel(padded, own_ref, other_ref, fh, fl, tw, sh, sl, out_ref):
    groups = own_ref.shape[0] // GROUP
    rows = own_ref.shape[1] // LANES
    used = rows * GROUP
    me = lax.axis_index("tp")
    total = None
    for lag_ref, half in ((own_ref, me), (other_ref, 1 - me)):
        cols = []
        for g in range(groups):
            tiles = [lag_ref[g * GROUP : (g + 1) * GROUP, n * LANES : (n + 1) * LANES] for n in range(rows)]
            cols.append(jnp.concatenate(tiles, axis=0))
        begin = pl.multiple_of(half * used, LANES)
        table = (fh[:, pl.ds(begin, used)], fl[:, pl.ds(begin, used)])
        part = mm3(table, split(jnp.concatenate(cols, axis=1)))
        total = part if total is None else total + part
    out_ref[...] = inner_spectrum(total, tw, (sh[...], sl[...]), padded, groups)


def signal_spectrum(x, seqs, fh, fl, tw, sh, sl, padded):
    rows = x.shape[0] // seqs
    groups = x.shape[1] // GROUP
    used = rows * GROUP
    flat = gathered(x, seqs, rows, groups).astype(BF)
    a = mm(fh[:, :used], flat) + mm(fl[:, :used], flat)
    return inner_spectrum(a, tw, (sh[...], sl[...]), padded, seqs * groups)


def filtered(spec, h_ref, seqs, conjugate, tw, ih, il, bh, bl, padded, shape):
    rows = shape[0] // seqs
    groups = shape[1] // GROUP
    used = rows * GROUP
    prod = product(spec, jnp.concatenate([h_ref[...]] * seqs, axis=0), conjugate)
    (y,) = signal_of(prod, (ih[...], il[...]), tw, [(bh[:used, :], bl[:used, :])], padded, seqs * groups)
    return scattered(y, seqs, rows, groups)


def conv_forward_kernel(padded, seqs, x_ref, h_ref, fh, fl, tw, sh, sl, ih, il, bh, bl, y_ref, spec_ref):
    x = x_ref[...].astype(F32)
    spec = signal_spectrum(x, seqs, fh, fl, tw, sh, sl, padded)
    spec_ref[...] = spec
    y_ref[...] = filtered(spec, h_ref, seqs, False, tw, ih, il, bh, bl, padded, x.shape).astype(BF)


def conv_backward_kernel(padded, seqs, real, g_ref, sm_ref, p_ref, y_ref, taps_ref, h_ref, fh, fl, tw, sh, sl, ih, il, bh, bl,
                         pg_ref, spec_ref, st_ref, icg_ref):
    count, chans, _ = g_ref.shape
    gated = g_ref[...].astype(F32)
    conv_grad = gated * sm_ref[:, 2 * chans :, :]
    spec = signal_spectrum(conv_grad, seqs, fh, fl, tw, sh, sl, padded)
    spec_ref[...] = spec
    icg = filtered(spec, h_ref, seqs, True, tw, ih, il, bh, bl, padded, g_ref.shape)
    icg_ref[...] = icg.astype(BF).astype(F32)
    per_seq = count // seqs
    taps = tap_columns(taps_ref, real)
    lane = lax.broadcasted_iota(jnp.int32, (3 * chans, LANES), 1)

    def step(i, carry):
        next1, next2, acc0, acc1, acc2 = carry
        n = count - 1 - i
        keep = jnp.where(lax.rem(n + 1, per_seq) == 0, 0.0, 1.0)
        sm = sm_ref[n]
        back = icg_ref[n]
        sg = jnp.concatenate(
            [back * sm[chans : 2 * chans], back * sm[:chans], g_ref[n].astype(F32) * y_ref[n].astype(F32)], axis=0
        )
        r1 = pltpu.roll(sg, LANES - 1, 1)
        r2 = pltpu.roll(sg, LANES - 2, 1)
        s1 = jnp.where(lane < LANES - 1, r1, next1 * keep)
        s2 = jnp.where(lane < LANES - 2, r2, next2 * keep)
        pg_ref[n] = (taps[0] * sg + taps[1] * s1 + taps[2] * s2).astype(BF)
        p = p_ref[n]
        return r1, r2, acc0 + sg * p, acc1 + s1 * p, acc2 + s2 * p

    zero = jnp.zeros((3 * chans, LANES), F32)
    _, _, acc0, acc1, acc2 = lax.fori_loop(0, count, step, (zero,) * 5, unroll=4)
    out = zero
    for k, acc in enumerate((acc0, acc1, acc2)):
        out = jnp.where(lane == k, jnp.sum(acc, axis=1, keepdims=True), out)
    st_ref[...] = out


def filter_grad_kernel(padded, seqs, spec_ref, saved_ref, tw, ih, il, bh, bl, own_ref, other_ref):
    groups = own_ref.shape[0] // GROUP
    rows = own_ref.shape[1] // LANES
    used = rows * GROUP
    height = groups * GROUP * padded
    total = None
    for q in range(seqs):
        part = product(spec_ref[q * height : (q + 1) * height, :], saved_ref[q * height : (q + 1) * height, :], True)
        total = part if total is None else total + part
    me = lax.axis_index("tp")
    halves = []
    for half in (me, 1 - me):
        begin = pl.multiple_of(half * used, LANES)
        halves.append((bh[pl.ds(begin, used), :], bl[pl.ds(begin, used), :]))
    for out_ref, y in zip((own_ref, other_ref), signal_of(total, (ih[...], il[...]), tw, halves, padded, groups)):
        for g in range(groups):
            for n in range(rows):
                out_ref[g * GROUP : (g + 1) * GROUP, n * LANES : (n + 1) * LANES] = y[
                    n * GROUP : (n + 1) * GROUP, g * LANES : (g + 1) * LANES
                ]


def filter_spectrum(own, other, tables):
    padded = tables["padded"]
    return pl.pallas_call(
        functools.partial(filter_spectrum_kernel, padded),
        in_specs=vmem_specs(7),
        out_specs=vmem_specs(1)[0],
        out_shape=jax.ShapeDtypeStruct((own.shape[0] * padded, 2 * LANES), F32),
        compiler_params=params(),
        cost_estimate=cost(4 * 10**9, 4 * 10**6),
        name="filter_spectrum",
    )(own, other, *tables["forward"], tables["twiddle"], *tables["second"])


def transforms(tables):
    return (*tables["forward"], tables["twiddle"], *tables["second"], *tables["inverse"], *tables["backward"])


def conv_forward(x, spectrum, tables, seqs):
    padded = tables["padded"]
    return pl.pallas_call(
        functools.partial(conv_forward_kernel, padded, seqs),
        in_specs=vmem_specs(11),
        out_specs=vmem_specs(2),
        out_shape=[
            jax.ShapeDtypeStruct(x.shape, BF),
            jax.ShapeDtypeStruct((seqs * x.shape[1] * padded, 2 * LANES), F32),
        ],
        compiler_params=params(),
        cost_estimate=cost(5 * 10**9, 6 * 10**6),
        name="conv_forward",
    )(x, spectrum, *transforms(tables))


def conv_backward(gated, mixed, proj, conv_out, taps, spectrum, tables, seqs, real):
    padded = tables["padded"]
    count, chans, _ = gated.shape
    return pl.pallas_call(
        functools.partial(conv_backward_kernel, padded, seqs, real),
        in_specs=vmem_specs(15),
        out_specs=vmem_specs(3),
        out_shape=[
            jax.ShapeDtypeStruct((count, 3 * chans, LANES), BF),
            jax.ShapeDtypeStruct((seqs * chans * padded, 2 * LANES), F32),
            jax.ShapeDtypeStruct((3 * chans, LANES), F32),
        ],
        scratch_shapes=[pltpu.VMEM(gated.shape, F32)],
        compiler_params=params(),
        cost_estimate=cost(7 * 10**9, 9 * 10**6),
        name="conv_backward",
    )(gated, mixed, proj, conv_out, taps, spectrum, *transforms(tables))


def filter_grad_of(spec, saved, channels, seq_length, tables, seqs):
    padded = tables["padded"]
    return pl.pallas_call(
        functools.partial(filter_grad_kernel, padded, seqs),
        in_specs=vmem_specs(7),
        out_specs=vmem_specs(2),
        out_shape=[jax.ShapeDtypeStruct((channels, seq_length), F32)] * 2,
        compiler_params=params(),
        cost_estimate=cost(5 * 10**9, 6 * 10**6),
        name="filter_grad",
    )(spec, saved, tables["twiddle"], *tables["inverse"], *tables["backward"])


def source_of(place, turn, group):
    per_plane, relative = place
    seq = lax.axis_index("seq")
    plane = lax.div(seq, per_plane)
    inside = lax.rem(seq, per_plane)
    half, index = turn
    inner = lax.bitwise_xor(inside, index) if relative else index
    return (lax.bitwise_xor(plane, group) * per_plane + inner) * 2 + lax.bitwise_xor(lax.axis_index("tp"), half)


def own_channels(ref, index, chans):
    model = ref.shape[-1]
    linear = lax.axis_index("seq") * 2 + lax.axis_index("tp")
    first = linear * chans
    window = jnp.minimum(lax.div(first, LANES) * LANES, model - 2 * LANES)
    part = ref[index, :, pl.ds(pl.multiple_of(window, LANES), 2 * LANES)].astype(F32)
    part = pltpu.roll(part, lax.rem(2 * LANES - (first - window), 2 * LANES), 1)
    turned = part[:, :LANES].T
    return turned[: -(-chans // GROUP) * GROUP]


def tap_columns(taps_ref, chans):
    out = []
    for k in range(3):
        cols = own_channels(taps_ref, k, chans)
        out.append(jnp.concatenate([jnp.broadcast_to(cols[:, p : p + 1], (cols.shape[0], LANES)) for p in range(3)], axis=0))
    return out


def channel_mixer_kernel(place, turns, seqs, chans, w_ref, taps_ref, *refs):
    tiles, (p_ref, sm_ref) = refs[:-2], refs[-2:]
    count, rows3, _ = p_ref.shape
    wc = jnp.concatenate([own_channels(w_ref, p, chans) for p in range(3)], axis=0).astype(BF)
    for ref, turn_list in zip(tiles, turns):
        for q, turn in enumerate(turn_list):
            x = jnp.concatenate([ref[4 * q + z] for z in range(4)], axis=1)
            p = mm(wc, x).astype(BF).astype(F32)
            for z in range(4):
                p_ref[source_of(place, turn, z)] = p[:, z * LANES : (z + 1) * LANES]
    per_seq = count // seqs
    taps = tap_columns(taps_ref, chans)
    lane = lax.broadcasted_iota(jnp.int32, (rows3, LANES), 1)

    def step(n, carry):
        last1, last2 = carry
        keep = jnp.where(lax.rem(n, per_seq) == 0, 0.0, 1.0)
        p = p_ref[n]
        r1 = pltpu.roll(p, 1, 1)
        r2 = pltpu.roll(p, 2, 1)
        s1 = jnp.where(lane < 1, last1 * keep, r1)
        s2 = jnp.where(lane < 2, last2 * keep, r2)
        sm_ref[n] = taps[0] * p + taps[1] * s1 + taps[2] * s2
        return r1, r2

    zero = jnp.zeros((rows3, LANES), F32)
    lax.fori_loop(0, count, step, (zero, zero), unroll=4)


def channel_mixer(tiles, turns, place, w, taps, count, seqs, chans):
    rows3 = 3 * (-(-chans // GROUP) * GROUP)
    return pl.pallas_call(
        functools.partial(channel_mixer_kernel, place, turns, seqs, chans),
        in_specs=vmem_specs(2 + len(tiles)),
        out_specs=vmem_specs(2),
        out_shape=[jax.ShapeDtypeStruct((count, rows3, LANES), F32)] * 2,
        compiler_params=params(),
        cost_estimate=cost(3 * 10**9, 6 * 10**6),
        name="channel_mixer",
    )(w, taps, *tiles)


def in_grad_kernel(place, turns, pg_ref, st_ref, *refs):
    tiles, (out_ref, keep_ref) = refs[:-2], refs[-2:]
    total = None
    for ref, turn_list in zip(tiles, turns):
        for q, turn in enumerate(turn_list):
            x = jnp.concatenate([ref[4 * q + z] for z in range(4)], axis=1)
            g = jnp.concatenate([pg_ref[source_of(place, turn, z)] for z in range(4)], axis=1)
            part = mm_nt(g, x)
            total = part if total is None else total + part
    width = total.shape[1]
    keep_ref[...] = jnp.zeros_like(keep_ref)
    keep_ref[:, :width] = total
    keep_ref[:, width : width + 3] = st_ref[:, :3]
    out_ref[...] = keep_ref[...].astype(BF)


def in_grads(tiles, turns, place, pg, st):
    rows3 = pg.shape[1]
    return pl.pallas_call(
        functools.partial(in_grad_kernel, place, turns),
        in_specs=vmem_specs(2 + len(tiles)),
        out_specs=vmem_specs(1)[0],
        out_shape=jax.ShapeDtypeStruct((rows3, 2 * LANES), BF),
        scratch_shapes=[pltpu.VMEM((rows3, 2 * LANES), F32)],
        compiler_params=params(),
        cost_estimate=cost(3 * 10**9, 4 * 10**6),
        name="in_grads",
    )(pg, st, *tiles)


def erf_parts(g):
    x = jnp.abs(g) * (1.0 / math.sqrt(2.0))
    t = 1.0 / (1.0 + 0.3275911 * x)
    e = jnp.exp(-x * x)
    poly = t * (0.254829592 + t * (-0.284496736 + t * (1.421413741 + t * (-1.453152027 + t * 1.061405429))))
    tail = 0.5 * poly * e
    return jnp.where(g < 0, tail, 1.0 - tail), e


def norm_stats(v):
    centered = v - jnp.mean(v, axis=-1, keepdims=True)
    variance = jnp.mean(centered * centered, axis=-1, keepdims=True)
    r = lax.rsqrt(variance + EPSILON)
    return centered * r, r


def norm_backward(w, gain, xhat, r):
    a = w * gain
    return r * (a - jnp.mean(a, axis=-1, keepdims=True) - xhat * jnp.mean(a * xhat, axis=-1, keepdims=True))


def column(j, width):
    return slice(j * width, (j + 1) * width)


def own_part(ref, rows):
    return ref[pl.ds(pl.multiple_of(lax.axis_index("tp") * rows, rows), rows), :]


def mixer_in_kernel(per_plane, seq_length, x_ref, halo_ref, gain_ref, w_ref, taps_ref, og_ref, conv_ref, sm2_ref, z0, z1, z2, z3, keep_ref):
    rows = sm2_ref.shape[0]
    width = w_ref.shape[1]
    blocks = w_ref.shape[2] // width
    lead = halo_ref.shape[0]
    linear = lax.axis_index("seq") * 2 + lax.axis_index("tp")
    keep = jnp.where(lax.rem(linear * rows, seq_length) == 0, 0.0, 1.0)
    inner = x_ref[rows - lead : rows, :].astype(F32)
    halo = jnp.where(lax.axis_index("tp") == 0, halo_ref[...].astype(F32), inner) * keep
    x = jnp.concatenate([halo, own_part(x_ref, rows).astype(F32)], axis=0)
    xhat, _ = norm_stats(x)
    normed = xhat * gain_ref[...].reshape(1, -1)
    n1 = normed.astype(BF)
    mixed = []
    for p in range(3):
        proj = jnp.concatenate(
            [mm(n1[:, column(j, width)], w_ref[p, :, column(j, width)]) for j in range(blocks)], axis=1
        )
        proj = proj.astype(BF).astype(F32)
        mixed.append(
            taps_ref[0, p : p + 1, :] * proj[lead:]
            + taps_ref[1, p : p + 1, :] * proj[lead - 1 : lead - 1 + rows]
            + taps_ref[2, p : p + 1, :] * proj[lead - 2 : lead - 2 + rows]
        )
    sm2_ref[...] = mixed[2]
    conv_ref[...] = (mixed[0] * mixed[1]).T.astype(BF)
    nt = normed[lead:].T.astype(BF)
    ot = og_ref[...].astype(F32).T.astype(BF)
    for j in range(blocks):
        keep_ref[j, :width, :] = nt[column(j, width)]
        keep_ref[j, width:, :] = ot[column(j, width)]
    plane = lax.div(lax.axis_index("seq"), per_plane)
    for d, out in enumerate((z0, z1, z2, z3)):
        out[...] = keep_ref[lax.bitwise_xor(plane, d)]


def mixer_in(x, halo, gain, w, taps, og, per_plane, seq_length):
    rows, model = og.shape
    width = w.shape[1]
    return pl.pallas_call(
        functools.partial(mixer_in_kernel, per_plane, seq_length),
        in_specs=vmem_specs(6),
        out_specs=vmem_specs(6),
        out_shape=[jax.ShapeDtypeStruct((model, rows), BF), jax.ShapeDtypeStruct((rows, model), F32)]
        + [jax.ShapeDtypeStruct((2 * width, rows), BF)] * 4,
        scratch_shapes=[pltpu.VMEM((model // width, 2 * width, rows), BF)],
        compiler_params=params(),
        cost_estimate=cost(4 * 10**9, 4 * 10**6),
        name="mixer_in",
    )(x, halo, gain, w, taps, og)


def glu_block(x, og, w_pairs, d_pairs):
    down = None
    back = None
    for (wg, wu), wd in zip(w_pairs, d_pairs):
        gate = mm(x, wg)
        up = mm(x, wu)
        phi, e = erf_parts(gate)
        act = gate * phi
        hidden = (act * up).astype(BF)
        hg = mm_nt(og, wd)
        slope = phi + gate * (e * (1.0 / math.sqrt(2.0 * math.pi)))
        gg = (hg * up * slope).astype(BF)
        ug = (hg * act).astype(BF)
        down_part = mm(hidden, wd)
        back_part = mm_nt(gg, wg) + mm_nt(ug, wu)
        down = down_part if down is None else down + down_part
        back = back_part if back is None else back + back_part
    return down, back


def middle_kernel(per_plane, conv_ref, sm2_ref, x_ref, og_ref, gain_ref, wo_ref, ga_ref, gb_ref, da_ref, db_ref,
                  gg_ref, mid_ref, out_ref, wo_out, gain_out, z0, z1, z2, z3, keep_ref):
    width = wo_ref.shape[0]
    blocks = wo_ref.shape[1] // width
    conv = conv_ref[...].astype(F32).T
    gated = sm2_ref[...] * conv
    gated_low = gated.astype(BF)
    branch = jnp.concatenate(
        [mm(gated_low[:, column(j, width)], wo_ref[:, column(j, width)]) for j in range(blocks)], axis=1
    )
    middle = own_part(x_ref, conv.shape[0]).astype(F32) + branch
    gain = gain_ref[...].reshape(1, -1)
    xhat, r = norm_stats(middle)
    normed = xhat * gain
    n2 = normed.astype(BF)
    og = og_ref[...]
    downs, backs = [], []
    for j in range(blocks):
        down, back = glu_block(
            n2[:, column(j, width)],
            og[:, column(j, width)],
            [(ga_ref[j, 0], ga_ref[j, 1]), (gb_ref[j, 0], gb_ref[j, 1])],
            [da_ref[:, column(j, width)], db_ref[:, column(j, width)]],
        )
        downs.append(down)
        backs.append(back)
    out_ref[...] = (middle + jnp.concatenate(downs, axis=1)).astype(BF)
    n2_grad = jnp.concatenate(backs, axis=1)
    mid_grad = og.astype(F32) + norm_backward(n2_grad, gain, xhat, r)
    mid_ref[...] = mid_grad
    bg = mid_grad.astype(BF)
    gated_grad = jnp.concatenate(
        [mm_nt(bg[:, column(j, width)], wo_ref[:, column(j, width)]) for j in range(blocks)], axis=1
    )
    gg_ref[...] = gated_grad.T.astype(BF)
    gain_out[...] = jnp.sum(n2_grad * xhat, axis=0, keepdims=True).reshape(-1)
    weight = jnp.concatenate(
        [mm_tn(gated_low[:, column(j, width)], bg[:, column(j, width)]) for j in range(blocks)], axis=1
    ).astype(BF)
    lanes = wo_out.shape[1]
    wo_out[...] = jnp.concatenate([weight[:, :lanes], weight[:, lanes:]], axis=0)
    turned = normed.T.astype(BF)
    for j in range(blocks):
        keep_ref[j] = turned[column(j, width)]
    plane = lax.div(lax.axis_index("seq"), per_plane)
    for d, out in enumerate((z0, z1, z2, z3)):
        out[...] = keep_ref[lax.bitwise_xor(plane, d)]


def middle_part(conv, sm2, x, og, gain, wo, ga, gb, da, db, per_plane):
    rows, model = og.shape
    width = wo.shape[0]
    return pl.pallas_call(
        functools.partial(middle_kernel, per_plane),
        in_specs=vmem_specs(10),
        out_specs=vmem_specs(9),
        out_shape=[
            jax.ShapeDtypeStruct((model, rows), BF),
            jax.ShapeDtypeStruct((rows, model), F32),
            jax.ShapeDtypeStruct((rows, model), BF),
            jax.ShapeDtypeStruct((2 * width, model // 2), BF),
            jax.ShapeDtypeStruct((model,), F32),
        ]
        + [jax.ShapeDtypeStruct((width, rows), BF)] * 4,
        scratch_shapes=[pltpu.VMEM((model // width, width, rows), BF)],
        compiler_params=params(),
        cost_estimate=cost(9 * 10**9, 6 * 10**6),
        name="middle_part",
    )(conv, sm2, x, og, gain, wo, ga, gb, da, db)


def glu_grad_kernel(per_plane, za, zb, zc, zd, oa, ob, oc, od, ga_ref, gb_ref, da_ref, db_ref, own_ref, other_ref):
    j = lax.div(lax.axis_index("seq"), per_plane)
    width = ga_ref.shape[2]
    xt = jnp.concatenate([ref[...] for ref in (za, zb, zc, zd)], axis=1)
    ot = jnp.concatenate([ref[width:, :] for ref in (oa, ob, oc, od)], axis=1)
    x = xt.astype(F32).T.astype(BF)
    og = ot.astype(F32).T.astype(BF)
    for g_ref, d_ref, out_ref in ((gb_ref, db_ref, other_ref), (ga_ref, da_ref, own_ref)):
        wg, wu = g_ref[j, 0], g_ref[j, 1]
        wd = d_ref[:, :width]
        for k in range(1, d_ref.shape[1] // width):
            wd = jnp.where(j == k, d_ref[:, column(k, width)], wd)
        gate = mm(x, wg)
        up = mm(x, wu)
        phi, e = erf_parts(gate)
        act = gate * phi
        hidden = (act * up).astype(BF)
        hg = mm_nt(og, wd)
        slope = phi + gate * (e * (1.0 / math.sqrt(2.0 * math.pi)))
        out_ref[0:width, :] = mm(xt, (hg * up * slope).astype(BF)).astype(out_ref.dtype)
        out_ref[width : 2 * width, :] = mm(xt, (hg * act).astype(BF)).astype(out_ref.dtype)
        out_ref[2 * width : 3 * width, :] = mm(ot, hidden).astype(out_ref.dtype)


def glu_grads(z_parts, o_parts, ga, gb, da, db, per_plane):
    width, half = ga.shape[2:]
    return pl.pallas_call(
        functools.partial(glu_grad_kernel, per_plane),
        in_specs=vmem_specs(12),
        out_specs=vmem_specs(2),
        out_shape=[
            jax.ShapeDtypeStruct((3 * width, half), F32),
            jax.ShapeDtypeStruct((3 * width, half), BF),
        ],
        compiler_params=params(),
        cost_estimate=cost(9 * 10**9, 4 * 10**6),
        name="glu_grads",
    )(*z_parts, *o_parts, ga, gb, da, db)


def plane_add_kernel(own_ref, other_ref, mine_ref, theirs_ref, out_ref):
    total = (own_ref[...] + other_ref[...].astype(F32)).astype(BF)
    extra = (mine_ref[...].astype(F32) + theirs_ref[...].astype(F32)).astype(BF)
    count = out_ref.shape[0]
    rows, more = total.shape[0] // count, extra.shape[0] // count
    for k in range(count):
        out_ref[k, :rows, :] = total[k * rows : (k + 1) * rows]
        out_ref[k, rows:, :] = extra[k * more : (k + 1) * more]


def plane_add(own, other, mine, theirs, count):
    half = own.shape[1]
    rows = (own.shape[0] + mine.shape[0]) // count
    return pl.pallas_call(
        plane_add_kernel,
        in_specs=vmem_specs(4),
        out_specs=vmem_specs(1)[0],
        out_shape=jax.ShapeDtypeStruct((count, rows, half), BF),
        compiler_params=params(),
        cost_estimate=cost(10**8, 2 * 10**6),
        name="plane_add",
    )(own, other, mine, theirs)


def plane_join_kernel(cut, a0, a1, a2, a3, out_ref):
    refs = (a0, a1, a2, a3)
    last = sum(ref[cut:, :].astype(F32) for ref in refs).astype(BF)
    if len(out_ref.shape) == 2:
        for z, ref in enumerate(refs):
            out_ref[z * cut : (z + 1) * cut, :] = ref[:cut, :]
        out_ref[4 * cut :, :] = last
        return
    for k in range(out_ref.shape[0]):
        for z, ref in enumerate(refs):
            out_ref[k, z * cut : (z + 1) * cut, :] = ref[:cut, :]
        out_ref[k, 4 * cut :, :] = last


def plane_join(parts, cut, copies=()):
    rows, half = parts[0].shape
    return pl.pallas_call(
        functools.partial(plane_join_kernel, cut),
        in_specs=vmem_specs(4),
        out_specs=vmem_specs(1)[0],
        out_shape=jax.ShapeDtypeStruct((*copies, 3 * cut + rows, half), BF),
        compiler_params=params(),
        cost_estimate=cost(10**8, 2 * 10**6),
        name="plane_join",
    )(*parts)


def plane_sum_kernel(x_ref, out_ref):
    out_ref[...] = sum(x_ref[k].astype(F32) for k in range(x_ref.shape[0])).astype(BF)


def plane_sum(parts):
    return pl.pallas_call(
        plane_sum_kernel,
        in_specs=vmem_specs(1),
        out_specs=vmem_specs(1)[0],
        out_shape=jax.ShapeDtypeStruct(parts.shape[1:], BF),
        compiler_params=params(),
        cost_estimate=cost(10**8, 2 * 10**6),
        name="plane_sum",
    )(parts)


def finish_kernel(per_plane, width, a_ref, half_ref, back_ref,
                  gi_ref, go_ref, wo_ref, in_ref, keep_ref, last_ref):
    seq = lax.axis_index("seq")
    plane = lax.div(seq, per_plane)
    blocks, pieces, cut, half = keep_ref.shape
    for k in range(pieces):
        for z in range(blocks):
            keep_ref[lax.bitwise_xor(plane, z), k] = a_ref[k, z * cut : (z + 1) * cut, :].astype(F32)
        last_ref[k] = a_ref[k, blocks * cut :, :].astype(F32)
    outs = []
    for j in range(blocks):
        block = jnp.concatenate([keep_ref[j, k] for k in range(pieces)], axis=0)
        gi_ref[j, :, 0, :] = block[:width]
        gi_ref[j, :, 1, :] = block[width : 2 * width]
        outs.append(block[2 * width : 3 * width].T)
    go_ref[...] = jnp.concatenate(outs, axis=1)
    wo_ref[: width // 2, :half] = last_ref[0]
    wo_ref[width // 2 :, :half] = last_ref[1]
    wo_ref[: width // 2, half:] = last_ref[2]
    wo_ref[width // 2 :, half:] = last_ref[3]
    count = half_ref.shape[0]
    me = lax.axis_index("tp")
    in_ref[pl.ds(pl.multiple_of(me * count, count), count), :] = half_ref[...]
    in_ref[pl.ds(pl.multiple_of((1 - me) * count, count), count), :] = back_ref[...]


def finish(sums, half_rows, other_rows, per_plane, width):
    half = sums.shape[2]
    model = 4 * width
    return pl.pallas_call(
        functools.partial(finish_kernel, per_plane, width),
        in_specs=vmem_specs(3),
        out_specs=vmem_specs(4),
        out_shape=[
            jax.ShapeDtypeStruct((4, width, 2, half), F32),
            jax.ShapeDtypeStruct((half, model), F32),
            jax.ShapeDtypeStruct((width, model), F32),
            jax.ShapeDtypeStruct((2 * half_rows.shape[0], model), BF),
        ],
        scratch_shapes=[pltpu.VMEM((4, 4, 3 * width // 4, half), F32), pltpu.VMEM((4, width // 2, half), F32)],
        compiler_params=params(),
        cost_estimate=cost(10**8, 6 * 10**6),
        name="finish",
    )(sums, half_rows, other_rows)


def in_unpack_kernel(place, turns, w_ref, gain_ref, *refs):
    tiles, (gi_ref, st_ref, gain_out, w1_ref, b1_ref, w2_ref, gain2_ref, keep_ref) = refs[:-8], refs[-8:]
    _, width, model = gi_ref.shape
    count, rows3, _ = keep_ref.shape
    small = None
    for ref, (turn,) in zip(tiles, turns):
        for z in range(4):
            keep_ref[source_of(place, turn, z)] = ref[z * rows3 : (z + 1) * rows3, :].astype(F32)
        part = ref[4 * rows3 :, :].astype(F32)
        small = part if small is None else small + part
    hidden = w2_ref.shape[0]
    more = small.shape[0]
    w2_ref[:more, :] = small[:, :LANES]
    w2_ref[more:, :] = small[: hidden - more, LANES:]
    rest = small[hidden - more : hidden - more + 8, LANES:]
    w1_ref[...] = rest[:5]
    b1_ref[...] = rest[5:6].reshape(-1)
    rest = small[hidden - more + 8 :, LANES:]
    for k in range(model // LANES):
        gain2_ref[k * LANES : (k + 1) * LANES] = rest[k : k + 1].reshape(-1)
    chans = rows3 // 3
    blocks = model // width
    per_block = count // blocks
    gains = []
    for j in range(blocks):
        acc = None
        for p in range(3):
            got = jnp.concatenate(
                [keep_ref[j * per_block + k, p * chans : (p + 1) * chans, :] for k in range(per_block)], axis=0
            )
            turned = got.T
            gi_ref[p, :, column(j, width)] = turned[:width]
            for k in range(3):
                st_ref[k, p : p + 1, column(j, width)] = turned[width + k : width + k + 1]
            part = turned[:width] * w_ref[p, :, column(j, width)].astype(F32)
            acc = part if acc is None else acc + part
        gains.append(jnp.sum(acc.T, axis=0, keepdims=True))
    gain_out[...] = (jnp.concatenate(gains, axis=1) / gain_ref[...].reshape(1, -1)).reshape(-1)


def in_unpack(tiles, turns, place, w, gain):
    rows3 = (tiles[0].shape[0] - SMALL_ROWS) // 4
    hidden = LANES
    count = 4 * len(tiles)
    _, width, model = w.shape
    return pl.pallas_call(
        functools.partial(in_unpack_kernel, place, turns),
        in_specs=vmem_specs(2 + len(tiles)),
        out_specs=vmem_specs(7),
        out_shape=[
            jax.ShapeDtypeStruct((3, width, model), F32),
            jax.ShapeDtypeStruct((3, 3, model), F32),
            jax.ShapeDtypeStruct((model,), F32),
            jax.ShapeDtypeStruct((5, hidden), F32),
            jax.ShapeDtypeStruct((hidden,), F32),
            jax.ShapeDtypeStruct((hidden, hidden), F32),
            jax.ShapeDtypeStruct((model,), F32),
        ],
        scratch_shapes=[pltpu.VMEM((count, rows3, 2 * LANES), F32)],
        compiler_params=params(),
        cost_estimate=cost(10**8, 4 * 10**6),
        name="in_unpack",
    )(w, gain, *tiles)


def mixer_back_kernel(by_source, pg_ref, mid_ref, x_ref, gain_ref, w_ref, in_ref):
    rows, model = mid_ref.shape
    width = w_ref.shape[1]
    blocks = model // width
    if by_source:
        pg = pg_ref[...].astype(F32)
        count, rows3, _ = pg.shape
        chans = rows3 // 3
        parts = [
            pg[:, p * chans : (p + 1) * chans, :].reshape(count * chans, rows).astype(BF) for p in range(3)
        ]
    else:
        parts = [pg_ref[p] for p in range(3)]
    grads = []
    for j in range(blocks):
        total = None
        for p in range(3):
            part = mm(w_ref[p, :, column(j, width)], parts[p][column(j, width)])
            total = part if total is None else total + part
        grads.append(total)
    n1_grad = jnp.concatenate(grads, axis=0).T
    xhat, r = norm_stats(own_part(x_ref, rows).astype(F32))
    in_ref[...] = (mid_ref[...] + norm_backward(n1_grad, gain_ref[...].reshape(1, -1), xhat, r)).astype(BF)


def mixer_back(pg, mid, x, gain, w, by_source):
    return pl.pallas_call(
        functools.partial(mixer_back_kernel, by_source),
        in_specs=vmem_specs(5),
        out_specs=vmem_specs(1)[0],
        out_shape=jax.ShapeDtypeStruct(mid.shape, BF),
        compiler_params=params(),
        cost_estimate=cost(3 * 10**9, 4 * 10**6),
        name="mixer_back",
    )(pg, mid, x, gain, w)


def after(x, *others):
    return lax.optimization_barrier((x,) + others)[0]


def permuted(x, axes, count, by):
    pairs = [(i, i + by) for i in range(count) if 0 <= i + by < count]
    return lax.ppermute(x, axes, pairs)


def swapped(x):
    return lax.ppermute(x, "tp", [(0, 1), (1, 0)])


def crossed(x, mask):
    devices = lax.axis_size("seq")
    return lax.ppermute(x, "seq", [(i, i ^ mask) for i in range(devices)])


def exchanged(x, axes, groups=None):
    return lax.all_to_all(x, axes, 0, 0, axis_index_groups=groups, tiled=True)


def gathered_over(x, count, groups=None):
    return exchanged(jnp.broadcast_to(x[None], (count,) + x.shape), "seq", groups)


def local(
    layer_input,
    mixer_gain,
    in_proj,
    short_taps,
    filter_w1,
    filter_b1,
    filter_w2,
    filter_w3,
    filter_decay,
    out_proj,
    glu_gain,
    glu_in,
    glu_out,
    out_grad,
):
    tok_rows, model = layer_input.shape
    width = in_proj.shape[0]
    blocks = model // width
    half = glu_out.shape[0]
    seq_devices = lax.axis_size("seq")
    tp_devices = lax.axis_size("tp")
    devices = seq_devices * tp_devices
    both = ("seq", "tp")
    rows = tok_rows // tp_devices
    seq_length = min(MIN_LEN, tok_rows * seq_devices)
    seqs = tok_rows * seq_devices // seq_length
    per_plane = seq_devices // blocks
    quick = per_plane == 4 and not SLOW_PATH
    place = (per_plane, quick)
    chans = model // devices
    chans_padded = -(-chans // GROUP) * GROUP
    spare = chans_padded - chans
    hidden = filter_w2.shape[0]
    tp_index = lax.axis_index("tp")
    linear = lax.axis_index("seq") * tp_devices + tp_index
    tables = transform_tables(seq_length)
    features = feature_table(seq_length)
    within = [[g * per_plane + r for r in range(per_plane)] for g in range(blocks)]

    halo = permuted(layer_input[tok_rows - 16 :], "seq", seq_devices, 1)

    w3t = filter_w3.T.reshape(tp_devices, chans, hidden)
    w3t = jnp.pad(w3t, ((0, 0), (0, spare), (0, 0))).reshape(tp_devices * chans_padded, hidden)
    decay = jnp.pad(filter_decay.reshape(tp_devices, chans), ((0, 0), (0, spare))).reshape(-1)
    lag_own, lag_other, *saved = filter_forward(features, filter_w1, filter_b1, filter_w2, w3t, decay)
    lag_back = swapped(lag_other)

    w_in = in_proj.transpose(1, 0, 2)
    conv_rows, sm2, *sent = mixer_in(
        layer_input, after(halo, lag_own), mixer_gain, w_in, short_taps, out_grad, per_plane, seq_length
    )

    def to_channels(x):
        out = exchanged(x.reshape(devices, chans, rows), both)
        return jnp.pad(out, ((0, 0), (0, spare), (0, 0)))

    def to_tokens(x):
        return exchanged(x[:, :chans], both).reshape(model, rows)

    conv_channels = to_channels(conv_rows)
    early = [sent[0]] + [crossed(sent[d], d * per_plane) for d in range(1, blocks)]
    glu_own = after(glu_in, conv_rows).transpose(0, 2, 1, 3)
    down_own = after(glu_out, conv_rows)
    glu_other = swapped(glu_own)
    down_other = swapped(down_own)
    spectrum = filter_spectrum(after(lag_own, glu_own), lag_back, tables)
    conv_out, signal_spec = conv_forward(after(conv_channels, spectrum), spectrum, tables, seqs)
    conv_tokens = to_tokens(conv_out)

    early = [after(x, conv_out) for x in early]
    rows_in = jnp.stack([x[:width] for x in early])
    if quick:
        plane_tiles = [rows_in] + [crossed(rows_in, d) for d in range(1, per_plane)]
        turns = [[(0, d)] for d in range(per_plane)]
    else:
        plane_tiles = [gathered_over(rows_in, per_plane, within).reshape(per_plane * blocks, width, rows)]
        turns = [[(0, r) for r in range(per_plane)]]
    gated_grad, mid, layer_output, extra, gain_sum, *sent = middle_part(
        conv_tokens, sm2, layer_input, out_grad, glu_gain, out_proj, glu_own, glu_other,
        down_own, down_other, per_plane
    )
    gated_channels = to_channels(gated_grad)
    across = lambda parts: [parts[0]] + [crossed(parts[d], d * per_plane) for d in range(1, blocks)]
    late = across(sent)
    extra_back = swapped(extra)
    plane_tiles = [after(x, gated_grad) for x in plane_tiles]
    tiles = plane_tiles + [swapped(x) for x in plane_tiles]
    turns = turns + [[(1, r) for _, r in t] for t in turns]
    turns = tuple(tuple(t) for t in turns)
    proj_channels, mixed_channels = channel_mixer(tiles, turns, place, w_in, short_taps, devices, seqs, chans)

    late = [after(x, proj_channels, gated_channels) for x in late]
    g_own, g_other = glu_grads(late, early, glu_own, glu_other, down_own, down_other, per_plane)
    g_back = swapped(g_other)
    if quick:
        sums = exchanged(plane_add(g_own, g_back, extra, extra_back, per_plane), "seq", within)

    pg, grad_spec, tap_sums = conv_backward(
        after(gated_channels, g_own), mixed_channels, proj_channels, conv_out, short_taps, spectrum, tables, seqs, chans
    )
    pg_sent = pg.reshape(devices, 3, chans_padded, rows)[:, :, :chans].reshape(devices, 3 * chans, rows)
    if quick:
        pg_sent = after(pg_sent, sums)
    pg_tokens = exchanged(pg_sent, both)
    if chans != chans_padded:
        pg_tokens = pg_tokens.reshape(devices, 3, chans, rows).transpose(1, 0, 2, 3).reshape(3, model, rows)

    if quick:
        glu_piece = plane_sum(after(sums, pg))
        glu_parts = across([glu_piece] * blocks)
        grad_spec = after(grad_spec, glu_piece)
    fg_own, fg_other = filter_grad_of(grad_spec, signal_spec, chans_padded, seq_length, tables, seqs)
    fg_back = swapped(fg_other)
    in_piece = in_grads(tiles, turns, place, pg, after(tap_sums, fg_own))
    in_piece, g3 = filter_backward(fg_own, fg_back, features, filter_w2, w3t, decay, saved, in_piece, gain_sum)
    g3_back = swapped(g3)
    if quick:
        in_parts = across([in_piece] * blocks)
        glu_parts = plane_join([after(x, in_piece) for x in glu_parts], 3 * width // per_plane, (per_plane,))
        glu_full = exchanged(glu_parts, "seq", within)
        pg_tokens = after(pg_tokens, glu_parts)
    input_half = mixer_back(pg_tokens, mid, layer_input, mixer_gain, w_in, chans == chans_padded)
    input_other = swapped(input_half)

    if quick:
        in_parts = plane_join([after(x, input_half) for x in in_parts], 3 * chans_padded)
        in_full = [in_parts] + [crossed(in_parts, d) for d in range(1, per_plane)]
        in_full = in_full + [swapped(x) for x in in_full]
        glu_in_grad, glu_out_grad, out_proj_grad, input_grad = finish(
            glu_full, input_half, input_other, per_plane, width
        )
        in_proj_grad, short_taps_grad, mixer_gain_grad, w1_grad, b1_grad, w2_grad, glu_gain_grad = in_unpack(
            [after(x, out_proj_grad) for x in in_full], turns, place, w_in, mixer_gain
        )
        in_proj_grad = in_proj_grad.transpose(1, 0, 2)
    else:
        total = (g_own + g_back.astype(F32)).astype(BF)
        piece = exchanged(total, "seq", within).reshape(per_plane, -1, half)
        piece = jnp.sum(piece.astype(F32), axis=0).astype(BF)
        full = gathered_over(piece, seq_devices).reshape(blocks, -1, half).astype(F32)
        glu_in_grad = full[:, : 2 * width].reshape(blocks, 2, width, half).transpose(0, 2, 1, 3)
        glu_out_grad = full[:, 2 * width :].transpose(2, 0, 1).reshape(half, model)
        total = (extra.astype(F32) + extra_back.astype(F32)).astype(BF)
        piece = exchanged(total, "seq").reshape(seq_devices, -1, model // 2)
        piece = jnp.sum(piece.astype(F32), axis=0).astype(BF)
        full = gathered_over(piece, seq_devices).reshape(2, width, model // 2).astype(F32)
        out_proj_grad = full.transpose(1, 0, 2).reshape(width, model)
        mine = gathered_over(in_piece, seq_devices)
        theirs = swapped(mine)
        pair = jnp.where(tp_index == 0, jnp.stack([mine, theirs], 1), jnp.stack([theirs, mine], 1)).astype(F32)
        pair = pair.reshape(devices, -1, 2 * LANES)
        small = jnp.sum(pair[:, 3 * chans_padded :], axis=0)
        small = jnp.concatenate([small[:, :LANES], small[:, LANES:]], axis=0)
        w1_grad, b1_grad, w2_grad = small[hidden : hidden + 5], small[hidden + 5], small[:hidden]
        glu_gain_grad = small[hidden + 8 : hidden + 8 + model // LANES].reshape(model)
        pair = pair[:, : 3 * chans_padded].reshape(devices, 3, chans_padded, 2 * LANES)[:, :, :chans]
        pair = pair.transpose(1, 0, 2, 3).reshape(3, model, 2 * LANES)
        in_proj_grad = pair[:, :, :width].transpose(2, 0, 1)
        short_taps_grad = pair[:, :, width : width + 3].transpose(2, 0, 1)
        products = in_proj_grad * in_proj.astype(F32)
        products = jnp.sum(products.reshape(width, 3, blocks, width), axis=(1, 3))
        mixer_gain_grad = products.T.reshape(model) / mixer_gain
        input_grad = jnp.where(
            tp_index == 0,
            jnp.concatenate([input_half, input_other], axis=0),
            jnp.concatenate([input_other, input_half], axis=0),
        )

    mine = g3[:chans] + g3_back[chans_padded : chans_padded + chans]
    theirs = g3[chans_padded : chans_padded + chans] + g3_back[:chans]
    g3_full = jnp.where(
        tp_index == 0, jnp.concatenate([mine, theirs], axis=0), jnp.concatenate([theirs, mine], axis=0)
    ).T
    return (
        layer_output,
        input_grad,
        mixer_gain_grad,
        in_proj_grad,
        short_taps_grad,
        w1_grad,
        b1_grad,
        w2_grad,
        g3_full,
        out_proj_grad,
        glu_gain_grad,
        glu_in_grad,
        glu_out_grad,
    )


def solution(mesh):
    placed = (
        P("seq", None),
        P(),
        P(),
        P(),
        P(),
        P(),
        P(),
        P(None, "seq"),
        P("seq"),
        P(),
        P(),
        P(None, None, None, "tp"),
        P("tp", None),
        P(("seq", "tp"), None),
    )
    return jax.shard_map(
        local,
        mesh=mesh,
        in_specs=placed,
        out_specs=(
            P(("seq", "tp"), None),
            P("seq", None),
            P(),
            P(),
            P(),
            P(),
            P(),
            P(),
            P(None, "seq"),
            P(),
            P(),
            P(None, None, None, "tp"),
            P("tp", None),
        ),
        check_vma=False,
    )
```

```python
import math
import functools

import jax
import jax.numpy as jnp
import ml_dtypes
import numpy as np
from jax import lax
from jax.experimental import pallas as pl
from jax.experimental.pallas import tpu as pltpu
from jax.sharding import PartitionSpec as P

MIN_LEN = 8192
SLOW_PATH = False
EPSILON = 1e-05
LANES = 128
GROUP = 8
FILTER_LANES = 2048
SMALL_ROWS = 72
BF = jnp.bfloat16
F32 = jnp.float32

PI_HIGH = 3.140625
ROUNDER = 12582912.0
PI_LOW = 9.67653589793e-4
SIN_C = (1.0, -0.16666647791862488, 0.00833289884030819, -0.0001980081869987771, 2.590327312645968e-06)
COS_C = (0.9999999403953552, -0.4999990463256836, 0.041663575917482376, -0.0013853635173290968, 2.315232813998591e-05)


def vmem_specs(count):
    return [pl.BlockSpec(memory_space=pltpu.VMEM)] * count


def params(mib=60):
    return pltpu.CompilerParams(vmem_limit_bytes=mib * 1024 * 1024)


def cost(flops, bytes_accessed=0, transcendentals=0):
    return pl.CostEstimate(flops=flops // 20, bytes_accessed=bytes_accessed // 20, transcendentals=0)


def split_np(table):
    high = np.asarray(table, np.float32).astype(ml_dtypes.bfloat16)
    low = (np.asarray(table, np.float64) - high.astype(np.float64)).astype(ml_dtypes.bfloat16)
    return high, low


def split3_np(table):
    table = np.asarray(table, np.float64)
    high = table.astype(np.float32).astype(ml_dtypes.bfloat16)
    rest = table - high.astype(np.float64)
    mid = rest.astype(np.float32).astype(ml_dtypes.bfloat16)
    low = (rest - mid.astype(np.float64)).astype(np.float32).astype(ml_dtypes.bfloat16)
    return high, mid, low


@functools.lru_cache(maxsize=None)
def transform_tables(seq_length):
    period = 2 * seq_length
    first = period // LANES
    kept = first // 2 + 1
    padded = -(-kept // 8) * 8
    k = np.arange(padded)
    live = (k < kept).astype(np.float64)
    n = np.arange(first)
    angle = 2 * np.pi / first * ((k[:, None] * n[None, :]) % first)
    eye = np.eye(GROUP)
    stage = np.zeros((GROUP, 2, padded, first, GROUP))
    stage[:, 0] = np.einsum("kn,cd->cknd", np.cos(angle) * live[:, None], eye)
    stage[:, 1] = np.einsum("kn,cd->cknd", -np.sin(angle) * live[:, None], eye)
    forward = stage.reshape(GROUP * 2 * padded, first * GROUP)
    backward = forward.T
    m = np.arange(LANES)
    turn = 2 * np.pi / period * ((k[:, None] * m[None, :]) % period)
    weight = np.where((k == 0) | (k == first // 2), 1.0, 2.0) * live / period
    twiddle = np.stack(
        [np.cos(turn), np.sin(turn), np.cos(turn) * weight[:, None], np.sin(turn) * weight[:, None]]
    ).astype(np.float32)
    inner = 2 * np.pi / LANES * ((m[:, None] * m[None, :]) % LANES)
    c, s = np.cos(inner), np.sin(inner)
    second = np.block([[c, -s], [s, c]])
    return {
        "forward": split_np(forward),
        "backward": split_np(backward),
        "forward_used": split_np(forward[:, : first // 2 * GROUP]),
        "backward_used": split_np(backward[: first // 2 * GROUP]),
        "twiddle": twiddle,
        "second": split_np(second),
        "inverse": split_np(second.T),
        "first": first,
        "padded": padded,
    }


@functools.lru_cache(maxsize=None)
def feature_table(seq_length):
    period = 2 * seq_length
    index = np.arange(period)
    lag = np.where(index < seq_length, index, index - period)
    q = lag / seq_length
    rows = [q, np.cos(2 * np.pi * q), np.cos(4 * np.pi * q), np.sin(2 * np.pi * q), np.sin(4 * np.pi * q)]
    rows.append(np.ones_like(q))
    rows += [np.zeros_like(q)] * 2
    high, mid, low = split3_np(np.stack(rows))
    return np.concatenate([high, high, mid, high, mid, low], axis=0)


def split(values):
    high = values.astype(BF)
    low = (values - high.astype(F32)).astype(BF)
    return high, low


def first_weights(w1_ref, b1_ref):
    hidden = w1_ref.shape[1]
    rows = jnp.concatenate([w1_ref[...], b1_ref[...].reshape(1, hidden), jnp.zeros((2, hidden), F32)], axis=0)
    high = rows.astype(BF).astype(F32)
    mid = (rows - high).astype(BF).astype(F32)
    low = rows - high - mid
    return jnp.concatenate([high, mid, high, low, mid, high], axis=0).astype(BF)


def mm(a, b):
    return jnp.dot(a, b, preferred_element_type=F32)


def mm_nt(a, b):
    return lax.dot_general(a, b, (((1,), (1,)), ((), ())), preferred_element_type=F32)


def mm_tn(a, b):
    return lax.dot_general(a, b, (((0,), (0,)), ((), ())), preferred_element_type=F32)


def mm3(a, b):
    ah, al = a
    bh, bl = b
    return mm(ah, bh) + (mm(al, bh) + mm(ah, bl))


def mm3_tn(a, b):
    ah, al = a
    bh, bl = b
    return mm_tn(ah, bh) + (mm_tn(al, bh) + mm_tn(ah, bl))


def sine_cosine(x):
    n = (x * (0.5 / math.pi) + ROUNDER) - ROUNDER
    t = (x * 0.5 - n * PI_HIGH) - n * PI_LOW
    t2 = t * t
    s = SIN_C[4]
    for c in SIN_C[3::-1]:
        s = s * t2 + c
    s = s * t
    k = COS_C[4]
    for c in COS_C[3::-1]:
        k = k * t2 + c
    twice = s + s
    return twice * k, 1.0 - twice * s


def lag_decay(decay, start, width, seq_length):
    lane = lax.broadcasted_iota(jnp.int32, decay.shape[:1] + (width,), 1) + start
    lag = jnp.where(lane < seq_length, lane, 2 * seq_length - lane).astype(F32)
    return jnp.exp(lag * (decay[:, :1] * (-1.0 / seq_length)))


def stacked_weights(w):
    high, low = split(w)
    zero = jnp.zeros_like(high)
    return jnp.concatenate(
        [jnp.concatenate([high, high], axis=1), jnp.concatenate([low, zero], axis=1)], axis=0
    )


def stacked_product(weights, values):
    out = mm(weights, jnp.concatenate(split(values), axis=0))
    rows = out.shape[0] // 2
    return out[:rows] + out[rows:]


def decay_columns(ref):
    row = jnp.broadcast_to(ref[...].reshape(1, -1), (LANES, ref.shape[0]))
    rows = row.T
    half = ref.shape[0] // 2
    a, b = rows[:half], rows[half:]
    first = lax.axis_index("tp") == 0
    return jnp.concatenate([jnp.where(first, a, b), jnp.where(first, b, a)], axis=0)


def own_first(ref):
    half = ref.shape[0] // 2
    me = lax.axis_index("tp")
    return jnp.concatenate([ref[pl.ds(me * half, half), :], ref[pl.ds((1 - me) * half, half), :]], axis=0)


def filter_forward_kernel(feat_ref, w1_ref, b1_ref, w2_ref, w3_ref, decay_ref, own_ref, other_ref, a_ref, ac_ref, b_ref, bc_ref):
    length = own_ref.shape[1]
    channels = own_ref.shape[0]
    width = min(FILTER_LANES, length)
    begin = lax.axis_index("tp") * length
    w1 = first_weights(w1_ref, b1_ref)
    w2 = stacked_weights(w2_ref[...].T)
    w3 = stacked_weights(own_first(w3_ref))
    decay = decay_columns(decay_ref)
    for lo in range(0, length, width):
        lanes = slice(lo, lo + width)
        start = pl.multiple_of(begin + lo, LANES)
        s1, c1 = sine_cosine(mm_tn(w1, feat_ref[:, pl.ds(start, width)]))
        a_ref[:, lanes] = s1.astype(BF)
        ac_ref[:, lanes] = c1.astype(BF)
        s2, c2 = sine_cosine(stacked_product(w2, s1))
        b_ref[:, lanes] = s2.astype(BF)
        bc_ref[:, lanes] = c2.astype(BF)
        lag = stacked_product(w3, s2) * lag_decay(decay, start, width, length)
        own_ref[:, lanes] = lag[:channels]
        other_ref[:, lanes] = lag[channels:]


def filter_forward(features, w1, b1, w2, w3t, decay):
    hidden = w2.shape[0]
    channels = w3t.shape[0] // 2
    length = features.shape[1] // 2
    return pl.pallas_call(
        filter_forward_kernel,
        in_specs=vmem_specs(6),
        out_specs=vmem_specs(6),
        out_shape=[jax.ShapeDtypeStruct((channels, length), F32)] * 2
        + [jax.ShapeDtypeStruct((hidden, length), BF)] * 4,
        compiler_params=params(),
        cost_estimate=cost(8 * 10**9, 8 * 10**6),
        name="filter_forward",
    )(features, w1, b1, w2, w3t, decay)


def inner_spectrum(a, twiddle_ref, second, padded, columns):
    tc, ts = twiddle_ref[0], twiddle_ref[1]
    parts = []
    for col in range(columns):
        lanes = slice(col * LANES, (col + 1) * LANES)
        for c in range(GROUP):
            base = c * 2 * padded
            re = a[base : base + padded, lanes]
            im = a[base + padded : base + 2 * padded, lanes]
            parts.append(jnp.concatenate([re * tc + im * ts, im * tc - re * ts], axis=1))
    return mm3(split(jnp.concatenate(parts, axis=0)), second)


def signal_of(spec, inverse, twiddle_ref, back, padded, columns):
    b = mm3(split(spec), inverse)
    tc, ts = twiddle_ref[2], twiddle_ref[3]
    cols = []
    for col in range(columns):
        parts = []
        for c in range(GROUP):
            base = (col * GROUP + c) * padded
            re = b[base : base + padded, :LANES]
            im = b[base : base + padded, LANES:]
            parts.append(re * tc - im * ts)
            parts.append(im * tc + re * ts)
        cols.append(jnp.concatenate(parts, axis=0))
    z = split(jnp.concatenate(cols, axis=1))
    return [mm3(rows, z) for rows in back]


def gathered(x, seqs, rows, groups):
    cols = []
    for q in range(seqs):
        for g in range(groups):
            block = x[q * rows : (q + 1) * rows, g * GROUP : (g + 1) * GROUP, :]
            cols.append(block.reshape(rows * GROUP, LANES))
    return jnp.concatenate(cols, axis=1)


def scattered(y, seqs, rows, groups):
    out = []
    for q in range(seqs):
        cols = [
            y[:, (q * groups + g) * LANES : (q * groups + g + 1) * LANES].reshape(rows, GROUP, LANES)
            for g in range(groups)
        ]
        out.append(jnp.concatenate(cols, axis=1))
    return jnp.concatenate(out, axis=0)


def product(a, b, conjugate):
    ar, ai = a[:, :LANES], a[:, LANES:]
    br, bi = b[:, :LANES], b[:, LANES:]
    if conjugate:
        return jnp.concatenate([ar * br + ai * bi, ai * br - ar * bi], axis=1)
    return jnp.concatenate([ar * br - ai * bi, ar * bi + ai * br], axis=1)


def filter_spectrum_kernel(padded, own_ref, other_ref, fh, fl, tw, sh, sl, out_ref):
    groups = own_ref.shape[0] // GROUP
    rows = own_ref.shape[1] // LANES
    used = rows * GROUP
    me = lax.axis_index("tp")
    total = None
    for lag_ref, half in ((own_ref, me), (other_ref, 1 - me)):
        cols = []
        for g in range(groups):
            tiles = [lag_ref[g * GROUP : (g + 1) * GROUP, n * LANES : (n + 1) * LANES] for n in range(rows)]
            cols.append(jnp.concatenate(tiles, axis=0))
        begin = pl.multiple_of(half * used, LANES)
        table = (fh[:, pl.ds(begin, used)], fl[:, pl.ds(begin, used)])
        part = mm3(table, split(jnp.concatenate(cols, axis=1)))
        total = part if total is None else total + part
    out_ref[...] = inner_spectrum(total, tw, (sh[...], sl[...]), padded, groups)


def signal_spectrum(x, seqs, fh, fl, tw, sh, sl, padded):
    rows = x.shape[0] // seqs
    groups = x.shape[1] // GROUP
    used = rows * GROUP
    flat = gathered(x, seqs, rows, groups).astype(BF)
    a = mm(fh[:, :used], flat) + mm(fl[:, :used], flat)
    return inner_spectrum(a, tw, (sh[...], sl[...]), padded, seqs * groups)


def filtered(spec, h_ref, seqs, conjugate, tw, ih, il, bh, bl, padded, shape):
    rows = shape[0] // seqs
    groups = shape[1] // GROUP
    used = rows * GROUP
    prod = product(spec, jnp.concatenate([h_ref[...]] * seqs, axis=0), conjugate)
    (y,) = signal_of(prod, (ih[...], il[...]), tw, [(bh[:used, :], bl[:used, :])], padded, seqs * groups)
    return scattered(y, seqs, rows, groups)


def conv_forward_kernel(padded, seqs, x_ref, h_ref, fh, fl, tw, sh, sl, ih, il, bh, bl, y_ref, spec_ref):
    x = x_ref[...].astype(F32)
    spec = signal_spectrum(x, seqs, fh, fl, tw, sh, sl, padded)
    spec_ref[...] = spec
    y_ref[...] = filtered(spec, h_ref, seqs, False, tw, ih, il, bh, bl, padded, x.shape).astype(BF)


def conv_backward_kernel(padded, seqs, real, g_ref, sm_ref, p_ref, y_ref, saved_ref, taps_ref, h_ref, fh, fl, tw, sh, sl, ih, il, bh, bl,
                         pg_ref, cross_ref, st_ref, icg_ref):
    count, chans, _ = g_ref.shape
    gated = g_ref[...].astype(F32)
    conv_grad = gated * sm_ref[:, 2 * chans :, :]
    spec = signal_spectrum(conv_grad, seqs, fh, fl, tw, sh, sl, padded)
    cross = product(spec, saved_ref[...], True)
    height = cross_ref.shape[0]
    cross_ref[...] = sum(cross[q * height : (q + 1) * height] for q in range(seqs))
    icg = filtered(spec, h_ref, seqs, True, tw, ih, il, bh, bl, padded, g_ref.shape)
    icg_ref[...] = icg.astype(BF).astype(F32)
    per_seq = count // seqs
    taps = tap_columns(taps_ref, real)
    lane = lax.broadcasted_iota(jnp.int32, (3 * chans, LANES), 1)

    def step(i, carry):
        next1, next2, acc0, acc1, acc2 = carry
        n = count - 1 - i
        keep = jnp.where(lax.rem(n + 1, per_seq) == 0, 0.0, 1.0)
        sm = sm_ref[n]
        back = icg_ref[n]
        sg = jnp.concatenate(
            [back * sm[chans : 2 * chans], back * sm[:chans], g_ref[n].astype(F32) * y_ref[n].astype(F32)], axis=0
        )
        r1 = pltpu.roll(sg, LANES - 1, 1)
        r2 = pltpu.roll(sg, LANES - 2, 1)
        s1 = jnp.where(lane < LANES - 1, r1, next1 * keep)
        s2 = jnp.where(lane < LANES - 2, r2, next2 * keep)
        pg_ref[n] = (taps[0] * sg + taps[1] * s1 + taps[2] * s2).astype(BF)
        p = p_ref[n]
        return r1, r2, acc0 + sg * p, acc1 + s1 * p, acc2 + s2 * p

    zero = jnp.zeros((3 * chans, LANES), F32)
    _, _, acc0, acc1, acc2 = lax.fori_loop(0, count, step, (zero,) * 5, unroll=4)
    out = zero
    for k, acc in enumerate((acc0, acc1, acc2)):
        out = jnp.where(lane == k, jnp.sum(acc, axis=1, keepdims=True), out)
    st_ref[...] = out


def filter_spectrum(own, other, tables):
    padded = tables["padded"]
    return pl.pallas_call(
        functools.partial(filter_spectrum_kernel, padded),
        in_specs=vmem_specs(7),
        out_specs=vmem_specs(1)[0],
        out_shape=jax.ShapeDtypeStruct((own.shape[0] * padded, 2 * LANES), F32),
        compiler_params=params(),
        cost_estimate=cost(4 * 10**9, 4 * 10**6),
        name="filter_spectrum",
    )(own, other, *tables["forward"], tables["twiddle"], *tables["second"])


def transforms(tables):
    return (*tables["forward_used"], tables["twiddle"], *tables["second"], *tables["inverse"], *tables["backward_used"])


def conv_forward(x, spectrum, tables, seqs):
    padded = tables["padded"]
    return pl.pallas_call(
        functools.partial(conv_forward_kernel, padded, seqs),
        in_specs=vmem_specs(11),
        out_specs=vmem_specs(2),
        out_shape=[
            jax.ShapeDtypeStruct(x.shape, BF),
            jax.ShapeDtypeStruct((seqs * x.shape[1] * padded, 2 * LANES), F32),
        ],
        compiler_params=params(),
        cost_estimate=cost(5 * 10**9, 6 * 10**6),
        name="conv_forward",
    )(x, spectrum, *transforms(tables))


def conv_backward(gated, mixed, proj, conv_out, saved, taps, spectrum, tables, seqs, real):
    padded = tables["padded"]
    count, chans, _ = gated.shape
    return pl.pallas_call(
        functools.partial(conv_backward_kernel, padded, seqs, real),
        in_specs=vmem_specs(16),
        out_specs=vmem_specs(3),
        out_shape=[
            jax.ShapeDtypeStruct((count, 3 * chans, LANES), BF),
            jax.ShapeDtypeStruct((chans * padded, 2 * LANES), F32),
            jax.ShapeDtypeStruct((3 * chans, LANES), F32),
        ],
        scratch_shapes=[pltpu.VMEM(gated.shape, F32)],
        compiler_params=params(),
        cost_estimate=cost(7 * 10**9, 9 * 10**6),
        name="conv_backward",
    )(gated, mixed, proj, conv_out, saved, taps, spectrum, *transforms(tables))


def source_of(place, turn, group):
    per_plane, relative = place
    seq = lax.axis_index("seq")
    plane = lax.div(seq, per_plane)
    inside = lax.rem(seq, per_plane)
    half, index = turn
    inner = lax.bitwise_xor(inside, index) if relative else index
    return (lax.bitwise_xor(plane, group) * per_plane + inner) * 2 + lax.bitwise_xor(lax.axis_index("tp"), half)


def own_channels(ref, index, chans):
    model = ref.shape[-1]
    linear = lax.axis_index("seq") * 2 + lax.axis_index("tp")
    first = linear * chans
    window = jnp.minimum(lax.div(first, LANES) * LANES, model - 2 * LANES)
    part = ref[index, :, pl.ds(pl.multiple_of(window, LANES), 2 * LANES)].astype(F32)
    part = pltpu.roll(part, lax.rem(2 * LANES - (first - window), 2 * LANES), 1)
    turned = part[:, :LANES].T
    return turned[: -(-chans // GROUP) * GROUP]


def tap_columns(taps_ref, chans):
    out = []
    for k in range(3):
        cols = own_channels(taps_ref, k, chans)
        out.append(jnp.concatenate([jnp.broadcast_to(cols[:, p : p + 1], (cols.shape[0], LANES)) for p in range(3)], axis=0))
    return out


def channel_mixer_kernel(place, turns, seqs, chans, w_ref, taps_ref, *refs):
    tiles, (p_ref, sm_ref) = refs[:-2], refs[-2:]
    count, rows3, _ = p_ref.shape
    wc = jnp.concatenate([own_channels(w_ref, p, chans) for p in range(3)], axis=0).astype(BF)
    for ref, turn_list in zip(tiles, turns):
        for q, turn in enumerate(turn_list):
            x = jnp.concatenate([ref[4 * q + z] for z in range(4)], axis=1)
            p = mm(wc, x).astype(BF).astype(F32)
            for z in range(4):
                p_ref[source_of(place, turn, z)] = p[:, z * LANES : (z + 1) * LANES]
    per_seq = count // seqs
    taps = tap_columns(taps_ref, chans)
    lane = lax.broadcasted_iota(jnp.int32, (rows3, LANES), 1)

    def step(n, carry):
        last1, last2 = carry
        keep = jnp.where(lax.rem(n, per_seq) == 0, 0.0, 1.0)
        p = p_ref[n]
        r1 = pltpu.roll(p, 1, 1)
        r2 = pltpu.roll(p, 2, 1)
        s1 = jnp.where(lane < 1, last1 * keep, r1)
        s2 = jnp.where(lane < 2, last2 * keep, r2)
        sm_ref[n] = taps[0] * p + taps[1] * s1 + taps[2] * s2
        return r1, r2

    zero = jnp.zeros((rows3, LANES), F32)
    lax.fori_loop(0, count, step, (zero, zero), unroll=4)


def channel_mixer(tiles, turns, place, w, taps, count, seqs, chans):
    rows3 = 3 * (-(-chans // GROUP) * GROUP)
    return pl.pallas_call(
        functools.partial(channel_mixer_kernel, place, turns, seqs, chans),
        in_specs=vmem_specs(2 + len(tiles)),
        out_specs=vmem_specs(2),
        out_shape=[jax.ShapeDtypeStruct((count, rows3, LANES), F32)] * 2,
        compiler_params=params(),
        cost_estimate=cost(3 * 10**9, 6 * 10**6),
        name="channel_mixer",
    )(w, taps, *tiles)


def channel_grads_kernel(place, turns, padded, count, pg_ref, st_ref, own_ref, other_ref, tw, ih, il, bh, bl, feat_ref, w2_ref,
                         w3_ref, decay_ref, gain_ref, a_ref, ac_ref, b_ref, bc_ref, *refs):
    tiles, (out_ref, g3_ref, keep_ref, lag_ref) = refs[:count], refs[count:]
    total = None
    for ref, turn_list in zip(tiles, turns):
        for q, turn in enumerate(turn_list):
            x = jnp.concatenate([ref[4 * q + z] for z in range(4)], axis=1)
            g = jnp.concatenate([pg_ref[source_of(place, turn, z)] for z in range(4)], axis=1)
            part = mm_nt(g, x)
            total = part if total is None else total + part
    rows3, width = total.shape
    keep_ref[...] = jnp.zeros_like(keep_ref)
    keep_ref[:rows3, :width] = total
    keep_ref[:rows3, width : width + 3] = st_ref[:, :3]

    length = lag_ref.shape[1]
    rows = length // LANES
    used = rows * GROUP
    channels = lag_ref.shape[0] // 2
    groups = channels // GROUP
    begin = pl.multiple_of(lax.axis_index("tp") * used, LANES)
    back = (bh[pl.ds(begin, used), :], bl[pl.ds(begin, used), :])
    for half, ref in enumerate((own_ref, other_ref)):
        (y,) = signal_of(ref[...], (ih[...], il[...]), tw, [back], padded, groups)
        for g in range(groups):
            base = half * channels + g * GROUP
            for n in range(rows):
                lag_ref[base : base + GROUP, n * LANES : (n + 1) * LANES] = y[
                    n * GROUP : (n + 1) * GROUP, g * LANES : (g + 1) * LANES
                ]

    span = min(FILTER_LANES, length)
    begin = lax.axis_index("tp") * length
    w2 = stacked_weights(w2_ref[...])
    w3 = split(own_first(w3_ref))
    decay = decay_columns(decay_ref)
    g1 = g2 = g3 = 0.0
    for lo in range(0, length, span):
        lanes = slice(lo, lo + span)
        start = pl.multiple_of(begin + lo, LANES)
        wh, wl = split(lag_ref[:, lanes] * lag_decay(decay, start, span, length))
        second = b_ref[:, lanes]
        g3 += mm_nt(wh, second) + mm_nt(wl, second)
        pre2 = mm3_tn(w3, (wh, wl)) * bc_ref[:, lanes].astype(F32)
        g2 += mm_nt(a_ref[:, lanes], pre2.astype(BF))
        pre1 = stacked_product(w2, pre2) * ac_ref[:, lanes].astype(F32)
        g1 += mm_nt(feat_ref[:8, pl.ds(start, span)], pre1.astype(BF))
    g3_ref[...] = g3
    more = out_ref.shape[0] - rows3
    gains = [gain_ref[k * LANES : (k + 1) * LANES].reshape(1, LANES) for k in range(gain_ref.shape[0] // LANES)]
    gains += [jnp.zeros((8 - len(gains), LANES), F32)]
    keep_ref[rows3:, :LANES] = g2[:more]
    keep_ref[rows3:, LANES:] = jnp.concatenate([g2[more:], g1] + gains, axis=0)
    out_ref[...] = keep_ref[...].astype(BF)


def channel_grads(tiles, turns, place, pg, st, own, other, tables, features, w2, w3t, decay, gain, saved):
    rows3 = pg.shape[1]
    hidden = w2.shape[0]
    length = features.shape[1] // 2
    return pl.pallas_call(
        functools.partial(channel_grads_kernel, place, turns, tables["padded"], len(tiles)),
        in_specs=vmem_specs(18 + len(tiles)),
        out_specs=vmem_specs(2),
        out_shape=[
            jax.ShapeDtypeStruct((rows3 + SMALL_ROWS, 2 * LANES), BF),
            jax.ShapeDtypeStruct((w3t.shape[0], hidden), F32),
        ],
        scratch_shapes=[
            pltpu.VMEM((rows3 + SMALL_ROWS, 2 * LANES), F32),
            pltpu.VMEM((w3t.shape[0], length), F32),
        ],
        compiler_params=params(),
        cost_estimate=cost(8 * 10**9, 8 * 10**6),
        name="channel_grads",
    )(pg, st, own, other, tables["twiddle"], *tables["inverse"], *tables["backward"], features, w2, w3t, decay, gain,
      *saved, *tiles)


def erf_parts(g):
    x = jnp.abs(g) * (1.0 / math.sqrt(2.0))
    t = 1.0 / (1.0 + 0.3275911 * x)
    e = jnp.exp(-x * x)
    poly = t * (0.254829592 + t * (-0.284496736 + t * (1.421413741 + t * (-1.453152027 + t * 1.061405429))))
    tail = 0.5 * poly * e
    return jnp.where(g < 0, tail, 1.0 - tail), e


def norm_stats(v):
    centered = v - jnp.mean(v, axis=-1, keepdims=True)
    variance = jnp.mean(centered * centered, axis=-1, keepdims=True)
    r = lax.rsqrt(variance + EPSILON)
    return centered * r, r


def norm_backward(w, gain, xhat, r):
    a = w * gain
    return r * (a - jnp.mean(a, axis=-1, keepdims=True) - xhat * jnp.mean(a * xhat, axis=-1, keepdims=True))


def column(j, width):
    return slice(j * width, (j + 1) * width)


def own_part(ref, rows):
    return ref[pl.ds(pl.multiple_of(lax.axis_index("tp") * rows, rows), rows), :]


def mixer_in_kernel(per_plane, seq_length, x_ref, halo_ref, gain_ref, w_ref, taps_ref, og_ref, conv_ref, sm2_ref, z0, z1, z2, z3, keep_ref):
    rows = sm2_ref.shape[0]
    width = w_ref.shape[1]
    blocks = w_ref.shape[2] // width
    lead = halo_ref.shape[0]
    linear = lax.axis_index("seq") * 2 + lax.axis_index("tp")
    keep = jnp.where(lax.rem(linear * rows, seq_length) == 0, 0.0, 1.0)
    inner = x_ref[rows - lead : rows, :].astype(F32)
    halo = jnp.where(lax.axis_index("tp") == 0, halo_ref[...].astype(F32), inner) * keep
    x = jnp.concatenate([halo, own_part(x_ref, rows).astype(F32)], axis=0)
    xhat, _ = norm_stats(x)
    normed = xhat * gain_ref[...].reshape(1, -1)
    n1 = normed.astype(BF)
    mixed = []
    for p in range(3):
        proj = jnp.concatenate(
            [mm(n1[:, column(j, width)], w_ref[p, :, column(j, width)]) for j in range(blocks)], axis=1
        )
        proj = proj.astype(BF).astype(F32)
        mixed.append(
            taps_ref[0, p : p + 1, :] * proj[lead:]
            + taps_ref[1, p : p + 1, :] * proj[lead - 1 : lead - 1 + rows]
            + taps_ref[2, p : p + 1, :] * proj[lead - 2 : lead - 2 + rows]
        )
    sm2_ref[...] = mixed[2]
    conv_ref[...] = (mixed[0] * mixed[1]).T.astype(BF)
    nt = normed[lead:].T.astype(BF)
    ot = og_ref[...].astype(F32).T.astype(BF)
    for j in range(blocks):
        keep_ref[j, :width, :] = nt[column(j, width)]
        keep_ref[j, width:, :] = ot[column(j, width)]
    plane = lax.div(lax.axis_index("seq"), per_plane)
    for d, out in enumerate((z0, z1, z2, z3)):
        out[...] = keep_ref[lax.bitwise_xor(plane, d)]


def mixer_in(x, halo, gain, w, taps, og, per_plane, seq_length):
    rows, model = og.shape
    width = w.shape[1]
    return pl.pallas_call(
        functools.partial(mixer_in_kernel, per_plane, seq_length),
        in_specs=vmem_specs(6),
        out_specs=vmem_specs(6),
        out_shape=[jax.ShapeDtypeStruct((model, rows), BF), jax.ShapeDtypeStruct((rows, model), F32)]
        + [jax.ShapeDtypeStruct((2 * width, rows), BF)] * 4,
        scratch_shapes=[pltpu.VMEM((model // width, 2 * width, rows), BF)],
        compiler_params=params(24),
        cost_estimate=cost(4 * 10**9, 4 * 10**6),
        name="mixer_in",
    )(x, halo, gain, w, taps, og)


def glu_block(x, og, w_pairs, d_pairs):
    down = None
    back = None
    for (wg, wu), wd in zip(w_pairs, d_pairs):
        gate = mm(x, wg)
        up = mm(x, wu)
        phi, e = erf_parts(gate)
        act = gate * phi
        hidden = (act * up).astype(BF)
        hg = mm_nt(og, wd)
        slope = phi + gate * (e * (1.0 / math.sqrt(2.0 * math.pi)))
        gg = (hg * up * slope).astype(BF)
        ug = (hg * act).astype(BF)
        down_part = mm(hidden, wd)
        back_part = mm_nt(gg, wg) + mm_nt(ug, wu)
        down = down_part if down is None else down + down_part
        back = back_part if back is None else back + back_part
    return down, back


def middle_kernel(per_plane, conv_ref, sm2_ref, x_ref, og_ref, gain_ref, wo_ref, ga_ref, gb_ref, da_ref, db_ref,
                  gg_ref, mid_ref, out_ref, wo_out, gain_out, z0, z1, z2, z3, keep_ref):
    width = wo_ref.shape[0]
    blocks = wo_ref.shape[1] // width
    conv = conv_ref[...].astype(F32).T
    gated = sm2_ref[...] * conv
    gated_low = gated.astype(BF)
    branch = jnp.concatenate(
        [mm(gated_low[:, column(j, width)], wo_ref[:, column(j, width)]) for j in range(blocks)], axis=1
    )
    middle = own_part(x_ref, conv.shape[0]).astype(F32) + branch
    gain = gain_ref[...].reshape(1, -1)
    xhat, r = norm_stats(middle)
    normed = xhat * gain
    n2 = normed.astype(BF)
    og = og_ref[...]
    downs, backs = [], []
    for j in range(blocks):
        down, back = glu_block(
            n2[:, column(j, width)],
            og[:, column(j, width)],
            [(ga_ref[j, 0], ga_ref[j, 1]), (gb_ref[j, 0], gb_ref[j, 1])],
            [da_ref[:, column(j, width)], db_ref[:, column(j, width)]],
        )
        downs.append(down)
        backs.append(back)
    out_ref[...] = (middle + jnp.concatenate(downs, axis=1)).astype(BF)
    n2_grad = jnp.concatenate(backs, axis=1)
    mid_grad = og.astype(F32) + norm_backward(n2_grad, gain, xhat, r)
    mid_ref[...] = mid_grad
    bg = mid_grad.astype(BF)
    gated_grad = jnp.concatenate(
        [mm_nt(bg[:, column(j, width)], wo_ref[:, column(j, width)]) for j in range(blocks)], axis=1
    )
    gg_ref[...] = gated_grad.T.astype(BF)
    gain_out[...] = jnp.sum(n2_grad * xhat, axis=0, keepdims=True).reshape(-1)
    weight = jnp.concatenate(
        [mm_tn(gated_low[:, column(j, width)], bg[:, column(j, width)]) for j in range(blocks)], axis=1
    ).astype(BF)
    lanes = wo_out.shape[1]
    wo_out[...] = jnp.concatenate([weight[:, :lanes], weight[:, lanes:]], axis=0)
    turned = normed.T.astype(BF)
    for j in range(blocks):
        keep_ref[j] = turned[column(j, width)]
    plane = lax.div(lax.axis_index("seq"), per_plane)
    for d, out in enumerate((z0, z1, z2, z3)):
        out[...] = keep_ref[lax.bitwise_xor(plane, d)]


def middle_part(conv, sm2, x, og, gain, wo, ga, gb, da, db, per_plane):
    rows, model = og.shape
    width = wo.shape[0]
    return pl.pallas_call(
        functools.partial(middle_kernel, per_plane),
        in_specs=vmem_specs(10),
        out_specs=vmem_specs(9),
        out_shape=[
            jax.ShapeDtypeStruct((model, rows), BF),
            jax.ShapeDtypeStruct((rows, model), F32),
            jax.ShapeDtypeStruct((rows, model), BF),
            jax.ShapeDtypeStruct((2 * width, model // 2), BF),
            jax.ShapeDtypeStruct((model,), F32),
        ]
        + [jax.ShapeDtypeStruct((width, rows), BF)] * 4,
        scratch_shapes=[pltpu.VMEM((model // width, width, rows), BF)],
        compiler_params=params(),
        cost_estimate=cost(9 * 10**9, 6 * 10**6),
        name="middle_part",
    )(conv, sm2, x, og, gain, wo, ga, gb, da, db)


def glu_grad_kernel(per_plane, za, zb, zc, zd, oa, ob, oc, od, ga_ref, gb_ref, da_ref, db_ref, own_ref, other_ref):
    j = lax.div(lax.axis_index("seq"), per_plane)
    width = ga_ref.shape[2]
    xt = jnp.concatenate([ref[...] for ref in (za, zb, zc, zd)], axis=1)
    ot = jnp.concatenate([ref[width:, :] for ref in (oa, ob, oc, od)], axis=1)
    x = xt.astype(F32).T.astype(BF)
    og = ot.astype(F32).T.astype(BF)
    for g_ref, d_ref, out_ref in ((gb_ref, db_ref, other_ref), (ga_ref, da_ref, own_ref)):
        wg, wu = g_ref[j, 0], g_ref[j, 1]
        wd = d_ref[:, :width]
        for k in range(1, d_ref.shape[1] // width):
            wd = jnp.where(j == k, d_ref[:, column(k, width)], wd)
        gate = mm(x, wg)
        up = mm(x, wu)
        phi, e = erf_parts(gate)
        act = gate * phi
        hidden = (act * up).astype(BF)
        hg = mm_nt(og, wd)
        slope = phi + gate * (e * (1.0 / math.sqrt(2.0 * math.pi)))
        out_ref[0:width, :] = mm(xt, (hg * up * slope).astype(BF)).astype(out_ref.dtype)
        out_ref[width : 2 * width, :] = mm(xt, (hg * act).astype(BF)).astype(out_ref.dtype)
        out_ref[2 * width : 3 * width, :] = mm(ot, hidden).astype(out_ref.dtype)


def glu_grads(z_parts, o_parts, ga, gb, da, db, per_plane):
    width, half = ga.shape[2:]
    return pl.pallas_call(
        functools.partial(glu_grad_kernel, per_plane),
        in_specs=vmem_specs(12),
        out_specs=vmem_specs(2),
        out_shape=[
            jax.ShapeDtypeStruct((3 * width, half), F32),
            jax.ShapeDtypeStruct((3 * width, half), BF),
        ],
        compiler_params=params(40),
        cost_estimate=cost(9 * 10**9, 4 * 10**6),
        name="glu_grads",
    )(*z_parts, *o_parts, ga, gb, da, db)


def plane_add_kernel(own_ref, other_ref, mine_ref, theirs_ref, out_ref):
    total = (own_ref[...] + other_ref[...].astype(F32)).astype(BF)
    extra = (mine_ref[...].astype(F32) + theirs_ref[...].astype(F32)).astype(BF)
    count = out_ref.shape[0]
    rows, more = total.shape[0] // count, extra.shape[0] // count
    for k in range(count):
        out_ref[k, :rows, :] = total[k * rows : (k + 1) * rows]
        out_ref[k, rows:, :] = extra[k * more : (k + 1) * more]


def plane_add(own, other, mine, theirs, count):
    half = own.shape[1]
    rows = (own.shape[0] + mine.shape[0]) // count
    return pl.pallas_call(
        plane_add_kernel,
        in_specs=vmem_specs(4),
        out_specs=vmem_specs(1)[0],
        out_shape=jax.ShapeDtypeStruct((count, rows, half), BF),
        compiler_params=params(8),
        cost_estimate=cost(10**8, 2 * 10**6),
        name="plane_add",
    )(own, other, mine, theirs)


def plane_join_kernel(cut, a0, a1, a2, a3, out_ref):
    refs = (a0, a1, a2, a3)
    last = sum(ref[cut:, :].astype(F32) for ref in refs).astype(BF)
    if len(out_ref.shape) == 2:
        for z, ref in enumerate(refs):
            out_ref[z * cut : (z + 1) * cut, :] = ref[:cut, :]
        out_ref[4 * cut :, :] = last
        return
    for k in range(out_ref.shape[0]):
        for z, ref in enumerate(refs):
            out_ref[k, z * cut : (z + 1) * cut, :] = ref[:cut, :]
        out_ref[k, 4 * cut :, :] = last


def plane_join(parts, cut, copies=()):
    rows, half = parts[0].shape
    return pl.pallas_call(
        functools.partial(plane_join_kernel, cut),
        in_specs=vmem_specs(4),
        out_specs=vmem_specs(1)[0],
        out_shape=jax.ShapeDtypeStruct((*copies, 3 * cut + rows, half), BF),
        compiler_params=params(8),
        cost_estimate=cost(10**8, 2 * 10**6),
        name="plane_join",
    )(*parts)


def plane_sum_kernel(x_ref, out_ref):
    out_ref[...] = sum(x_ref[k].astype(F32) for k in range(x_ref.shape[0])).astype(BF)


def plane_sum(parts):
    return pl.pallas_call(
        plane_sum_kernel,
        in_specs=vmem_specs(1),
        out_specs=vmem_specs(1)[0],
        out_shape=jax.ShapeDtypeStruct(parts.shape[1:], BF),
        compiler_params=params(8),
        cost_estimate=cost(10**8, 2 * 10**6),
        name="plane_sum",
    )(parts)


def finish_kernel(per_plane, width, a_ref, half_ref, back_ref,
                  gi_ref, go_ref, wo_ref, in_ref, keep_ref, last_ref):
    seq = lax.axis_index("seq")
    plane = lax.div(seq, per_plane)
    blocks, pieces, cut, half = keep_ref.shape
    for k in range(pieces):
        for z in range(blocks):
            keep_ref[lax.bitwise_xor(plane, z), k] = a_ref[k, z * cut : (z + 1) * cut, :].astype(F32)
        last_ref[k] = a_ref[k, blocks * cut :, :].astype(F32)
    outs = []
    for j in range(blocks):
        block = jnp.concatenate([keep_ref[j, k] for k in range(pieces)], axis=0)
        gi_ref[j, :, 0, :] = block[:width]
        gi_ref[j, :, 1, :] = block[width : 2 * width]
        outs.append(block[2 * width : 3 * width].T)
    go_ref[...] = jnp.concatenate(outs, axis=1)
    wo_ref[: width // 2, :half] = last_ref[0]
    wo_ref[width // 2 :, :half] = last_ref[1]
    wo_ref[: width // 2, half:] = last_ref[2]
    wo_ref[width // 2 :, half:] = last_ref[3]
    count = half_ref.shape[0]
    me = lax.axis_index("tp")
    in_ref[pl.ds(pl.multiple_of(me * count, count), count), :] = half_ref[...]
    in_ref[pl.ds(pl.multiple_of((1 - me) * count, count), count), :] = back_ref[...]


def finish(sums, half_rows, other_rows, per_plane, width):
    half = sums.shape[2]
    model = 4 * width
    return pl.pallas_call(
        functools.partial(finish_kernel, per_plane, width),
        in_specs=vmem_specs(3),
        out_specs=vmem_specs(4),
        out_shape=[
            jax.ShapeDtypeStruct((4, width, 2, half), F32),
            jax.ShapeDtypeStruct((half, model), F32),
            jax.ShapeDtypeStruct((width, model), F32),
            jax.ShapeDtypeStruct((2 * half_rows.shape[0], model), BF),
        ],
        scratch_shapes=[pltpu.VMEM((4, 4, 3 * width // 4, half), F32), pltpu.VMEM((4, width // 2, half), F32)],
        compiler_params=params(32),
        cost_estimate=cost(10**8, 6 * 10**6),
        name="finish",
    )(sums, half_rows, other_rows)


def in_unpack_kernel(place, w_ref, gain_ref, *refs):
    tiles, (gi_ref, st_ref, gain_out, w1_ref, b1_ref, w2_ref, gain2_ref, keep_ref) = refs[:-8], refs[-8:]
    _, width, model = gi_ref.shape
    count, rows3, _ = keep_ref.shape
    small = None
    for k, ref in enumerate(tiles):
        half, z = divmod(k, 4)
        for inner in range(4):
            keep_ref[source_of(place, (half, inner), z)] = ref[inner * rows3 : (inner + 1) * rows3, :].astype(F32)
        part = ref[4 * rows3 :, :].astype(F32)
        small = part if small is None else small + part
    hidden = w2_ref.shape[0]
    more = small.shape[0]
    w2_ref[:more, :] = small[:, :LANES]
    w2_ref[more:, :] = small[: hidden - more, LANES:]
    rest = small[hidden - more : hidden - more + 8, LANES:]
    w1_ref[...] = rest[:5]
    b1_ref[...] = rest[5:6].reshape(-1)
    rest = small[hidden - more + 8 :, LANES:]
    for k in range(model // LANES):
        gain2_ref[k * LANES : (k + 1) * LANES] = rest[k : k + 1].reshape(-1)
    chans = rows3 // 3
    blocks = model // width
    per_block = count // blocks
    gains = []
    for j in range(blocks):
        acc = None
        for p in range(3):
            got = jnp.concatenate(
                [keep_ref[j * per_block + k, p * chans : (p + 1) * chans, :] for k in range(per_block)], axis=0
            )
            turned = got.T
            gi_ref[p, :, column(j, width)] = turned[:width]
            for k in range(3):
                st_ref[k, p : p + 1, column(j, width)] = turned[width + k : width + k + 1]
            part = turned[:width] * w_ref[p, :, column(j, width)].astype(F32)
            acc = part if acc is None else acc + part
        gains.append(jnp.sum(acc.T, axis=0, keepdims=True))
    gain_out[...] = (jnp.concatenate(gains, axis=1) / gain_ref[...].reshape(1, -1)).reshape(-1)


def in_unpack(tiles, place, w, gain):
    rows3 = (tiles[0].shape[0] - SMALL_ROWS) // 4
    hidden = LANES
    count = 4 * len(tiles)
    _, width, model = w.shape
    return pl.pallas_call(
        functools.partial(in_unpack_kernel, place),
        in_specs=vmem_specs(2 + len(tiles)),
        out_specs=vmem_specs(7),
        out_shape=[
            jax.ShapeDtypeStruct((3, width, model), F32),
            jax.ShapeDtypeStruct((3, 3, model), F32),
            jax.ShapeDtypeStruct((model,), F32),
            jax.ShapeDtypeStruct((5, hidden), F32),
            jax.ShapeDtypeStruct((hidden,), F32),
            jax.ShapeDtypeStruct((hidden, hidden), F32),
            jax.ShapeDtypeStruct((model,), F32),
        ],
        scratch_shapes=[pltpu.VMEM((count, rows3, 2 * LANES), F32)],
        compiler_params=params(24),
        cost_estimate=cost(10**8, 4 * 10**6),
        name="in_unpack",
    )(w, gain, *tiles)


def mixer_back_kernel(by_source, pg_ref, mid_ref, x_ref, gain_ref, w_ref, in_ref):
    rows, model = mid_ref.shape
    width = w_ref.shape[1]
    blocks = model // width
    if by_source:
        pg = pg_ref[...].astype(F32)
        count, rows3, _ = pg.shape
        chans = rows3 // 3
        parts = [
            pg[:, p * chans : (p + 1) * chans, :].reshape(count * chans, rows).astype(BF) for p in range(3)
        ]
    else:
        parts = [pg_ref[p] for p in range(3)]
    grads = []
    for j in range(blocks):
        total = None
        for p in range(3):
            part = mm(w_ref[p, :, column(j, width)], parts[p][column(j, width)])
            total = part if total is None else total + part
        grads.append(total)
    n1_grad = jnp.concatenate(grads, axis=0).T
    xhat, r = norm_stats(own_part(x_ref, rows).astype(F32))
    in_ref[...] = (mid_ref[...] + norm_backward(n1_grad, gain_ref[...].reshape(1, -1), xhat, r)).astype(BF)


def mixer_back(pg, mid, x, gain, w, by_source):
    return pl.pallas_call(
        functools.partial(mixer_back_kernel, by_source),
        in_specs=vmem_specs(5),
        out_specs=vmem_specs(1)[0],
        out_shape=jax.ShapeDtypeStruct(mid.shape, BF),
        compiler_params=params(16),
        cost_estimate=cost(3 * 10**9, 4 * 10**6),
        name="mixer_back",
    )(pg, mid, x, gain, w)


def after(x, *others):
    return lax.optimization_barrier((x,) + others)[0]


def permuted(x, axes, count, by):
    pairs = [(i, i + by) for i in range(count) if 0 <= i + by < count]
    return lax.ppermute(x, axes, pairs)


def swapped(x):
    return lax.ppermute(x, "tp", [(0, 1), (1, 0)])


def crossed(x, mask):
    devices = lax.axis_size("seq")
    return lax.ppermute(x, "seq", [(i, i ^ mask) for i in range(devices)])


def exchanged(x, axes, groups=None):
    return lax.all_to_all(x, axes, 0, 0, axis_index_groups=groups, tiled=True)


def gathered_over(x, count, groups=None):
    return exchanged(jnp.broadcast_to(x[None], (count,) + x.shape), "seq", groups)


def local(
    layer_input,
    mixer_gain,
    in_proj,
    short_taps,
    filter_w1,
    filter_b1,
    filter_w2,
    filter_w3,
    filter_decay,
    out_proj,
    glu_gain,
    glu_in,
    glu_out,
    out_grad,
):
    tok_rows, model = layer_input.shape
    width = in_proj.shape[0]
    blocks = model // width
    half = glu_out.shape[0]
    seq_devices = lax.axis_size("seq")
    tp_devices = lax.axis_size("tp")
    devices = seq_devices * tp_devices
    both = ("seq", "tp")
    rows = tok_rows // tp_devices
    seq_length = min(MIN_LEN, tok_rows * seq_devices)
    seqs = tok_rows * seq_devices // seq_length
    per_plane = seq_devices // blocks
    quick = per_plane == 4 and not SLOW_PATH
    place = (per_plane, quick)
    chans = model // devices
    chans_padded = -(-chans // GROUP) * GROUP
    spare = chans_padded - chans
    hidden = filter_w2.shape[0]
    tp_index = lax.axis_index("tp")
    linear = lax.axis_index("seq") * tp_devices + tp_index
    tables = transform_tables(seq_length)
    features = feature_table(seq_length)
    within = [[g * per_plane + r for r in range(per_plane)] for g in range(blocks)]

    halo = permuted(layer_input[tok_rows - 16 :], "seq", seq_devices, 1)

    w3t = filter_w3.T.reshape(tp_devices, chans, hidden)
    w3t = jnp.pad(w3t, ((0, 0), (0, spare), (0, 0))).reshape(tp_devices * chans_padded, hidden)
    decay = jnp.pad(filter_decay.reshape(tp_devices, chans), ((0, 0), (0, spare))).reshape(-1)
    lag_own, lag_other, *saved = filter_forward(features, filter_w1, filter_b1, filter_w2, w3t, decay)
    lag_back = swapped(lag_other)

    w_in = in_proj.transpose(1, 0, 2)
    conv_rows, sm2, *sent = mixer_in(
        layer_input, after(halo, lag_own), mixer_gain, w_in, short_taps, out_grad, per_plane, seq_length
    )

    def to_channels(x):
        out = exchanged(x.reshape(devices, chans, rows), both)
        return jnp.pad(out, ((0, 0), (0, spare), (0, 0)))

    def to_tokens(x):
        return exchanged(x[:, :chans], both).reshape(model, rows)

    conv_channels = to_channels(conv_rows)
    early = [sent[0]] + [crossed(sent[d], d * per_plane) for d in range(1, blocks)]
    glu_own = after(glu_in, conv_rows).transpose(0, 2, 1, 3)
    down_own = after(glu_out, conv_rows)
    glu_other = swapped(glu_own)
    down_other = swapped(down_own)
    spectrum = filter_spectrum(after(lag_own, glu_own), lag_back, tables)
    conv_out, signal_spec = conv_forward(after(conv_channels, spectrum), spectrum, tables, seqs)
    conv_tokens = to_tokens(conv_out)

    early = [after(x, conv_out) for x in early]
    rows_in = jnp.stack([x[:width] for x in early])
    if quick:
        plane_tiles = [rows_in] + [crossed(rows_in, d) for d in range(1, per_plane)]
        turns = [[(0, d)] for d in range(per_plane)]
    else:
        plane_tiles = [gathered_over(rows_in, per_plane, within).reshape(per_plane * blocks, width, rows)]
        turns = [[(0, r) for r in range(per_plane)]]
    gated_grad, mid, layer_output, extra, gain_sum, *sent = middle_part(
        conv_tokens, sm2, layer_input, out_grad, glu_gain, out_proj, glu_own, glu_other,
        down_own, down_other, per_plane
    )
    gated_channels = to_channels(gated_grad)
    across = lambda parts: [parts[0]] + [crossed(parts[d], d * per_plane) for d in range(1, blocks)]
    late = across(sent)
    extra_back = swapped(extra)
    plane_tiles = [after(x, gated_grad) for x in plane_tiles]
    tiles = plane_tiles + [swapped(x) for x in plane_tiles]
    turns = turns + [[(1, r) for _, r in t] for t in turns]
    turns = tuple(tuple(t) for t in turns)
    proj_channels, mixed_channels = channel_mixer(tiles, turns, place, w_in, short_taps, devices, seqs, chans)

    late = [after(x, proj_channels, gated_channels) for x in late]
    g_own, g_other = glu_grads(late, early, glu_own, glu_other, down_own, down_other, per_plane)
    g_back = swapped(g_other)
    if quick:
        sums = exchanged(plane_add(g_own, g_back, extra, extra_back, per_plane), "seq", within)

    pg, cross, tap_sums = conv_backward(
        after(gated_channels, g_own), mixed_channels, proj_channels, conv_out, signal_spec, short_taps, spectrum, tables,
        seqs, chans
    )
    pg_sent = pg.reshape(devices, 3, chans_padded, rows)[:, :, :chans].reshape(devices, 3 * chans, rows)
    if quick:
        pg_sent = after(pg_sent, sums)
    pg_tokens = exchanged(pg_sent, both)
    if chans != chans_padded:
        pg_tokens = pg_tokens.reshape(devices, 3, chans, rows).transpose(1, 0, 2, 3).reshape(3, model, rows)

    if quick:
        glu_piece = plane_sum(after(sums, pg))
        glu_parts = across([glu_piece] * blocks)
        tap_sums = after(tap_sums, glu_piece)
    cross_back = swapped(cross)
    in_piece, g3 = channel_grads(
        tiles, turns, place, pg, tap_sums, cross, cross_back, tables, features, filter_w2, w3t, decay, gain_sum, saved
    )
    g3_back = swapped(g3)
    if quick:
        in_parts = [in_piece] + [crossed(in_piece, d) for d in range(1, per_plane)]
        glu_parts = plane_join([after(x, in_piece) for x in glu_parts], 3 * width // per_plane, (per_plane,))
        glu_full = exchanged(after(glu_parts, *in_parts), "seq", within)
        in_parts = plane_join([after(x, glu_parts) for x in in_parts], 3 * chans_padded)
        in_full = across([in_parts] * blocks)
        pg_tokens = after(pg_tokens, in_parts)
    input_half = mixer_back(pg_tokens, mid, layer_input, mixer_gain, w_in, chans == chans_padded)
    input_other = swapped(input_half)

    if quick:
        in_full = in_full + [swapped(x) for x in in_full]
        in_proj_grad, short_taps_grad, mixer_gain_grad, w1_grad, b1_grad, w2_grad, glu_gain_grad = in_unpack(
            [after(x, input_half) for x in in_full], place, w_in, mixer_gain
        )
        glu_in_grad, glu_out_grad, out_proj_grad, input_grad = finish(
            after(glu_full, glu_gain_grad), input_half, input_other, per_plane, width
        )
        in_proj_grad = in_proj_grad.transpose(1, 0, 2)
    else:
        total = (g_own + g_back.astype(F32)).astype(BF)
        piece = exchanged(total, "seq", within).reshape(per_plane, -1, half)
        piece = jnp.sum(piece.astype(F32), axis=0).astype(BF)
        full = gathered_over(piece, seq_devices).reshape(blocks, -1, half).astype(F32)
        glu_in_grad = full[:, : 2 * width].reshape(blocks, 2, width, half).transpose(0, 2, 1, 3)
        glu_out_grad = full[:, 2 * width :].transpose(2, 0, 1).reshape(half, model)
        total = (extra.astype(F32) + extra_back.astype(F32)).astype(BF)
        piece = exchanged(total, "seq").reshape(seq_devices, -1, model // 2)
        piece = jnp.sum(piece.astype(F32), axis=0).astype(BF)
        full = gathered_over(piece, seq_devices).reshape(2, width, model // 2).astype(F32)
        out_proj_grad = full.transpose(1, 0, 2).reshape(width, model)
        mine = gathered_over(in_piece, seq_devices)
        theirs = swapped(mine)
        pair = jnp.where(tp_index == 0, jnp.stack([mine, theirs], 1), jnp.stack([theirs, mine], 1)).astype(F32)
        pair = pair.reshape(devices, -1, 2 * LANES)
        small = jnp.sum(pair[:, 3 * chans_padded :], axis=0)
        small = jnp.concatenate([small[:, :LANES], small[:, LANES:]], axis=0)
        w1_grad, b1_grad, w2_grad = small[hidden : hidden + 5], small[hidden + 5], small[:hidden]
        glu_gain_grad = small[hidden + 8 : hidden + 8 + model // LANES].reshape(model)
        pair = pair[:, : 3 * chans_padded].reshape(devices, 3, chans_padded, 2 * LANES)[:, :, :chans]
        pair = pair.transpose(1, 0, 2, 3).reshape(3, model, 2 * LANES)
        in_proj_grad = pair[:, :, :width].transpose(2, 0, 1)
        short_taps_grad = pair[:, :, width : width + 3].transpose(2, 0, 1)
        products = in_proj_grad * in_proj.astype(F32)
        products = jnp.sum(products.reshape(width, 3, blocks, width), axis=(1, 3))
        mixer_gain_grad = products.T.reshape(model) / mixer_gain
        input_grad = jnp.where(
            tp_index == 0,
            jnp.concatenate([input_half, input_other], axis=0),
            jnp.concatenate([input_other, input_half], axis=0),
        )

    mine = g3[:chans] + g3_back[chans_padded : chans_padded + chans]
    theirs = g3[chans_padded : chans_padded + chans] + g3_back[:chans]
    g3_full = jnp.where(
        tp_index == 0, jnp.concatenate([mine, theirs], axis=0), jnp.concatenate([theirs, mine], axis=0)
    ).T
    return (
        layer_output,
        input_grad,
        mixer_gain_grad,
        in_proj_grad,
        short_taps_grad,
        w1_grad,
        b1_grad,
        w2_grad,
        g3_full,
        out_proj_grad,
        glu_gain_grad,
        glu_in_grad,
        glu_out_grad,
    )


def solution(mesh):
    placed = (
        P("seq", None),
        P(),
        P(),
        P(),
        P(),
        P(),
        P(),
        P(None, "seq"),
        P("seq"),
        P(),
        P(),
        P(None, None, None, "tp"),
        P("tp", None),
        P(("seq", "tp"), None),
    )
    return jax.shard_map(
        local,
        mesh=mesh,
        in_specs=placed,
        out_specs=(
            P(("seq", "tp"), None),
            P("seq", None),
            P(),
            P(),
            P(),
            P(),
            P(),
            P(),
            P(None, "seq"),
            P(),
            P(),
            P(None, None, None, "tp"),
            P("tp", None),
        ),
        check_vma=False,
    )
```

```python
import math
import functools

import jax
import jax.numpy as jnp
import ml_dtypes
import numpy as np
from jax import lax
from jax.experimental import pallas as pl
from jax.experimental.pallas import tpu as pltpu
from jax.sharding import PartitionSpec as P

MIN_LEN = 8192
SLOW_PATH = False
EPSILON = 1e-05
LANES = 128
GROUP = 8
FILTER_LANES = 2048
SMALL_ROWS = 72
BF = jnp.bfloat16
F32 = jnp.float32

PI_HIGH = 3.140625
ROUNDER = 12582912.0
PI_LOW = 9.67653589793e-4
SIN_C = (1.0, -0.16666647791862488, 0.00833289884030819, -0.0001980081869987771, 2.590327312645968e-06)
COS_C = (0.9999999403953552, -0.4999990463256836, 0.041663575917482376, -0.0013853635173290968, 2.315232813998591e-05)


def vmem_specs(count):
    return [pl.BlockSpec(memory_space=pltpu.VMEM)] * count


def params(mib=60):
    return pltpu.CompilerParams(vmem_limit_bytes=mib * 1024 * 1024)


def cost(flops, bytes_accessed=0, transcendentals=0):
    return pl.CostEstimate(flops=flops // 20, bytes_accessed=bytes_accessed // 20, transcendentals=0)


def split_np(table):
    high = np.asarray(table, np.float32).astype(ml_dtypes.bfloat16)
    low = (np.asarray(table, np.float64) - high.astype(np.float64)).astype(ml_dtypes.bfloat16)
    return high, low


def split3_np(table):
    table = np.asarray(table, np.float64)
    high = table.astype(np.float32).astype(ml_dtypes.bfloat16)
    rest = table - high.astype(np.float64)
    mid = rest.astype(np.float32).astype(ml_dtypes.bfloat16)
    low = (rest - mid.astype(np.float64)).astype(np.float32).astype(ml_dtypes.bfloat16)
    return high, mid, low


@functools.lru_cache(maxsize=None)
def transform_tables(seq_length):
    period = 2 * seq_length
    first = period // LANES
    kept = first // 2 + 1
    padded = -(-kept // 8) * 8
    k = np.arange(padded)
    live = (k < kept).astype(np.float64)
    n = np.arange(first)
    angle = 2 * np.pi / first * ((k[:, None] * n[None, :]) % first)
    eye = np.eye(GROUP)
    stage = np.zeros((GROUP, 2, padded, first, GROUP))
    stage[:, 0] = np.einsum("kn,cd->cknd", np.cos(angle) * live[:, None], eye)
    stage[:, 1] = np.einsum("kn,cd->cknd", -np.sin(angle) * live[:, None], eye)
    forward = stage.reshape(GROUP * 2 * padded, first * GROUP)
    backward = forward.T
    m = np.arange(LANES)
    turn = 2 * np.pi / period * ((k[:, None] * m[None, :]) % period)
    weight = np.where((k == 0) | (k == first // 2), 1.0, 2.0) * live / period
    twiddle = np.stack(
        [np.cos(turn), np.sin(turn), np.cos(turn) * weight[:, None], np.sin(turn) * weight[:, None]]
    ).astype(np.float32)
    inner = 2 * np.pi / LANES * ((m[:, None] * m[None, :]) % LANES)
    c, s = np.cos(inner), np.sin(inner)
    second = np.block([[c, -s], [s, c]])
    return {
        "forward": split_np(forward),
        "backward": split_np(backward),
        "forward_used": split_np(forward[:, : first // 2 * GROUP]),
        "backward_used": split_np(backward[: first // 2 * GROUP]),
        "twiddle": twiddle,
        "second": split_np(second),
        "inverse": split_np(second.T),
        "first": first,
        "padded": padded,
    }


@functools.lru_cache(maxsize=None)
def feature_table(seq_length):
    period = 2 * seq_length
    index = np.arange(period)
    lag = np.where(index < seq_length, index, index - period)
    q = lag / seq_length
    rows = [q, np.cos(2 * np.pi * q), np.cos(4 * np.pi * q), np.sin(2 * np.pi * q), np.sin(4 * np.pi * q)]
    rows.append(np.ones_like(q))
    rows += [np.zeros_like(q)] * 2
    high, mid, low = split3_np(np.stack(rows))
    return np.concatenate([high, high, mid, high, mid, low], axis=0)


def split(values):
    high = values.astype(BF)
    low = (values - high.astype(F32)).astype(BF)
    return high, low


def first_weights(w1_ref, b1_ref):
    hidden = w1_ref.shape[1]
    rows = jnp.concatenate([w1_ref[...], b1_ref[...].reshape(1, hidden), jnp.zeros((2, hidden), F32)], axis=0)
    high = rows.astype(BF).astype(F32)
    mid = (rows - high).astype(BF).astype(F32)
    low = rows - high - mid
    return jnp.concatenate([high, mid, high, low, mid, high], axis=0).astype(BF)


def mm(a, b):
    return jnp.dot(a, b, preferred_element_type=F32)


def mm_nt(a, b):
    return lax.dot_general(a, b, (((1,), (1,)), ((), ())), preferred_element_type=F32)


def mm_tn(a, b):
    return lax.dot_general(a, b, (((0,), (0,)), ((), ())), preferred_element_type=F32)


def mm3(a, b):
    ah, al = a
    bh, bl = b
    return mm(ah, bh) + (mm(al, bh) + mm(ah, bl))


def mm3_tn(a, b):
    ah, al = a
    bh, bl = b
    return mm_tn(ah, bh) + (mm_tn(al, bh) + mm_tn(ah, bl))


def sine_cosine(x):
    n = (x * (0.5 / math.pi) + ROUNDER) - ROUNDER
    t = (x * 0.5 - n * PI_HIGH) - n * PI_LOW
    t2 = t * t
    s = SIN_C[4]
    for c in SIN_C[3::-1]:
        s = s * t2 + c
    s = s * t
    k = COS_C[4]
    for c in COS_C[3::-1]:
        k = k * t2 + c
    twice = s + s
    return twice * k, 1.0 - twice * s


def lag_decay(decay, start, width, seq_length):
    lane = lax.broadcasted_iota(jnp.int32, decay.shape[:1] + (width,), 1) + start
    lag = jnp.where(lane < seq_length, lane, 2 * seq_length - lane).astype(F32)
    return jnp.exp(lag * (decay[:, :1] * (-1.0 / seq_length)))


def stacked_weights(w):
    high, low = split(w)
    zero = jnp.zeros_like(high)
    return jnp.concatenate(
        [jnp.concatenate([high, high], axis=1), jnp.concatenate([low, zero], axis=1)], axis=0
    )


def stacked_product(weights, values):
    out = mm(weights, jnp.concatenate(split(values), axis=0))
    rows = out.shape[0] // 2
    return out[:rows] + out[rows:]


def decay_columns(ref):
    row = jnp.broadcast_to(ref[...].reshape(1, -1), (LANES, ref.shape[0]))
    rows = row.T
    half = ref.shape[0] // 2
    a, b = rows[:half], rows[half:]
    first = lax.axis_index("tp") == 0
    return jnp.concatenate([jnp.where(first, a, b), jnp.where(first, b, a)], axis=0)


def own_first(ref):
    half = ref.shape[0] // 2
    me = lax.axis_index("tp")
    return jnp.concatenate([ref[pl.ds(me * half, half), :], ref[pl.ds((1 - me) * half, half), :]], axis=0)


def filter_forward_kernel(feat_ref, w1_ref, b1_ref, w2_ref, w3_ref, decay_ref, own_ref, other_ref, a_ref, ac_ref, b_ref, bc_ref):
    length = own_ref.shape[1]
    channels = own_ref.shape[0]
    width = min(FILTER_LANES, length)
    begin = lax.axis_index("tp") * length
    w1 = first_weights(w1_ref, b1_ref)
    w2 = stacked_weights(w2_ref[...].T)
    w3 = stacked_weights(own_first(w3_ref))
    decay = decay_columns(decay_ref)
    for lo in range(0, length, width):
        lanes = slice(lo, lo + width)
        start = pl.multiple_of(begin + lo, LANES)
        s1, c1 = sine_cosine(mm_tn(w1, feat_ref[:, pl.ds(start, width)]))
        a_ref[:, lanes] = s1.astype(BF)
        ac_ref[:, lanes] = c1.astype(BF)
        s2, c2 = sine_cosine(stacked_product(w2, s1))
        b_ref[:, lanes] = s2.astype(BF)
        bc_ref[:, lanes] = c2.astype(BF)
        lag = stacked_product(w3, s2) * lag_decay(decay, start, width, length)
        own_ref[:, lanes] = lag[:channels]
        other_ref[:, lanes] = lag[channels:]


def filter_forward(features, w1, b1, w2, w3t, decay):
    hidden = w2.shape[0]
    channels = w3t.shape[0] // 2
    length = features.shape[1] // 2
    return pl.pallas_call(
        filter_forward_kernel,
        in_specs=vmem_specs(6),
        out_specs=vmem_specs(6),
        out_shape=[jax.ShapeDtypeStruct((channels, length), F32)] * 2
        + [jax.ShapeDtypeStruct((hidden, length), BF)] * 4,
        compiler_params=params(),
        cost_estimate=cost(8 * 10**9, 8 * 10**6),
        name="filter_forward",
    )(features, w1, b1, w2, w3t, decay)


def inner_spectrum(a, twiddle_ref, second, padded, columns):
    tc, ts = twiddle_ref[0], twiddle_ref[1]
    parts = []
    for col in range(columns):
        lanes = slice(col * LANES, (col + 1) * LANES)
        for c in range(GROUP):
            base = c * 2 * padded
            re = a[base : base + padded, lanes]
            im = a[base + padded : base + 2 * padded, lanes]
            parts.append(jnp.concatenate([re * tc + im * ts, im * tc - re * ts], axis=1))
    return mm3(split(jnp.concatenate(parts, axis=0)), second)


def signal_of(spec, inverse, twiddle_ref, back, padded, columns):
    b = mm3(split(spec), inverse)
    tc, ts = twiddle_ref[2], twiddle_ref[3]
    cols = []
    for col in range(columns):
        parts = []
        for c in range(GROUP):
            base = (col * GROUP + c) * padded
            re = b[base : base + padded, :LANES]
            im = b[base : base + padded, LANES:]
            parts.append(re * tc - im * ts)
            parts.append(im * tc + re * ts)
        cols.append(jnp.concatenate(parts, axis=0))
    z = split(jnp.concatenate(cols, axis=1))
    return [mm3(rows, z) for rows in back]


def gathered(x, seqs, rows, groups):
    cols = []
    for q in range(seqs):
        for g in range(groups):
            block = x[q * rows : (q + 1) * rows, g * GROUP : (g + 1) * GROUP, :]
            cols.append(block.reshape(rows * GROUP, LANES))
    return jnp.concatenate(cols, axis=1)


def scattered(y, seqs, rows, groups):
    out = []
    for q in range(seqs):
        cols = [
            y[:, (q * groups + g) * LANES : (q * groups + g + 1) * LANES].reshape(rows, GROUP, LANES)
            for g in range(groups)
        ]
        out.append(jnp.concatenate(cols, axis=1))
    return jnp.concatenate(out, axis=0)


def product(a, b, conjugate):
    ar, ai = a[:, :LANES], a[:, LANES:]
    br, bi = b[:, :LANES], b[:, LANES:]
    if conjugate:
        return jnp.concatenate([ar * br + ai * bi, ai * br - ar * bi], axis=1)
    return jnp.concatenate([ar * br - ai * bi, ar * bi + ai * br], axis=1)


def filter_spectrum_kernel(padded, own_ref, other_ref, fh, fl, tw, sh, sl, out_ref):
    groups = own_ref.shape[0] // GROUP
    rows = own_ref.shape[1] // LANES
    used = rows * GROUP
    me = lax.axis_index("tp")
    total = None
    for lag_ref, half in ((own_ref, me), (other_ref, 1 - me)):
        cols = []
        for g in range(groups):
            tiles = [lag_ref[g * GROUP : (g + 1) * GROUP, n * LANES : (n + 1) * LANES] for n in range(rows)]
            cols.append(jnp.concatenate(tiles, axis=0))
        begin = pl.multiple_of(half * used, LANES)
        table = (fh[:, pl.ds(begin, used)], fl[:, pl.ds(begin, used)])
        part = mm3(table, split(jnp.concatenate(cols, axis=1)))
        total = part if total is None else total + part
    out_ref[...] = inner_spectrum(total, tw, (sh[...], sl[...]), padded, groups)


def signal_spectrum(x, seqs, fh, fl, tw, sh, sl, padded):
    rows = x.shape[0] // seqs
    groups = x.shape[1] // GROUP
    used = rows * GROUP
    flat = gathered(x, seqs, rows, groups).astype(BF)
    a = mm(fh[:, :used], flat) + mm(fl[:, :used], flat)
    return inner_spectrum(a, tw, (sh[...], sl[...]), padded, seqs * groups)


def filtered(spec, h_ref, seqs, conjugate, tw, ih, il, bh, bl, padded, shape):
    rows = shape[0] // seqs
    groups = shape[1] // GROUP
    used = rows * GROUP
    prod = product(spec, jnp.concatenate([h_ref[...]] * seqs, axis=0), conjugate)
    (y,) = signal_of(prod, (ih[...], il[...]), tw, [(bh[:used, :], bl[:used, :])], padded, seqs * groups)
    return scattered(y, seqs, rows, groups)


def conv_forward_kernel(padded, seqs, x_ref, h_ref, fh, fl, tw, sh, sl, ih, il, bh, bl, y_ref, spec_ref):
    x = x_ref[...].astype(F32)
    spec = signal_spectrum(x, seqs, fh, fl, tw, sh, sl, padded)
    spec_ref[...] = spec
    y_ref[...] = filtered(spec, h_ref, seqs, False, tw, ih, il, bh, bl, padded, x.shape).astype(BF)


def conv_backward_kernel(padded, seqs, real, g_ref, sm_ref, p_ref, y_ref, saved_ref, taps_ref, h_ref, fh, fl, tw, sh, sl, ih, il, bh, bl,
                         pg_ref, cross_ref, st_ref, icg_ref):
    count, chans, _ = g_ref.shape
    gated = g_ref[...].astype(F32)
    conv_grad = gated * sm_ref[:, 2 * chans :, :]
    spec = signal_spectrum(conv_grad, seqs, fh, fl, tw, sh, sl, padded)
    cross = product(spec, saved_ref[...], True)
    height = cross_ref.shape[0]
    cross_ref[...] = sum(cross[q * height : (q + 1) * height] for q in range(seqs))
    icg = filtered(spec, h_ref, seqs, True, tw, ih, il, bh, bl, padded, g_ref.shape)
    icg_ref[...] = icg.astype(BF).astype(F32)
    per_seq = count // seqs
    taps = tap_columns(taps_ref, real)
    lane = lax.broadcasted_iota(jnp.int32, (3 * chans, LANES), 1)

    def step(i, carry):
        next1, next2, acc0, acc1, acc2 = carry
        n = count - 1 - i
        keep = jnp.where(lax.rem(n + 1, per_seq) == 0, 0.0, 1.0)
        sm = sm_ref[n]
        back = icg_ref[n]
        sg = jnp.concatenate(
            [back * sm[chans : 2 * chans], back * sm[:chans], g_ref[n].astype(F32) * y_ref[n].astype(F32)], axis=0
        )
        r1 = pltpu.roll(sg, LANES - 1, 1)
        r2 = pltpu.roll(sg, LANES - 2, 1)
        s1 = jnp.where(lane < LANES - 1, r1, next1 * keep)
        s2 = jnp.where(lane < LANES - 2, r2, next2 * keep)
        pg_ref[n] = (taps[0] * sg + taps[1] * s1 + taps[2] * s2).astype(BF)
        p = p_ref[n]
        return r1, r2, acc0 + sg * p, acc1 + s1 * p, acc2 + s2 * p

    zero = jnp.zeros((3 * chans, LANES), F32)
    _, _, acc0, acc1, acc2 = lax.fori_loop(0, count, step, (zero,) * 5, unroll=4)
    out = zero
    for k, acc in enumerate((acc0, acc1, acc2)):
        out = jnp.where(lane == k, jnp.sum(acc, axis=1, keepdims=True), out)
    st_ref[...] = out


def filter_spectrum(own, other, tables):
    padded = tables["padded"]
    return pl.pallas_call(
        functools.partial(filter_spectrum_kernel, padded),
        in_specs=vmem_specs(7),
        out_specs=vmem_specs(1)[0],
        out_shape=jax.ShapeDtypeStruct((own.shape[0] * padded, 2 * LANES), F32),
        compiler_params=params(),
        cost_estimate=cost(4 * 10**9, 4 * 10**6),
        name="filter_spectrum",
    )(own, other, *tables["forward"], tables["twiddle"], *tables["second"])


def transforms(tables):
    return (*tables["forward_used"], tables["twiddle"], *tables["second"], *tables["inverse"], *tables["backward_used"])


def conv_forward(x, spectrum, tables, seqs):
    padded = tables["padded"]
    return pl.pallas_call(
        functools.partial(conv_forward_kernel, padded, seqs),
        in_specs=vmem_specs(11),
        out_specs=vmem_specs(2),
        out_shape=[
            jax.ShapeDtypeStruct(x.shape, BF),
            jax.ShapeDtypeStruct((seqs * x.shape[1] * padded, 2 * LANES), F32),
        ],
        compiler_params=params(),
        cost_estimate=cost(5 * 10**9, 6 * 10**6),
        name="conv_forward",
    )(x, spectrum, *transforms(tables))


def conv_backward(gated, mixed, proj, conv_out, saved, taps, spectrum, tables, seqs, real):
    padded = tables["padded"]
    count, chans, _ = gated.shape
    return pl.pallas_call(
        functools.partial(conv_backward_kernel, padded, seqs, real),
        in_specs=vmem_specs(16),
        out_specs=vmem_specs(3),
        out_shape=[
            jax.ShapeDtypeStruct((count, 3 * chans, LANES), BF),
            jax.ShapeDtypeStruct((chans * padded, 2 * LANES), F32),
            jax.ShapeDtypeStruct((3 * chans, LANES), F32),
        ],
        scratch_shapes=[pltpu.VMEM(gated.shape, F32)],
        compiler_params=params(),
        cost_estimate=cost(7 * 10**9, 9 * 10**6),
        name="conv_backward",
    )(gated, mixed, proj, conv_out, saved, taps, spectrum, *transforms(tables))


def source_of(place, turn, group):
    per_plane, relative = place
    seq = lax.axis_index("seq")
    plane = lax.div(seq, per_plane)
    inside = lax.rem(seq, per_plane)
    half, index = turn
    inner = lax.bitwise_xor(inside, index) if relative else index
    return (lax.bitwise_xor(plane, group) * per_plane + inner) * 2 + lax.bitwise_xor(lax.axis_index("tp"), half)


def own_channels(ref, index, chans):
    model = ref.shape[-1]
    linear = lax.axis_index("seq") * 2 + lax.axis_index("tp")
    first = linear * chans
    window = jnp.minimum(lax.div(first, LANES) * LANES, model - 2 * LANES)
    part = ref[index, :, pl.ds(pl.multiple_of(window, LANES), 2 * LANES)].astype(F32)
    part = pltpu.roll(part, lax.rem(2 * LANES - (first - window), 2 * LANES), 1)
    turned = part[:, :LANES].T
    return turned[: -(-chans // GROUP) * GROUP]


def tap_columns(taps_ref, chans):
    out = []
    for k in range(3):
        cols = own_channels(taps_ref, k, chans)
        out.append(jnp.concatenate([jnp.broadcast_to(cols[:, p : p + 1], (cols.shape[0], LANES)) for p in range(3)], axis=0))
    return out


def channel_mixer_kernel(place, turns, seqs, chans, w_ref, taps_ref, *refs):
    tiles, (p_ref, sm_ref) = refs[:-2], refs[-2:]
    count, rows3, _ = p_ref.shape
    wc = jnp.concatenate([own_channels(w_ref, p, chans) for p in range(3)], axis=0).astype(BF)
    for ref, turn_list in zip(tiles, turns):
        for q, turn in enumerate(turn_list):
            x = jnp.concatenate([ref[4 * q + z] for z in range(4)], axis=1)
            p = mm(wc, x).astype(BF).astype(F32)
            for z in range(4):
                p_ref[source_of(place, turn, z)] = p[:, z * LANES : (z + 1) * LANES]
    per_seq = count // seqs
    taps = tap_columns(taps_ref, chans)
    lane = lax.broadcasted_iota(jnp.int32, (rows3, LANES), 1)

    def step(n, carry):
        last1, last2 = carry
        keep = jnp.where(lax.rem(n, per_seq) == 0, 0.0, 1.0)
        p = p_ref[n]
        r1 = pltpu.roll(p, 1, 1)
        r2 = pltpu.roll(p, 2, 1)
        s1 = jnp.where(lane < 1, last1 * keep, r1)
        s2 = jnp.where(lane < 2, last2 * keep, r2)
        sm_ref[n] = taps[0] * p + taps[1] * s1 + taps[2] * s2
        return r1, r2

    zero = jnp.zeros((rows3, LANES), F32)
    lax.fori_loop(0, count, step, (zero, zero), unroll=4)


def channel_mixer(tiles, turns, place, w, taps, count, seqs, chans):
    rows3 = 3 * (-(-chans // GROUP) * GROUP)
    return pl.pallas_call(
        functools.partial(channel_mixer_kernel, place, turns, seqs, chans),
        in_specs=vmem_specs(2 + len(tiles)),
        out_specs=vmem_specs(2),
        out_shape=[jax.ShapeDtypeStruct((count, rows3, LANES), F32)] * 2,
        compiler_params=params(),
        cost_estimate=cost(3 * 10**9, 6 * 10**6),
        name="channel_mixer",
    )(w, taps, *tiles)


def channel_grads_kernel(place, turns, padded, count, pg_ref, st_ref, own_ref, other_ref, tw, ih, il, bh, bl, feat_ref, w2_ref,
                         w3_ref, decay_ref, gain_ref, a_ref, ac_ref, b_ref, bc_ref, *refs):
    tiles, (out_ref, g3_ref, keep_ref, lag_ref) = refs[:count], refs[count:]
    total = None
    for ref, turn_list in zip(tiles, turns):
        for q, turn in enumerate(turn_list):
            x = jnp.concatenate([ref[4 * q + z] for z in range(4)], axis=1)
            g = jnp.concatenate([pg_ref[source_of(place, turn, z)] for z in range(4)], axis=1)
            part = mm_nt(g, x)
            total = part if total is None else total + part
    rows3, width = total.shape
    keep_ref[...] = jnp.zeros_like(keep_ref)
    keep_ref[:rows3, :width] = total
    keep_ref[:rows3, width : width + 3] = st_ref[:, :3]

    length = lag_ref.shape[1]
    rows = length // LANES
    used = rows * GROUP
    channels = lag_ref.shape[0] // 2
    groups = channels // GROUP
    begin = pl.multiple_of(lax.axis_index("tp") * used, LANES)
    back = (bh[pl.ds(begin, used), :], bl[pl.ds(begin, used), :])
    for half, ref in enumerate((own_ref, other_ref)):
        (y,) = signal_of(ref[...], (ih[...], il[...]), tw, [back], padded, groups)
        for g in range(groups):
            base = half * channels + g * GROUP
            for n in range(rows):
                lag_ref[base : base + GROUP, n * LANES : (n + 1) * LANES] = y[
                    n * GROUP : (n + 1) * GROUP, g * LANES : (g + 1) * LANES
                ]

    span = min(FILTER_LANES, length)
    begin = lax.axis_index("tp") * length
    w2 = stacked_weights(w2_ref[...])
    w3 = split(own_first(w3_ref))
    decay = decay_columns(decay_ref)
    g1 = g2 = g3 = 0.0
    for lo in range(0, length, span):
        lanes = slice(lo, lo + span)
        start = pl.multiple_of(begin + lo, LANES)
        wh, wl = split(lag_ref[:, lanes] * lag_decay(decay, start, span, length))
        second = b_ref[:, lanes]
        g3 += mm_nt(wh, second) + mm_nt(wl, second)
        pre2 = mm3_tn(w3, (wh, wl)) * bc_ref[:, lanes].astype(F32)
        g2 += mm_nt(a_ref[:, lanes], pre2.astype(BF))
        pre1 = stacked_product(w2, pre2) * ac_ref[:, lanes].astype(F32)
        g1 += mm_nt(feat_ref[:8, pl.ds(start, span)], pre1.astype(BF))
    g3_ref[...] = g3
    more = out_ref.shape[0] - rows3
    gains = [gain_ref[k * LANES : (k + 1) * LANES].reshape(1, LANES) for k in range(gain_ref.shape[0] // LANES)]
    gains += [jnp.zeros((8 - len(gains), LANES), F32)]
    keep_ref[rows3:, :LANES] = g2[:more]
    keep_ref[rows3:, LANES:] = jnp.concatenate([g2[more:], g1] + gains, axis=0)
    out_ref[...] = keep_ref[...].astype(BF)


def channel_grads(tiles, turns, place, pg, st, own, other, tables, features, w2, w3t, decay, gain, saved):
    rows3 = pg.shape[1]
    hidden = w2.shape[0]
    length = features.shape[1] // 2
    return pl.pallas_call(
        functools.partial(channel_grads_kernel, place, turns, tables["padded"], len(tiles)),
        in_specs=vmem_specs(18 + len(tiles)),
        out_specs=vmem_specs(2),
        out_shape=[
            jax.ShapeDtypeStruct((rows3 + SMALL_ROWS, 2 * LANES), BF),
            jax.ShapeDtypeStruct((w3t.shape[0], hidden), F32),
        ],
        scratch_shapes=[
            pltpu.VMEM((rows3 + SMALL_ROWS, 2 * LANES), F32),
            pltpu.VMEM((w3t.shape[0], length), F32),
        ],
        compiler_params=params(),
        cost_estimate=cost(8 * 10**9, 8 * 10**6),
        name="channel_grads",
    )(pg, st, own, other, tables["twiddle"], *tables["inverse"], *tables["backward"], features, w2, w3t, decay, gain,
      *saved, *tiles)


def erf_parts(g):
    x = jnp.abs(g) * (1.0 / math.sqrt(2.0))
    t = 1.0 / (1.0 + 0.3275911 * x)
    e = jnp.exp(-x * x)
    poly = t * (0.254829592 + t * (-0.284496736 + t * (1.421413741 + t * (-1.453152027 + t * 1.061405429))))
    tail = 0.5 * poly * e
    return jnp.where(g < 0, tail, 1.0 - tail), e


def norm_stats(v):
    centered = v - jnp.mean(v, axis=-1, keepdims=True)
    variance = jnp.mean(centered * centered, axis=-1, keepdims=True)
    r = lax.rsqrt(variance + EPSILON)
    return centered * r, r


def norm_backward(w, gain, xhat, r):
    a = w * gain
    return r * (a - jnp.mean(a, axis=-1, keepdims=True) - xhat * jnp.mean(a * xhat, axis=-1, keepdims=True))


def column(j, width):
    return slice(j * width, (j + 1) * width)


def own_part(ref, rows):
    return ref[pl.ds(pl.multiple_of(lax.axis_index("tp") * rows, rows), rows), :]


def mixer_in_kernel(per_plane, seq_length, x_ref, halo_ref, gain_ref, w_ref, taps_ref, og_ref, conv_ref, sm2_ref, z0, z1, z2, z3, keep_ref):
    rows = sm2_ref.shape[0]
    width = w_ref.shape[1]
    blocks = w_ref.shape[2] // width
    lead = halo_ref.shape[0]
    linear = lax.axis_index("seq") * 2 + lax.axis_index("tp")
    keep = jnp.where(lax.rem(linear * rows, seq_length) == 0, 0.0, 1.0)
    inner = x_ref[rows - lead : rows, :].astype(F32)
    halo = jnp.where(lax.axis_index("tp") == 0, halo_ref[...].astype(F32), inner) * keep
    x = jnp.concatenate([halo, own_part(x_ref, rows).astype(F32)], axis=0)
    xhat, _ = norm_stats(x)
    normed = xhat * gain_ref[...].reshape(1, -1)
    n1 = normed.astype(BF)
    mixed = []
    for p in range(3):
        proj = jnp.concatenate(
            [mm(n1[:, column(j, width)], w_ref[p, :, column(j, width)]) for j in range(blocks)], axis=1
        )
        proj = proj.astype(BF).astype(F32)
        mixed.append(
            taps_ref[0, p : p + 1, :] * proj[lead:]
            + taps_ref[1, p : p + 1, :] * proj[lead - 1 : lead - 1 + rows]
            + taps_ref[2, p : p + 1, :] * proj[lead - 2 : lead - 2 + rows]
        )
    sm2_ref[...] = mixed[2]
    conv_ref[...] = (mixed[0] * mixed[1]).T.astype(BF)
    nt = normed[lead:].T.astype(BF)
    ot = og_ref[...].astype(F32).T.astype(BF)
    for j in range(blocks):
        keep_ref[j, :width, :] = nt[column(j, width)]
        keep_ref[j, width:, :] = ot[column(j, width)]
    plane = lax.div(lax.axis_index("seq"), per_plane)
    for d, out in enumerate((z0, z1, z2, z3)):
        out[...] = keep_ref[lax.bitwise_xor(plane, d)]


def mixer_in(x, halo, gain, w, taps, og, per_plane, seq_length):
    rows, model = og.shape
    width = w.shape[1]
    return pl.pallas_call(
        functools.partial(mixer_in_kernel, per_plane, seq_length),
        in_specs=vmem_specs(6),
        out_specs=vmem_specs(6),
        out_shape=[jax.ShapeDtypeStruct((model, rows), BF), jax.ShapeDtypeStruct((rows, model), F32)]
        + [jax.ShapeDtypeStruct((2 * width, rows), BF)] * 4,
        scratch_shapes=[pltpu.VMEM((model // width, 2 * width, rows), BF)],
        compiler_params=params(24),
        cost_estimate=cost(4 * 10**9, 4 * 10**6),
        name="mixer_in",
    )(x, halo, gain, w, taps, og)


def glu_block(x, og, w_pairs, d_pairs):
    down = None
    back = None
    for (wg, wu), wd in zip(w_pairs, d_pairs):
        gate = mm(x, wg)
        up = mm(x, wu)
        phi, e = erf_parts(gate)
        act = gate * phi
        hidden = (act * up).astype(BF)
        hg = mm_nt(og, wd)
        slope = phi + gate * (e * (1.0 / math.sqrt(2.0 * math.pi)))
        gg = (hg * up * slope).astype(BF)
        ug = (hg * act).astype(BF)
        down_part = mm(hidden, wd)
        back_part = mm_nt(gg, wg) + mm_nt(ug, wu)
        down = down_part if down is None else down + down_part
        back = back_part if back is None else back + back_part
    return down, back


def middle_kernel(per_plane, conv_ref, sm2_ref, x_ref, og_ref, gain_ref, wo_ref, ga_ref, gb_ref, da_ref, db_ref,
                  gg_ref, mid_ref, out_ref, wo_own, wo_other, gain_out, z0, z1, z2, z3, keep_ref):
    width = wo_ref.shape[0]
    blocks = wo_ref.shape[1] // width
    conv = conv_ref[...].astype(F32).T
    gated = sm2_ref[...] * conv
    gated_low = gated.astype(BF)
    branch = jnp.concatenate(
        [mm(gated_low[:, column(j, width)], wo_ref[:, column(j, width)]) for j in range(blocks)], axis=1
    )
    middle = own_part(x_ref, conv.shape[0]).astype(F32) + branch
    gain = gain_ref[...].reshape(1, -1)
    xhat, r = norm_stats(middle)
    normed = xhat * gain
    n2 = normed.astype(BF)
    og = og_ref[...]
    downs, backs = [], []
    for j in range(blocks):
        down, back = glu_block(
            n2[:, column(j, width)],
            og[:, column(j, width)],
            [(ga_ref[j, 0], ga_ref[j, 1]), (gb_ref[j, 0], gb_ref[j, 1])],
            [da_ref[:, column(j, width)], db_ref[:, column(j, width)]],
        )
        downs.append(down)
        backs.append(back)
    out_ref[...] = (middle + jnp.concatenate(downs, axis=1)).astype(BF)
    n2_grad = jnp.concatenate(backs, axis=1)
    mid_grad = og.astype(F32) + norm_backward(n2_grad, gain, xhat, r)
    mid_ref[...] = mid_grad
    bg = mid_grad.astype(BF)
    gated_grad = jnp.concatenate(
        [mm_nt(bg[:, column(j, width)], wo_ref[:, column(j, width)]) for j in range(blocks)], axis=1
    )
    gg_ref[...] = gated_grad.T.astype(BF)
    gain_out[...] = jnp.sum(n2_grad * xhat, axis=0, keepdims=True).reshape(-1)
    weight = jnp.concatenate(
        [mm_tn(gated_low[:, column(j, width)], bg[:, column(j, width)]) for j in range(blocks)], axis=1
    )
    lanes = wo_own.shape[1]
    first = lax.axis_index("tp") == 0
    wo_own[...] = jnp.where(first, weight[:, :lanes], weight[:, lanes:]).astype(BF)
    wo_other[...] = jnp.where(first, weight[:, lanes:], weight[:, :lanes]).astype(BF)
    turned = normed.T.astype(BF)
    for j in range(blocks):
        keep_ref[j] = turned[column(j, width)]
    plane = lax.div(lax.axis_index("seq"), per_plane)
    for d, out in enumerate((z0, z1, z2, z3)):
        out[...] = keep_ref[lax.bitwise_xor(plane, d)]


def middle_part(conv, sm2, x, og, gain, wo, ga, gb, da, db, per_plane):
    rows, model = og.shape
    width = wo.shape[0]
    return pl.pallas_call(
        functools.partial(middle_kernel, per_plane),
        in_specs=vmem_specs(10),
        out_specs=vmem_specs(10),
        out_shape=[
            jax.ShapeDtypeStruct((model, rows), BF),
            jax.ShapeDtypeStruct((rows, model), F32),
            jax.ShapeDtypeStruct((rows, model), BF),
            jax.ShapeDtypeStruct((width, model // 2), BF),
            jax.ShapeDtypeStruct((width, model // 2), BF),
            jax.ShapeDtypeStruct((model,), F32),
        ]
        + [jax.ShapeDtypeStruct((width, rows), BF)] * 4,
        scratch_shapes=[pltpu.VMEM((model // width, width, rows), BF)],
        compiler_params=params(),
        cost_estimate=cost(9 * 10**9, 6 * 10**6),
        name="middle_part",
    )(conv, sm2, x, og, gain, wo, ga, gb, da, db)


def glu_grad_kernel(per_plane, za, zb, zc, zd, oa, ob, oc, od, ga_ref, gb_ref, da_ref, db_ref, own_ref, other_ref):
    j = lax.div(lax.axis_index("seq"), per_plane)
    width = ga_ref.shape[2]
    xt = jnp.concatenate([ref[...] for ref in (za, zb, zc, zd)], axis=1)
    ot = jnp.concatenate([ref[width:, :] for ref in (oa, ob, oc, od)], axis=1)
    x = xt.astype(F32).T.astype(BF)
    og = ot.astype(F32).T.astype(BF)
    for g_ref, d_ref, out_ref in ((gb_ref, db_ref, other_ref), (ga_ref, da_ref, own_ref)):
        wg, wu = g_ref[j, 0], g_ref[j, 1]
        wd = d_ref[:, :width]
        for k in range(1, d_ref.shape[1] // width):
            wd = jnp.where(j == k, d_ref[:, column(k, width)], wd)
        gate = mm(x, wg)
        up = mm(x, wu)
        phi, e = erf_parts(gate)
        act = gate * phi
        hidden = (act * up).astype(BF)
        hg = mm_nt(og, wd)
        slope = phi + gate * (e * (1.0 / math.sqrt(2.0 * math.pi)))
        out_ref[0:width, :] = mm(xt, (hg * up * slope).astype(BF)).astype(out_ref.dtype)
        out_ref[width : 2 * width, :] = mm(xt, (hg * act).astype(BF)).astype(out_ref.dtype)
        out_ref[2 * width : 3 * width, :] = mm(ot, hidden).astype(out_ref.dtype)


def glu_grads(z_parts, o_parts, ga, gb, da, db, per_plane):
    width, half = ga.shape[2:]
    return pl.pallas_call(
        functools.partial(glu_grad_kernel, per_plane),
        in_specs=vmem_specs(12),
        out_specs=vmem_specs(2),
        out_shape=[
            jax.ShapeDtypeStruct((3 * width, half), F32),
            jax.ShapeDtypeStruct((3 * width, half), BF),
        ],
        compiler_params=params(40),
        cost_estimate=cost(9 * 10**9, 4 * 10**6),
        name="glu_grads",
    )(*z_parts, *o_parts, ga, gb, da, db)


def plane_add_kernel(own_ref, other_ref, mine_ref, theirs_ref, out_ref):
    total = (own_ref[...] + other_ref[...].astype(F32)).astype(BF)
    extra = (mine_ref[...].astype(F32) + theirs_ref[...].astype(F32)).astype(BF)
    count = out_ref.shape[0]
    rows, more = total.shape[0] // count, extra.shape[0] // count
    for k in range(count):
        out_ref[k, :rows, :] = total[k * rows : (k + 1) * rows]
        out_ref[k, rows:, :] = extra[k * more : (k + 1) * more]


def plane_add(own, other, mine, theirs, count):
    half = own.shape[1]
    rows = (own.shape[0] + mine.shape[0]) // count
    return pl.pallas_call(
        plane_add_kernel,
        in_specs=vmem_specs(4),
        out_specs=vmem_specs(1)[0],
        out_shape=jax.ShapeDtypeStruct((count, rows, half), BF),
        compiler_params=params(8),
        cost_estimate=cost(10**8, 2 * 10**6),
        name="plane_add",
    )(own, other, mine, theirs)


def plane_join_kernel(cut, a0, a1, a2, a3, out_ref):
    refs = (a0, a1, a2, a3)
    last = sum(ref[cut:, :].astype(F32) for ref in refs).astype(BF)
    if len(out_ref.shape) == 2:
        for z, ref in enumerate(refs):
            out_ref[z * cut : (z + 1) * cut, :] = ref[:cut, :]
        out_ref[4 * cut :, :] = last
        return
    for k in range(out_ref.shape[0]):
        for z, ref in enumerate(refs):
            out_ref[k, z * cut : (z + 1) * cut, :] = ref[:cut, :]
        out_ref[k, 4 * cut :, :] = last


def plane_join(parts, cut, copies=()):
    rows, half = parts[0].shape
    return pl.pallas_call(
        functools.partial(plane_join_kernel, cut),
        in_specs=vmem_specs(4),
        out_specs=vmem_specs(1)[0],
        out_shape=jax.ShapeDtypeStruct((*copies, 3 * cut + rows, half), BF),
        compiler_params=params(8),
        cost_estimate=cost(10**8, 2 * 10**6),
        name="plane_join",
    )(*parts)


def plane_sum_kernel(x_ref, out_ref):
    out_ref[...] = sum(x_ref[k].astype(F32) for k in range(x_ref.shape[0])).astype(BF)


def plane_sum(parts):
    return pl.pallas_call(
        plane_sum_kernel,
        in_specs=vmem_specs(1),
        out_specs=vmem_specs(1)[0],
        out_shape=jax.ShapeDtypeStruct(parts.shape[1:], BF),
        compiler_params=params(8),
        cost_estimate=cost(10**8, 2 * 10**6),
        name="plane_sum",
    )(parts)


def finish_kernel(per_plane, width, a_ref, half_ref, back_ref,
                  gi_ref, go_ref, in_ref, keep_ref):
    seq = lax.axis_index("seq")
    plane = lax.div(seq, per_plane)
    blocks, pieces, cut, half = keep_ref.shape
    for k in range(pieces):
        for z in range(blocks):
            keep_ref[lax.bitwise_xor(plane, z), k] = a_ref[k, z * cut : (z + 1) * cut, :].astype(F32)
    outs = []
    for j in range(blocks):
        block = jnp.concatenate([keep_ref[j, k] for k in range(pieces)], axis=0)
        gi_ref[j, :, 0, :] = block[:width]
        gi_ref[j, :, 1, :] = block[width : 2 * width]
        outs.append(block[2 * width : 3 * width].T)
    go_ref[...] = jnp.concatenate(outs, axis=1)
    count = half_ref.shape[0]
    me = lax.axis_index("tp")
    in_ref[pl.ds(pl.multiple_of(me * count, count), count), :] = half_ref[...]
    in_ref[pl.ds(pl.multiple_of((1 - me) * count, count), count), :] = back_ref[...]


def finish(sums, half_rows, other_rows, per_plane, width):
    half = sums.shape[2]
    model = 4 * width
    return pl.pallas_call(
        functools.partial(finish_kernel, per_plane, width),
        in_specs=vmem_specs(3),
        out_specs=vmem_specs(3),
        out_shape=[
            jax.ShapeDtypeStruct((4, width, 2, half), F32),
            jax.ShapeDtypeStruct((half, model), F32),
            jax.ShapeDtypeStruct((2 * half_rows.shape[0], model), BF),
        ],
        scratch_shapes=[pltpu.VMEM((4, 4, 3 * width // 4, half), F32)],
        compiler_params=params(32),
        cost_estimate=cost(10**8, 6 * 10**6),
        name="finish",
    )(sums, half_rows, other_rows)


def out_unpack_kernel(mine_ref, theirs_ref, wo_ref):
    first = lax.axis_index("tp") == 0
    mine, theirs = mine_ref[...].astype(F32), theirs_ref[...].astype(F32)
    left, right = jnp.where(first, mine, theirs), jnp.where(first, theirs, mine)
    _, cut, lanes = left.shape
    for k in range(left.shape[0]):
        wo_ref[k * cut : (k + 1) * cut, :lanes] = left[k]
        wo_ref[k * cut : (k + 1) * cut, lanes:] = right[k]


def out_unpack(mine, theirs):
    count, rows, lanes = mine.shape
    return pl.pallas_call(
        out_unpack_kernel,
        in_specs=vmem_specs(2),
        out_specs=vmem_specs(1)[0],
        out_shape=jax.ShapeDtypeStruct((count * rows, 2 * lanes), F32),
        compiler_params=params(8),
        cost_estimate=cost(10**8, 10**6),
        name="out_unpack",
    )(mine, theirs)


def in_unpack_kernel(place, w_ref, gain_ref, *refs):
    tiles, (gi_ref, st_ref, gain_out, w1_ref, b1_ref, w2_ref, gain2_ref, keep_ref) = refs[:-8], refs[-8:]
    _, width, model = gi_ref.shape
    count, rows3, _ = keep_ref.shape
    small = None
    for k, ref in enumerate(tiles):
        half, z = divmod(k, 4)
        for inner in range(4):
            keep_ref[source_of(place, (half, inner), z)] = ref[inner * rows3 : (inner + 1) * rows3, :].astype(F32)
        part = ref[4 * rows3 :, :].astype(F32)
        small = part if small is None else small + part
    hidden = w2_ref.shape[0]
    more = small.shape[0]
    w2_ref[:more, :] = small[:, :LANES]
    w2_ref[more:, :] = small[: hidden - more, LANES:]
    rest = small[hidden - more : hidden - more + 8, LANES:]
    w1_ref[...] = rest[:5]
    b1_ref[...] = rest[5:6].reshape(-1)
    rest = small[hidden - more + 8 :, LANES:]
    for k in range(model // LANES):
        gain2_ref[k * LANES : (k + 1) * LANES] = rest[k : k + 1].reshape(-1)
    chans = rows3 // 3
    blocks = model // width
    per_block = count // blocks
    gains = []
    for j in range(blocks):
        acc = None
        for p in range(3):
            got = jnp.concatenate(
                [keep_ref[j * per_block + k, p * chans : (p + 1) * chans, :] for k in range(per_block)], axis=0
            )
            turned = got.T
            gi_ref[p, :, column(j, width)] = turned[:width]
            for k in range(3):
                st_ref[k, p : p + 1, column(j, width)] = turned[width + k : width + k + 1]
            part = turned[:width] * w_ref[p, :, column(j, width)].astype(F32)
            acc = part if acc is None else acc + part
        gains.append(jnp.sum(acc.T, axis=0, keepdims=True))
    gain_out[...] = (jnp.concatenate(gains, axis=1) / gain_ref[...].reshape(1, -1)).reshape(-1)


def in_unpack(tiles, place, w, gain):
    rows3 = (tiles[0].shape[0] - SMALL_ROWS) // 4
    hidden = LANES
    count = 4 * len(tiles)
    _, width, model = w.shape
    return pl.pallas_call(
        functools.partial(in_unpack_kernel, place),
        in_specs=vmem_specs(2 + len(tiles)),
        out_specs=vmem_specs(7),
        out_shape=[
            jax.ShapeDtypeStruct((3, width, model), F32),
            jax.ShapeDtypeStruct((3, 3, model), F32),
            jax.ShapeDtypeStruct((model,), F32),
            jax.ShapeDtypeStruct((5, hidden), F32),
            jax.ShapeDtypeStruct((hidden,), F32),
            jax.ShapeDtypeStruct((hidden, hidden), F32),
            jax.ShapeDtypeStruct((model,), F32),
        ],
        scratch_shapes=[pltpu.VMEM((count, rows3, 2 * LANES), F32)],
        compiler_params=params(24),
        cost_estimate=cost(10**8, 4 * 10**6),
        name="in_unpack",
    )(w, gain, *tiles)


def mixer_back_kernel(by_source, pg_ref, mid_ref, x_ref, gain_ref, w_ref, in_ref):
    rows, model = mid_ref.shape
    width = w_ref.shape[1]
    blocks = model // width
    if by_source:
        pg = pg_ref[...].astype(F32)
        count, rows3, _ = pg.shape
        chans = rows3 // 3
        parts = [
            pg[:, p * chans : (p + 1) * chans, :].reshape(count * chans, rows).astype(BF) for p in range(3)
        ]
    else:
        parts = [pg_ref[p] for p in range(3)]
    grads = []
    for j in range(blocks):
        total = None
        for p in range(3):
            part = mm(w_ref[p, :, column(j, width)], parts[p][column(j, width)])
            total = part if total is None else total + part
        grads.append(total)
    n1_grad = jnp.concatenate(grads, axis=0).T
    xhat, r = norm_stats(own_part(x_ref, rows).astype(F32))
    in_ref[...] = (mid_ref[...] + norm_backward(n1_grad, gain_ref[...].reshape(1, -1), xhat, r)).astype(BF)


def mixer_back(pg, mid, x, gain, w, by_source):
    return pl.pallas_call(
        functools.partial(mixer_back_kernel, by_source),
        in_specs=vmem_specs(5),
        out_specs=vmem_specs(1)[0],
        out_shape=jax.ShapeDtypeStruct(mid.shape, BF),
        compiler_params=params(16),
        cost_estimate=cost(3 * 10**9, 4 * 10**6),
        name="mixer_back",
    )(pg, mid, x, gain, w)


def after(x, *others):
    return lax.optimization_barrier((x,) + others)[0]


def permuted(x, axes, count, by):
    pairs = [(i, i + by) for i in range(count) if 0 <= i + by < count]
    return lax.ppermute(x, axes, pairs)


def swapped(x):
    return lax.ppermute(x, "tp", [(0, 1), (1, 0)])


def crossed(x, mask):
    devices = lax.axis_size("seq")
    return lax.ppermute(x, "seq", [(i, i ^ mask) for i in range(devices)])


def exchanged(x, axes, groups=None):
    return lax.all_to_all(x, axes, 0, 0, axis_index_groups=groups, tiled=True)


def gathered_over(x, count, groups=None):
    return exchanged(jnp.broadcast_to(x[None], (count,) + x.shape), "seq", groups)


def local(
    layer_input,
    mixer_gain,
    in_proj,
    short_taps,
    filter_w1,
    filter_b1,
    filter_w2,
    filter_w3,
    filter_decay,
    out_proj,
    glu_gain,
    glu_in,
    glu_out,
    out_grad,
):
    tok_rows, model = layer_input.shape
    width = in_proj.shape[0]
    blocks = model // width
    half = glu_out.shape[0]
    seq_devices = lax.axis_size("seq")
    tp_devices = lax.axis_size("tp")
    devices = seq_devices * tp_devices
    both = ("seq", "tp")
    rows = tok_rows // tp_devices
    seq_length = min(MIN_LEN, tok_rows * seq_devices)
    seqs = tok_rows * seq_devices // seq_length
    per_plane = seq_devices // blocks
    quick = per_plane == 4 and not SLOW_PATH
    place = (per_plane, quick)
    chans = model // devices
    chans_padded = -(-chans // GROUP) * GROUP
    spare = chans_padded - chans
    hidden = filter_w2.shape[0]
    tp_index = lax.axis_index("tp")
    linear = lax.axis_index("seq") * tp_devices + tp_index
    tables = transform_tables(seq_length)
    features = feature_table(seq_length)
    within = [[g * per_plane + r for r in range(per_plane)] for g in range(blocks)]

    halo = permuted(layer_input[tok_rows - 16 :], "seq", seq_devices, 1)

    w3t = filter_w3.T.reshape(tp_devices, chans, hidden)
    w3t = jnp.pad(w3t, ((0, 0), (0, spare), (0, 0))).reshape(tp_devices * chans_padded, hidden)
    decay = jnp.pad(filter_decay.reshape(tp_devices, chans), ((0, 0), (0, spare))).reshape(-1)
    lag_own, lag_other, *saved = filter_forward(features, filter_w1, filter_b1, filter_w2, w3t, decay)
    lag_back = swapped(lag_other)

    w_in = in_proj.transpose(1, 0, 2)
    conv_rows, sm2, *sent = mixer_in(
        layer_input, after(halo, lag_own), mixer_gain, w_in, short_taps, out_grad, per_plane, seq_length
    )

    def to_channels(x):
        out = exchanged(x.reshape(devices, chans, rows), both)
        return jnp.pad(out, ((0, 0), (0, spare), (0, 0)))

    def to_tokens(x):
        return exchanged(x[:, :chans], both).reshape(model, rows)

    conv_channels = to_channels(conv_rows)
    early = [sent[0]] + [crossed(sent[d], d * per_plane) for d in range(1, blocks)]
    glu_own = after(glu_in, conv_rows).transpose(0, 2, 1, 3)
    down_own = after(glu_out, conv_rows)
    glu_other = swapped(glu_own)
    down_other = swapped(down_own)
    spectrum = filter_spectrum(after(lag_own, glu_own), lag_back, tables)
    conv_out, signal_spec = conv_forward(after(conv_channels, spectrum), spectrum, tables, seqs)
    conv_tokens = to_tokens(conv_out)

    early = [after(x, conv_out) for x in early]
    rows_in = jnp.stack([x[:width] for x in early])
    if quick:
        plane_tiles = [rows_in] + [crossed(rows_in, d) for d in range(1, per_plane)]
        turns = [[(0, d)] for d in range(per_plane)]
    else:
        plane_tiles = [gathered_over(rows_in, per_plane, within).reshape(per_plane * blocks, width, rows)]
        turns = [[(0, r) for r in range(per_plane)]]
    gated_grad, mid, layer_output, extra, extra_other, gain_sum, *sent = middle_part(
        conv_tokens, sm2, layer_input, out_grad, glu_gain, out_proj, glu_own, glu_other,
        down_own, down_other, per_plane
    )
    gated_channels = to_channels(gated_grad)
    across = lambda parts: [parts[0]] + [crossed(parts[d], d * per_plane) for d in range(1, blocks)]
    late = across(sent)
    extra_back = swapped(extra_other)
    plane_tiles = [after(x, gated_grad) for x in plane_tiles]
    tiles = plane_tiles + [swapped(x) for x in plane_tiles]
    turns = turns + [[(1, r) for _, r in t] for t in turns]
    turns = tuple(tuple(t) for t in turns)
    proj_channels, mixed_channels = channel_mixer(tiles, turns, place, w_in, short_taps, devices, seqs, chans)

    late = [after(x, proj_channels, gated_channels) for x in late]
    g_own, g_other = glu_grads(late, early, glu_own, glu_other, down_own, down_other, per_plane)
    g_back = swapped(g_other)
    if quick:
        sums = exchanged(plane_add(g_own, g_back, extra, extra_back, per_plane), "seq", within)

    pg, cross, tap_sums = conv_backward(
        after(gated_channels, g_own), mixed_channels, proj_channels, conv_out, signal_spec, short_taps, spectrum, tables,
        seqs, chans
    )
    pg_sent = pg.reshape(devices, 3, chans_padded, rows)[:, :, :chans].reshape(devices, 3 * chans, rows)
    if quick:
        pg_sent = after(pg_sent, sums)
    pg_tokens = exchanged(pg_sent, both)
    if chans != chans_padded:
        pg_tokens = pg_tokens.reshape(devices, 3, chans, rows).transpose(1, 0, 2, 3).reshape(3, model, rows)

    if quick:
        glu_piece = plane_sum(after(sums, pg))
        glu_parts = across([glu_piece] * blocks)
        tap_sums = after(tap_sums, glu_piece)
    cross_back = swapped(cross)
    in_piece, g3 = channel_grads(
        tiles, turns, place, pg, tap_sums, cross, cross_back, tables, features, filter_w2, w3t, decay, gain_sum, saved
    )
    g3_back = swapped(g3)
    if quick:
        in_parts = [in_piece] + [crossed(in_piece, d) for d in range(1, per_plane)]
        glu_parts = plane_join([after(x, in_piece) for x in glu_parts], 3 * width // per_plane, (per_plane,))
        pg_tokens = after(pg_tokens, glu_parts)
    input_half = mixer_back(pg_tokens, mid, layer_input, mixer_gain, w_in, chans == chans_padded)
    input_other = swapped(input_half)

    if quick:
        in_parts = plane_join([after(x, input_half) for x in in_parts], 3 * chans_padded)
        in_full = across([in_parts] * blocks)
        glu_full = exchanged(after(glu_parts, in_parts), "seq", within)
        in_full = in_full + [swapped(x) for x in in_full]
        in_proj_grad, short_taps_grad, mixer_gain_grad, w1_grad, b1_grad, w2_grad, glu_gain_grad = in_unpack(
            in_full, place, w_in, mixer_gain
        )
        glu_full = after(glu_full, glu_gain_grad)
        out_mine = glu_full[:, 3 * width :, :]
        out_theirs = swapped(out_mine)
        glu_in_grad, glu_out_grad, input_grad = finish(
            after(glu_full, out_mine), input_half, input_other, per_plane, width
        )
        out_proj_grad = out_unpack(out_mine, after(out_theirs, glu_out_grad))
        in_proj_grad = in_proj_grad.transpose(1, 0, 2)
    else:
        total = (g_own + g_back.astype(F32)).astype(BF)
        piece = exchanged(total, "seq", within).reshape(per_plane, -1, half)
        piece = jnp.sum(piece.astype(F32), axis=0).astype(BF)
        full = gathered_over(piece, seq_devices).reshape(blocks, -1, half).astype(F32)
        glu_in_grad = full[:, : 2 * width].reshape(blocks, 2, width, half).transpose(0, 2, 1, 3)
        glu_out_grad = full[:, 2 * width :].transpose(2, 0, 1).reshape(half, model)
        total = (extra.astype(F32) + extra_back.astype(F32)).astype(BF)
        piece = exchanged(total.reshape(seq_devices, -1), "seq")
        piece = jnp.sum(piece.astype(F32), axis=0).astype(BF)
        mine = gathered_over(piece, seq_devices).reshape(width, model // 2).astype(F32)
        theirs = swapped(mine)
        out_proj_grad = jnp.where(
            tp_index == 0, jnp.concatenate([mine, theirs], axis=1), jnp.concatenate([theirs, mine], axis=1)
        )
        mine = gathered_over(in_piece, seq_devices)
        theirs = swapped(mine)
        pair = jnp.where(tp_index == 0, jnp.stack([mine, theirs], 1), jnp.stack([theirs, mine], 1)).astype(F32)
        pair = pair.reshape(devices, -1, 2 * LANES)
        small = jnp.sum(pair[:, 3 * chans_padded :], axis=0)
        small = jnp.concatenate([small[:, :LANES], small[:, LANES:]], axis=0)
        w1_grad, b1_grad, w2_grad = small[hidden : hidden + 5], small[hidden + 5], small[:hidden]
        glu_gain_grad = small[hidden + 8 : hidden + 8 + model // LANES].reshape(model)
        pair = pair[:, : 3 * chans_padded].reshape(devices, 3, chans_padded, 2 * LANES)[:, :, :chans]
        pair = pair.transpose(1, 0, 2, 3).reshape(3, model, 2 * LANES)
        in_proj_grad = pair[:, :, :width].transpose(2, 0, 1)
        short_taps_grad = pair[:, :, width : width + 3].transpose(2, 0, 1)
        products = in_proj_grad * in_proj.astype(F32)
        products = jnp.sum(products.reshape(width, 3, blocks, width), axis=(1, 3))
        mixer_gain_grad = products.T.reshape(model) / mixer_gain
        input_grad = jnp.where(
            tp_index == 0,
            jnp.concatenate([input_half, input_other], axis=0),
            jnp.concatenate([input_other, input_half], axis=0),
        )

    mine = g3[:chans] + g3_back[chans_padded : chans_padded + chans]
    theirs = g3[chans_padded : chans_padded + chans] + g3_back[:chans]
    g3_full = jnp.where(
        tp_index == 0, jnp.concatenate([mine, theirs], axis=0), jnp.concatenate([theirs, mine], axis=0)
    ).T
    return (
        layer_output,
        input_grad,
        mixer_gain_grad,
        in_proj_grad,
        short_taps_grad,
        w1_grad,
        b1_grad,
        w2_grad,
        g3_full,
        out_proj_grad,
        glu_gain_grad,
        glu_in_grad,
        glu_out_grad,
    )


def solution(mesh):
    placed = (
        P("seq", None),
        P(),
        P(),
        P(),
        P(),
        P(),
        P(),
        P(None, "seq"),
        P("seq"),
        P(),
        P(),
        P(None, None, None, "tp"),
        P("tp", None),
        P(("seq", "tp"), None),
    )
    return jax.shard_map(
        local,
        mesh=mesh,
        in_specs=placed,
        out_specs=(
            P(("seq", "tp"), None),
            P("seq", None),
            P(),
            P(),
            P(),
            P(),
            P(),
            P(),
            P(None, "seq"),
            P(),
            P(),
            P(None, None, None, "tp"),
            P("tp", None),
        ),
        check_vma=False,
    )
```

```python
import math
import functools

import jax
import jax.numpy as jnp
import ml_dtypes
import numpy as np
from jax import lax
from jax.experimental import pallas as pl
from jax.experimental.pallas import tpu as pltpu
from jax.sharding import PartitionSpec as P

MIN_LEN = 8192
SLOW_PATH = False
EPSILON = 1e-05
LANES = 128
GROUP = 8
FILTER_LANES = 2048
SMALL_ROWS = 72
BACK_MIB = 24
BF = jnp.bfloat16
F32 = jnp.float32

PI_HIGH = 3.140625
ROUNDER = 12582912.0
PI_LOW = 9.67653589793e-4
SIN_C = (1.0, -0.16666647791862488, 0.00833289884030819, -0.0001980081869987771, 2.590327312645968e-06)
COS_C = (0.9999999403953552, -0.4999990463256836, 0.041663575917482376, -0.0013853635173290968, 2.315232813998591e-05)


def vmem_specs(count):
    return [pl.BlockSpec(memory_space=pltpu.VMEM)] * count


def params(mib=60):
    return pltpu.CompilerParams(vmem_limit_bytes=mib * 1024 * 1024)


def cost(flops, bytes_accessed=0, transcendentals=0):
    return pl.CostEstimate(flops=flops // 20, bytes_accessed=bytes_accessed // 20, transcendentals=0)


def split_np(table):
    high = np.asarray(table, np.float32).astype(ml_dtypes.bfloat16)
    low = (np.asarray(table, np.float64) - high.astype(np.float64)).astype(ml_dtypes.bfloat16)
    return high, low


def split3_np(table):
    table = np.asarray(table, np.float64)
    high = table.astype(np.float32).astype(ml_dtypes.bfloat16)
    rest = table - high.astype(np.float64)
    mid = rest.astype(np.float32).astype(ml_dtypes.bfloat16)
    low = (rest - mid.astype(np.float64)).astype(np.float32).astype(ml_dtypes.bfloat16)
    return high, mid, low


@functools.lru_cache(maxsize=None)
def transform_tables(seq_length):
    period = 2 * seq_length
    first = period // LANES
    kept = first // 2 + 1
    padded = -(-kept // 8) * 8
    k = np.arange(padded)
    live = (k < kept).astype(np.float64)
    n = np.arange(first)
    angle = 2 * np.pi / first * ((k[:, None] * n[None, :]) % first)
    eye = np.eye(GROUP)
    stage = np.zeros((GROUP, 2, padded, first, GROUP))
    stage[:, 0] = np.einsum("kn,cd->cknd", np.cos(angle) * live[:, None], eye)
    stage[:, 1] = np.einsum("kn,cd->cknd", -np.sin(angle) * live[:, None], eye)
    forward = stage.reshape(GROUP * 2 * padded, first * GROUP)
    backward = forward.T
    m = np.arange(LANES)
    turn = 2 * np.pi / period * ((k[:, None] * m[None, :]) % period)
    weight = np.where((k == 0) | (k == first // 2), 1.0, 2.0) * live / period
    twiddle = np.stack(
        [np.cos(turn), np.sin(turn), np.cos(turn) * weight[:, None], np.sin(turn) * weight[:, None]]
    ).astype(np.float32)
    inner = 2 * np.pi / LANES * ((m[:, None] * m[None, :]) % LANES)
    c, s = np.cos(inner), np.sin(inner)
    second = np.block([[c, -s], [s, c]])
    return {
        "forward": split_np(forward),
        "backward": split_np(backward),
        "forward_used": split_np(forward[:, : first // 2 * GROUP]),
        "backward_used": split_np(backward[: first // 2 * GROUP]),
        "twiddle": twiddle,
        "second": split_np(second),
        "inverse": split_np(second.T),
        "first": first,
        "padded": padded,
    }


@functools.lru_cache(maxsize=None)
def feature_table(seq_length):
    period = 2 * seq_length
    index = np.arange(period)
    lag = np.where(index < seq_length, index, index - period)
    q = lag / seq_length
    rows = [q, np.cos(2 * np.pi * q), np.cos(4 * np.pi * q), np.sin(2 * np.pi * q), np.sin(4 * np.pi * q)]
    rows.append(np.ones_like(q))
    rows += [np.zeros_like(q)] * 2
    high, mid, low = split3_np(np.stack(rows))
    return np.concatenate([high, high, mid, high, mid, low], axis=0)


def split(values):
    high = values.astype(BF)
    low = (values - high.astype(F32)).astype(BF)
    return high, low


def first_weights(w1_ref, b1_ref):
    hidden = w1_ref.shape[1]
    rows = jnp.concatenate([w1_ref[...], b1_ref[...].reshape(1, hidden), jnp.zeros((2, hidden), F32)], axis=0)
    high = rows.astype(BF).astype(F32)
    mid = (rows - high).astype(BF).astype(F32)
    low = rows - high - mid
    return jnp.concatenate([high, mid, high, low, mid, high], axis=0).astype(BF)


def mm(a, b):
    return jnp.dot(a, b, preferred_element_type=F32)


def mm_nt(a, b):
    return lax.dot_general(a, b, (((1,), (1,)), ((), ())), preferred_element_type=F32)


def mm_tn(a, b):
    return lax.dot_general(a, b, (((0,), (0,)), ((), ())), preferred_element_type=F32)


def mm3(a, b):
    ah, al = a
    bh, bl = b
    return mm(ah, bh) + (mm(al, bh) + mm(ah, bl))


def mm3_tn(a, b):
    ah, al = a
    bh, bl = b
    return mm_tn(ah, bh) + (mm_tn(al, bh) + mm_tn(ah, bl))


def sine_cosine(x):
    n = (x * (0.5 / math.pi) + ROUNDER) - ROUNDER
    t = (x * 0.5 - n * PI_HIGH) - n * PI_LOW
    t2 = t * t
    s = SIN_C[4]
    for c in SIN_C[3::-1]:
        s = s * t2 + c
    s = s * t
    k = COS_C[4]
    for c in COS_C[3::-1]:
        k = k * t2 + c
    twice = s + s
    return twice * k, 1.0 - twice * s


def lag_decay(decay, start, width, seq_length):
    lane = lax.broadcasted_iota(jnp.int32, decay.shape[:1] + (width,), 1) + start
    lag = jnp.where(lane < seq_length, lane, 2 * seq_length - lane).astype(F32)
    return jnp.exp(lag * (decay[:, :1] * (-1.0 / seq_length)))


def stacked_weights(w):
    high, low = split(w)
    zero = jnp.zeros_like(high)
    return jnp.concatenate(
        [jnp.concatenate([high, high], axis=1), jnp.concatenate([low, zero], axis=1)], axis=0
    )


def stacked_product(weights, values):
    out = mm(weights, jnp.concatenate(split(values), axis=0))
    rows = out.shape[0] // 2
    return out[:rows] + out[rows:]


def decay_columns(ref):
    row = jnp.broadcast_to(ref[...].reshape(1, -1), (LANES, ref.shape[0]))
    rows = row.T
    half = ref.shape[0] // 2
    a, b = rows[:half], rows[half:]
    first = lax.axis_index("tp") == 0
    return jnp.concatenate([jnp.where(first, a, b), jnp.where(first, b, a)], axis=0)


def own_first(ref):
    half = ref.shape[0] // 2
    me = lax.axis_index("tp")
    return jnp.concatenate([ref[pl.ds(me * half, half), :], ref[pl.ds((1 - me) * half, half), :]], axis=0)


def filter_forward_kernel(feat_ref, w1_ref, b1_ref, w2_ref, w3_ref, decay_ref, own_ref, other_ref, a_ref, ac_ref, b_ref, bc_ref):
    length = own_ref.shape[1]
    channels = own_ref.shape[0]
    width = min(FILTER_LANES, length)
    begin = lax.axis_index("tp") * length
    w1 = first_weights(w1_ref, b1_ref)
    w2 = stacked_weights(w2_ref[...].T)
    w3 = stacked_weights(own_first(w3_ref))
    decay = decay_columns(decay_ref)
    for lo in range(0, length, width):
        lanes = slice(lo, lo + width)
        start = pl.multiple_of(begin + lo, LANES)
        s1, c1 = sine_cosine(mm_tn(w1, feat_ref[:, pl.ds(start, width)]))
        a_ref[:, lanes] = s1.astype(BF)
        ac_ref[:, lanes] = c1.astype(BF)
        s2, c2 = sine_cosine(stacked_product(w2, s1))
        b_ref[:, lanes] = s2.astype(BF)
        bc_ref[:, lanes] = c2.astype(BF)
        lag = stacked_product(w3, s2) * lag_decay(decay, start, width, length)
        own_ref[:, lanes] = lag[:channels]
        other_ref[:, lanes] = lag[channels:]


def filter_forward(features, w1, b1, w2, w3t, decay):
    hidden = w2.shape[0]
    channels = w3t.shape[0] // 2
    length = features.shape[1] // 2
    return pl.pallas_call(
        filter_forward_kernel,
        in_specs=vmem_specs(6),
        out_specs=vmem_specs(6),
        out_shape=[jax.ShapeDtypeStruct((channels, length), F32)] * 2
        + [jax.ShapeDtypeStruct((hidden, length), BF)] * 4,
        compiler_params=params(),
        cost_estimate=cost(8 * 10**9, 8 * 10**6),
        name="filter_forward",
    )(features, w1, b1, w2, w3t, decay)


def inner_spectrum(a, twiddle_ref, second, padded, columns):
    tc, ts = twiddle_ref[0], twiddle_ref[1]
    parts = []
    for col in range(columns):
        lanes = slice(col * LANES, (col + 1) * LANES)
        for c in range(GROUP):
            base = c * 2 * padded
            re = a[base : base + padded, lanes]
            im = a[base + padded : base + 2 * padded, lanes]
            parts.append(jnp.concatenate([re * tc + im * ts, im * tc - re * ts], axis=1))
    return mm3(split(jnp.concatenate(parts, axis=0)), second)


def signal_of(spec, inverse, twiddle_ref, back, padded, columns):
    b = mm3(split(spec), inverse)
    tc, ts = twiddle_ref[2], twiddle_ref[3]
    cols = []
    for col in range(columns):
        parts = []
        for c in range(GROUP):
            base = (col * GROUP + c) * padded
            re = b[base : base + padded, :LANES]
            im = b[base : base + padded, LANES:]
            parts.append(re * tc - im * ts)
            parts.append(im * tc + re * ts)
        cols.append(jnp.concatenate(parts, axis=0))
    z = split(jnp.concatenate(cols, axis=1))
    return [mm3(rows, z) for rows in back]


def gathered(x, seqs, rows, groups):
    cols = []
    for q in range(seqs):
        for g in range(groups):
            block = x[q * rows : (q + 1) * rows, g * GROUP : (g + 1) * GROUP, :]
            cols.append(block.reshape(rows * GROUP, LANES))
    return jnp.concatenate(cols, axis=1)


def scattered(y, seqs, rows, groups):
    out = []
    for q in range(seqs):
        cols = [
            y[:, (q * groups + g) * LANES : (q * groups + g + 1) * LANES].reshape(rows, GROUP, LANES)
            for g in range(groups)
        ]
        out.append(jnp.concatenate(cols, axis=1))
    return jnp.concatenate(out, axis=0)


def product(a, b, conjugate):
    ar, ai = a[:, :LANES], a[:, LANES:]
    br, bi = b[:, :LANES], b[:, LANES:]
    if conjugate:
        return jnp.concatenate([ar * br + ai * bi, ai * br - ar * bi], axis=1)
    return jnp.concatenate([ar * br - ai * bi, ar * bi + ai * br], axis=1)


def filter_spectrum_kernel(padded, own_ref, other_ref, fh, fl, tw, sh, sl, out_ref):
    groups = own_ref.shape[0] // GROUP
    rows = own_ref.shape[1] // LANES
    used = rows * GROUP
    me = lax.axis_index("tp")
    total = None
    for lag_ref, half in ((own_ref, me), (other_ref, 1 - me)):
        cols = []
        for g in range(groups):
            tiles = [lag_ref[g * GROUP : (g + 1) * GROUP, n * LANES : (n + 1) * LANES] for n in range(rows)]
            cols.append(jnp.concatenate(tiles, axis=0))
        begin = pl.multiple_of(half * used, LANES)
        table = (fh[:, pl.ds(begin, used)], fl[:, pl.ds(begin, used)])
        part = mm3(table, split(jnp.concatenate(cols, axis=1)))
        total = part if total is None else total + part
    out_ref[...] = inner_spectrum(total, tw, (sh[...], sl[...]), padded, groups)


def signal_spectrum(x, seqs, fh, fl, tw, sh, sl, padded):
    rows = x.shape[0] // seqs
    groups = x.shape[1] // GROUP
    used = rows * GROUP
    flat = gathered(x, seqs, rows, groups).astype(BF)
    a = mm(fh[:, :used], flat) + mm(fl[:, :used], flat)
    return inner_spectrum(a, tw, (sh[...], sl[...]), padded, seqs * groups)


def filtered(spec, h_ref, seqs, conjugate, tw, ih, il, bh, bl, padded, shape):
    rows = shape[0] // seqs
    groups = shape[1] // GROUP
    used = rows * GROUP
    prod = product(spec, jnp.concatenate([h_ref[...]] * seqs, axis=0), conjugate)
    (y,) = signal_of(prod, (ih[...], il[...]), tw, [(bh[:used, :], bl[:used, :])], padded, seqs * groups)
    return scattered(y, seqs, rows, groups)


def conv_forward_kernel(padded, seqs, x_ref, h_ref, fh, fl, tw, sh, sl, ih, il, bh, bl, y_ref, spec_ref):
    x = x_ref[...].astype(F32)
    spec = signal_spectrum(x, seqs, fh, fl, tw, sh, sl, padded)
    spec_ref[...] = spec
    y_ref[...] = filtered(spec, h_ref, seqs, False, tw, ih, il, bh, bl, padded, x.shape).astype(BF)


def conv_backward_kernel(padded, seqs, real, g_ref, sm_ref, p_ref, y_ref, saved_ref, taps_ref, h_ref, fh, fl, tw, sh, sl, ih, il, bh, bl,
                         pg_ref, cross_ref, st_ref, sent_ref, icg_ref):
    count, chans, _ = g_ref.shape
    gated = g_ref[...].astype(F32)
    conv_grad = gated * sm_ref[:, 2 * chans :, :]
    spec = signal_spectrum(conv_grad, seqs, fh, fl, tw, sh, sl, padded)
    cross = product(spec, saved_ref[...], True)
    height = cross_ref.shape[0]
    cross_ref[...] = sum(cross[q * height : (q + 1) * height] for q in range(seqs))
    icg = filtered(spec, h_ref, seqs, True, tw, ih, il, bh, bl, padded, g_ref.shape)
    icg_ref[...] = icg.astype(BF).astype(F32)
    per_seq = count // seqs
    taps = tap_columns(taps_ref, real)
    lane = lax.broadcasted_iota(jnp.int32, (3 * chans, LANES), 1)
    first_lanes = lane[:GROUP]

    def edge_of(back):
        out = jnp.zeros((GROUP, LANES), F32)
        for a in range(chans // GROUP):
            rows = back[a * GROUP : (a + 1) * GROUP]
            rows = pltpu.roll(rows, 2 * a, 1) if a else rows
            out = jnp.where((first_lanes >= 2 * a) & (first_lanes < 2 * a + 2), rows, out)
        return out

    def step(i, carry):
        next1, next2, acc0, acc1, acc2, next_edge = carry
        n = count - 1 - i
        keep = jnp.where(lax.rem(n + 1, per_seq) == 0, 0.0, 1.0)
        sm = sm_ref[n]
        back = icg_ref[n]
        sg = jnp.concatenate(
            [back * sm[chans : 2 * chans], back * sm[:chans], g_ref[n].astype(F32) * y_ref[n].astype(F32)], axis=0
        )
        r1 = pltpu.roll(sg, LANES - 1, 1)
        r2 = pltpu.roll(sg, LANES - 2, 1)
        s1 = jnp.where(lane < LANES - 1, r1, next1 * keep)
        s2 = jnp.where(lane < LANES - 2, r2, next2 * keep)
        pg_ref[n] = (taps[0] * sg + taps[1] * s1 + taps[2] * s2).astype(BF)
        sent_ref[n] = jnp.concatenate([back, next_edge * keep], axis=0).astype(BF)
        p = p_ref[n]
        return r1, r2, acc0 + sg * p, acc1 + s1 * p, acc2 + s2 * p, edge_of(back)

    zero = jnp.zeros((3 * chans, LANES), F32)
    _, _, acc0, acc1, acc2, _ = lax.fori_loop(0, count, step, (zero,) * 5 + (zero[:GROUP],), unroll=4)
    out = zero
    for k, acc in enumerate((acc0, acc1, acc2)):
        out = jnp.where(lane == k, jnp.sum(acc, axis=1, keepdims=True), out)
    st_ref[...] = out


def filter_spectrum(own, other, tables):
    padded = tables["padded"]
    return pl.pallas_call(
        functools.partial(filter_spectrum_kernel, padded),
        in_specs=vmem_specs(7),
        out_specs=vmem_specs(1)[0],
        out_shape=jax.ShapeDtypeStruct((own.shape[0] * padded, 2 * LANES), F32),
        compiler_params=params(),
        cost_estimate=cost(4 * 10**9, 4 * 10**6),
        name="filter_spectrum",
    )(own, other, *tables["forward"], tables["twiddle"], *tables["second"])


def transforms(tables):
    return (*tables["forward_used"], tables["twiddle"], *tables["second"], *tables["inverse"], *tables["backward_used"])


def conv_forward(x, spectrum, tables, seqs):
    padded = tables["padded"]
    return pl.pallas_call(
        functools.partial(conv_forward_kernel, padded, seqs),
        in_specs=vmem_specs(11),
        out_specs=vmem_specs(2),
        out_shape=[
            jax.ShapeDtypeStruct(x.shape, BF),
            jax.ShapeDtypeStruct((seqs * x.shape[1] * padded, 2 * LANES), F32),
        ],
        compiler_params=params(),
        cost_estimate=cost(5 * 10**9, 6 * 10**6),
        name="conv_forward",
    )(x, spectrum, *transforms(tables))


def conv_backward(gated, mixed, proj, conv_out, saved, taps, spectrum, tables, seqs, real):
    padded = tables["padded"]
    count, chans, _ = gated.shape
    return pl.pallas_call(
        functools.partial(conv_backward_kernel, padded, seqs, real),
        in_specs=vmem_specs(16),
        out_specs=vmem_specs(4),
        out_shape=[
            jax.ShapeDtypeStruct((count, 3 * chans, LANES), BF),
            jax.ShapeDtypeStruct((chans * padded, 2 * LANES), F32),
            jax.ShapeDtypeStruct((3 * chans, LANES), F32),
            jax.ShapeDtypeStruct((count, chans + GROUP, LANES), BF),
        ],
        scratch_shapes=[pltpu.VMEM(gated.shape, F32)],
        compiler_params=params(),
        cost_estimate=cost(7 * 10**9, 9 * 10**6),
        name="conv_backward",
    )(gated, mixed, proj, conv_out, saved, taps, spectrum, *transforms(tables))


def source_of(place, turn, group):
    per_plane, relative = place
    seq = lax.axis_index("seq")
    plane = lax.div(seq, per_plane)
    inside = lax.rem(seq, per_plane)
    half, index = turn
    inner = lax.bitwise_xor(inside, index) if relative else index
    return (lax.bitwise_xor(plane, group) * per_plane + inner) * 2 + lax.bitwise_xor(lax.axis_index("tp"), half)


def own_channels(ref, index, chans):
    model = ref.shape[-1]
    linear = lax.axis_index("seq") * 2 + lax.axis_index("tp")
    first = linear * chans
    window = jnp.minimum(lax.div(first, LANES) * LANES, model - 2 * LANES)
    part = ref[index, :, pl.ds(pl.multiple_of(window, LANES), 2 * LANES)].astype(F32)
    part = pltpu.roll(part, lax.rem(2 * LANES - (first - window), 2 * LANES), 1)
    turned = part[:, :LANES].T
    return turned[: -(-chans // GROUP) * GROUP]


def tap_columns(taps_ref, chans):
    out = []
    for k in range(3):
        cols = own_channels(taps_ref, k, chans)
        out.append(jnp.concatenate([jnp.broadcast_to(cols[:, p : p + 1], (cols.shape[0], LANES)) for p in range(3)], axis=0))
    return out


def channel_mixer_kernel(place, turns, seqs, chans, w_ref, taps_ref, *refs):
    tiles, (p_ref, sm_ref) = refs[:-2], refs[-2:]
    count, rows3, _ = p_ref.shape
    wc = jnp.concatenate([own_channels(w_ref, p, chans) for p in range(3)], axis=0).astype(BF)
    for ref, turn_list in zip(tiles, turns):
        for q, turn in enumerate(turn_list):
            x = jnp.concatenate([ref[4 * q + z] for z in range(4)], axis=1)
            p = mm(wc, x).astype(BF).astype(F32)
            for z in range(4):
                p_ref[source_of(place, turn, z)] = p[:, z * LANES : (z + 1) * LANES]
    per_seq = count // seqs
    taps = tap_columns(taps_ref, chans)
    lane = lax.broadcasted_iota(jnp.int32, (rows3, LANES), 1)

    def step(n, carry):
        last1, last2 = carry
        keep = jnp.where(lax.rem(n, per_seq) == 0, 0.0, 1.0)
        p = p_ref[n]
        r1 = pltpu.roll(p, 1, 1)
        r2 = pltpu.roll(p, 2, 1)
        s1 = jnp.where(lane < 1, last1 * keep, r1)
        s2 = jnp.where(lane < 2, last2 * keep, r2)
        sm_ref[n] = taps[0] * p + taps[1] * s1 + taps[2] * s2
        return r1, r2

    zero = jnp.zeros((rows3, LANES), F32)
    lax.fori_loop(0, count, step, (zero, zero), unroll=4)


def channel_mixer(tiles, turns, place, w, taps, count, seqs, chans):
    rows3 = 3 * (-(-chans // GROUP) * GROUP)
    return pl.pallas_call(
        functools.partial(channel_mixer_kernel, place, turns, seqs, chans),
        in_specs=vmem_specs(2 + len(tiles)),
        out_specs=vmem_specs(2),
        out_shape=[jax.ShapeDtypeStruct((count, rows3, LANES), F32)] * 2,
        compiler_params=params(),
        cost_estimate=cost(3 * 10**9, 6 * 10**6),
        name="channel_mixer",
    )(w, taps, *tiles)


def channel_grads_kernel(place, turns, padded, count, pg_ref, st_ref, own_ref, other_ref, tw, ih, il, bh, bl, feat_ref, w2_ref,
                         w3_ref, decay_ref, gain_ref, a_ref, ac_ref, b_ref, bc_ref, *refs):
    tiles, (out_ref, g3_ref, keep_ref, lag_ref) = refs[:count], refs[count:]
    total = None
    for ref, turn_list in zip(tiles, turns):
        for q, turn in enumerate(turn_list):
            x = jnp.concatenate([ref[4 * q + z] for z in range(4)], axis=1)
            g = jnp.concatenate([pg_ref[source_of(place, turn, z)] for z in range(4)], axis=1)
            part = mm_nt(g, x)
            total = part if total is None else total + part
    rows3, width = total.shape
    keep_ref[...] = jnp.zeros_like(keep_ref)
    keep_ref[:rows3, :width] = total
    keep_ref[:rows3, width : width + 3] = st_ref[:, :3]

    length = lag_ref.shape[1]
    rows = length // LANES
    used = rows * GROUP
    channels = lag_ref.shape[0] // 2
    groups = channels // GROUP
    begin = pl.multiple_of(lax.axis_index("tp") * used, LANES)
    back = (bh[pl.ds(begin, used), :], bl[pl.ds(begin, used), :])
    for half, ref in enumerate((own_ref, other_ref)):
        (y,) = signal_of(ref[...], (ih[...], il[...]), tw, [back], padded, groups)
        for g in range(groups):
            base = half * channels + g * GROUP
            for n in range(rows):
                lag_ref[base : base + GROUP, n * LANES : (n + 1) * LANES] = y[
                    n * GROUP : (n + 1) * GROUP, g * LANES : (g + 1) * LANES
                ]

    span = min(FILTER_LANES, length)
    begin = lax.axis_index("tp") * length
    w2 = stacked_weights(w2_ref[...])
    w3 = split(own_first(w3_ref))
    decay = decay_columns(decay_ref)
    g1 = g2 = g3 = 0.0
    for lo in range(0, length, span):
        lanes = slice(lo, lo + span)
        start = pl.multiple_of(begin + lo, LANES)
        wh, wl = split(lag_ref[:, lanes] * lag_decay(decay, start, span, length))
        second = b_ref[:, lanes]
        g3 += mm_nt(wh, second) + mm_nt(wl, second)
        pre2 = mm3_tn(w3, (wh, wl)) * bc_ref[:, lanes].astype(F32)
        g2 += mm_nt(a_ref[:, lanes], pre2.astype(BF))
        pre1 = stacked_product(w2, pre2) * ac_ref[:, lanes].astype(F32)
        g1 += mm_nt(feat_ref[:8, pl.ds(start, span)], pre1.astype(BF))
    g3_ref[...] = g3
    more = out_ref.shape[0] - rows3
    gains = [gain_ref[k * LANES : (k + 1) * LANES].reshape(1, LANES) for k in range(gain_ref.shape[0] // LANES)]
    gains += [jnp.zeros((8 - len(gains), LANES), F32)]
    keep_ref[rows3:, :LANES] = g2[:more]
    keep_ref[rows3:, LANES:] = jnp.concatenate([g2[more:], g1] + gains, axis=0)
    out_ref[...] = keep_ref[...].astype(BF)


def channel_grads(tiles, turns, place, pg, st, own, other, tables, features, w2, w3t, decay, gain, saved):
    rows3 = pg.shape[1]
    hidden = w2.shape[0]
    length = features.shape[1] // 2
    return pl.pallas_call(
        functools.partial(channel_grads_kernel, place, turns, tables["padded"], len(tiles)),
        in_specs=vmem_specs(18 + len(tiles)),
        out_specs=vmem_specs(2),
        out_shape=[
            jax.ShapeDtypeStruct((rows3 + SMALL_ROWS, 2 * LANES), BF),
            jax.ShapeDtypeStruct((w3t.shape[0], hidden), F32),
        ],
        scratch_shapes=[
            pltpu.VMEM((rows3 + SMALL_ROWS, 2 * LANES), F32),
            pltpu.VMEM((w3t.shape[0], length), F32),
        ],
        compiler_params=params(),
        cost_estimate=cost(8 * 10**9, 8 * 10**6),
        name="channel_grads",
    )(pg, st, own, other, tables["twiddle"], *tables["inverse"], *tables["backward"], features, w2, w3t, decay, gain,
      *saved, *tiles)


def erf_parts(g):
    x = jnp.abs(g) * (1.0 / math.sqrt(2.0))
    t = 1.0 / (1.0 + 0.3275911 * x)
    e = jnp.exp(-x * x)
    poly = t * (0.254829592 + t * (-0.284496736 + t * (1.421413741 + t * (-1.453152027 + t * 1.061405429))))
    tail = 0.5 * poly * e
    return jnp.where(g < 0, tail, 1.0 - tail), e


def norm_stats(v):
    centered = v - jnp.mean(v, axis=-1, keepdims=True)
    variance = jnp.mean(centered * centered, axis=-1, keepdims=True)
    r = lax.rsqrt(variance + EPSILON)
    return centered * r, r


def norm_backward(w, gain, xhat, r):
    a = w * gain
    return r * (a - jnp.mean(a, axis=-1, keepdims=True) - xhat * jnp.mean(a * xhat, axis=-1, keepdims=True))


def column(j, width):
    return slice(j * width, (j + 1) * width)


def own_part(ref, rows):
    return ref[pl.ds(pl.multiple_of(lax.axis_index("tp") * rows, rows), rows), :]


def mixer_in_kernel(per_plane, seq_length, x_ref, halo_ref, gain_ref, w_ref, taps_ref, og_ref, conv_ref, sm2_ref, proj_ref, start_ref,
                    z0, z1, z2, z3, keep_ref):
    rows = sm2_ref.shape[0]
    width = w_ref.shape[1]
    blocks = w_ref.shape[2] // width
    lead = halo_ref.shape[0]
    linear = lax.axis_index("seq") * 2 + lax.axis_index("tp")
    keep = jnp.where(lax.rem(linear * rows, seq_length) == 0, 0.0, 1.0)
    inner = x_ref[rows - lead : rows, :].astype(F32)
    halo = jnp.where(lax.axis_index("tp") == 0, halo_ref[...].astype(F32), inner) * keep
    x = jnp.concatenate([halo, own_part(x_ref, rows).astype(F32)], axis=0)
    xhat, _ = norm_stats(x)
    normed = xhat * gain_ref[...].reshape(1, -1)
    n1 = normed.astype(BF)
    mixed = []
    for p in range(3):
        proj = jnp.concatenate(
            [mm(n1[:, column(j, width)], w_ref[p, :, column(j, width)]) for j in range(blocks)], axis=1
        )
        low = proj.astype(BF)
        if p < 2:
            proj_ref[p] = low
        proj = low.astype(F32)
        mixed.append(
            taps_ref[0, p : p + 1, :] * proj[lead : lead + rows]
            + taps_ref[1, p : p + 1, :] * proj[lead - 1 : lead - 1 + rows]
            + taps_ref[2, p : p + 1, :] * proj[lead - 2 : lead - 2 + rows]
        )
    sm2_ref[...] = mixed[2]
    start_ref[:8, :] = mixed[0][:8]
    start_ref[8:, :] = mixed[1][:8]
    conv_ref[...] = (mixed[0] * mixed[1]).T.astype(BF)
    nt = normed[lead : lead + rows].T.astype(BF)
    ot = og_ref[...].astype(F32).T.astype(BF)
    for j in range(blocks):
        keep_ref[j, :width, :] = nt[column(j, width)]
        keep_ref[j, width:, :] = ot[column(j, width)]
    plane = lax.div(lax.axis_index("seq"), per_plane)
    for d, out in enumerate((z0, z1, z2, z3)):
        out[...] = keep_ref[lax.bitwise_xor(plane, d)]


def mixer_in(x, halo, gain, w, taps, og, per_plane, seq_length):
    rows, model = og.shape
    width = w.shape[1]
    return pl.pallas_call(
        functools.partial(mixer_in_kernel, per_plane, seq_length),
        in_specs=vmem_specs(6),
        out_specs=vmem_specs(8),
        out_shape=[
            jax.ShapeDtypeStruct((model, rows), BF),
            jax.ShapeDtypeStruct((rows, model), F32),
            jax.ShapeDtypeStruct((2, rows + halo.shape[0], model), BF),
            jax.ShapeDtypeStruct((16, model), F32),
        ]
        + [jax.ShapeDtypeStruct((2 * width, rows), BF)] * 4,
        scratch_shapes=[pltpu.VMEM((model // width, 2 * width, rows), BF)],
        compiler_params=params(24),
        cost_estimate=cost(4 * 10**9, 4 * 10**6),
        name="mixer_in",
    )(x, halo, gain, w, taps, og)


def glu_block(x, og, w_pairs, d_pairs):
    down = None
    back = None
    for (wg, wu), wd in zip(w_pairs, d_pairs):
        gate = mm(x, wg)
        up = mm(x, wu)
        phi, e = erf_parts(gate)
        act = gate * phi
        hidden = (act * up).astype(BF)
        hg = mm_nt(og, wd)
        slope = phi + gate * (e * (1.0 / math.sqrt(2.0 * math.pi)))
        gg = (hg * up * slope).astype(BF)
        ug = (hg * act).astype(BF)
        down_part = mm(hidden, wd)
        back_part = mm_nt(gg, wg) + mm_nt(ug, wu)
        down = down_part if down is None else down + down_part
        back = back_part if back is None else back + back_part
    return down, back


def middle_kernel(per_plane, conv_ref, sm2_ref, start_ref, x_ref, og_ref, gain_ref, wo_ref, ga_ref, gb_ref, da_ref, db_ref,
                  gg_ref, mid_ref, out_ref, wo_own, wo_other, gain_out, third_ref, edge_ref, z0, z1, z2, z3, keep_ref):
    width = wo_ref.shape[0]
    blocks = wo_ref.shape[1] // width
    conv = conv_ref[...].astype(F32).T
    gated = sm2_ref[...] * conv
    gated_low = gated.astype(BF)
    branch = jnp.concatenate(
        [mm(gated_low[:, column(j, width)], wo_ref[:, column(j, width)]) for j in range(blocks)], axis=1
    )
    middle = own_part(x_ref, conv.shape[0]).astype(F32) + branch
    gain = gain_ref[...].reshape(1, -1)
    xhat, r = norm_stats(middle)
    normed = xhat * gain
    n2 = normed.astype(BF)
    og = og_ref[...]
    downs, backs = [], []
    for j in range(blocks):
        down, back = glu_block(
            n2[:, column(j, width)],
            og[:, column(j, width)],
            [(ga_ref[j, 0], ga_ref[j, 1]), (gb_ref[j, 0], gb_ref[j, 1])],
            [da_ref[:, column(j, width)], db_ref[:, column(j, width)]],
        )
        downs.append(down)
        backs.append(back)
    out_ref[...] = (middle + jnp.concatenate(downs, axis=1)).astype(BF)
    n2_grad = jnp.concatenate(backs, axis=1)
    mid_grad = og.astype(F32) + norm_backward(n2_grad, gain, xhat, r)
    mid_ref[...] = mid_grad
    bg = mid_grad.astype(BF)
    gated_grad = jnp.concatenate(
        [mm_nt(bg[:, column(j, width)], wo_ref[:, column(j, width)]) for j in range(blocks)], axis=1
    )
    gg_ref[...] = gated_grad.T.astype(BF)
    third = gated_grad * conv
    third_ref[...] = third
    edge_ref[:8, :] = third[:8]
    edge_ref[8:, :] = start_ref[...]
    gain_out[...] = jnp.sum(n2_grad * xhat, axis=0, keepdims=True).reshape(-1)
    weight = jnp.concatenate(
        [mm_tn(gated_low[:, column(j, width)], bg[:, column(j, width)]) for j in range(blocks)], axis=1
    )
    lanes = wo_own.shape[1]
    first = lax.axis_index("tp") == 0
    wo_own[...] = jnp.where(first, weight[:, :lanes], weight[:, lanes:]).astype(BF)
    wo_other[...] = jnp.where(first, weight[:, lanes:], weight[:, :lanes]).astype(BF)
    turned = normed.T.astype(BF)
    for j in range(blocks):
        keep_ref[j] = turned[column(j, width)]
    plane = lax.div(lax.axis_index("seq"), per_plane)
    for d, out in enumerate((z0, z1, z2, z3)):
        out[...] = keep_ref[lax.bitwise_xor(plane, d)]


def middle_part(conv, sm2, start, x, og, gain, wo, ga, gb, da, db, per_plane):
    rows, model = og.shape
    width = wo.shape[0]
    return pl.pallas_call(
        functools.partial(middle_kernel, per_plane),
        in_specs=vmem_specs(11),
        out_specs=vmem_specs(12),
        out_shape=[
            jax.ShapeDtypeStruct((model, rows), BF),
            jax.ShapeDtypeStruct((rows, model), F32),
            jax.ShapeDtypeStruct((rows, model), BF),
            jax.ShapeDtypeStruct((width, model // 2), BF),
            jax.ShapeDtypeStruct((width, model // 2), BF),
            jax.ShapeDtypeStruct((model,), F32),
            jax.ShapeDtypeStruct((rows, model), F32),
            jax.ShapeDtypeStruct((24, model), F32),
        ]
        + [jax.ShapeDtypeStruct((width, rows), BF)] * 4,
        scratch_shapes=[pltpu.VMEM((model // width, width, rows), BF)],
        compiler_params=params(),
        cost_estimate=cost(9 * 10**9, 6 * 10**6),
        name="middle_part",
    )(conv, sm2, start, x, og, gain, wo, ga, gb, da, db)


def glu_grad_kernel(per_plane, za, zb, zc, zd, oa, ob, oc, od, ga_ref, gb_ref, da_ref, db_ref, own_ref, other_ref):
    j = lax.div(lax.axis_index("seq"), per_plane)
    width = ga_ref.shape[2]
    xt = jnp.concatenate([ref[...] for ref in (za, zb, zc, zd)], axis=1)
    ot = jnp.concatenate([ref[width:, :] for ref in (oa, ob, oc, od)], axis=1)
    x = xt.astype(F32).T.astype(BF)
    og = ot.astype(F32).T.astype(BF)
    for g_ref, d_ref, out_ref in ((gb_ref, db_ref, other_ref), (ga_ref, da_ref, own_ref)):
        wg, wu = g_ref[j, 0], g_ref[j, 1]
        wd = d_ref[:, :width]
        for k in range(1, d_ref.shape[1] // width):
            wd = jnp.where(j == k, d_ref[:, column(k, width)], wd)
        gate = mm(x, wg)
        up = mm(x, wu)
        phi, e = erf_parts(gate)
        act = gate * phi
        hidden = (act * up).astype(BF)
        hg = mm_nt(og, wd)
        slope = phi + gate * (e * (1.0 / math.sqrt(2.0 * math.pi)))
        out_ref[0:width, :] = mm(xt, (hg * up * slope).astype(BF)).astype(out_ref.dtype)
        out_ref[width : 2 * width, :] = mm(xt, (hg * act).astype(BF)).astype(out_ref.dtype)
        out_ref[2 * width : 3 * width, :] = mm(ot, hidden).astype(out_ref.dtype)


def glu_grads(z_parts, o_parts, ga, gb, da, db, per_plane):
    width, half = ga.shape[2:]
    return pl.pallas_call(
        functools.partial(glu_grad_kernel, per_plane),
        in_specs=vmem_specs(12),
        out_specs=vmem_specs(2),
        out_shape=[
            jax.ShapeDtypeStruct((3 * width, half), F32),
            jax.ShapeDtypeStruct((3 * width, half), BF),
        ],
        compiler_params=params(40),
        cost_estimate=cost(9 * 10**9, 4 * 10**6),
        name="glu_grads",
    )(*z_parts, *o_parts, ga, gb, da, db)


def plane_add_kernel(own_ref, other_ref, mine_ref, theirs_ref, out_ref):
    total = (own_ref[...] + other_ref[...].astype(F32)).astype(BF)
    extra = (mine_ref[...].astype(F32) + theirs_ref[...].astype(F32)).astype(BF)
    count = out_ref.shape[0]
    rows, more = total.shape[0] // count, extra.shape[0] // count
    for k in range(count):
        out_ref[k, :rows, :] = total[k * rows : (k + 1) * rows]
        out_ref[k, rows:, :] = extra[k * more : (k + 1) * more]


def plane_add(own, other, mine, theirs, count):
    half = own.shape[1]
    rows = (own.shape[0] + mine.shape[0]) // count
    return pl.pallas_call(
        plane_add_kernel,
        in_specs=vmem_specs(4),
        out_specs=vmem_specs(1)[0],
        out_shape=jax.ShapeDtypeStruct((count, rows, half), BF),
        compiler_params=params(8),
        cost_estimate=cost(10**8, 2 * 10**6),
        name="plane_add",
    )(own, other, mine, theirs)


def plane_join_kernel(cut, a0, a1, a2, a3, out_ref):
    refs = (a0, a1, a2, a3)
    last = sum(ref[cut:, :].astype(F32) for ref in refs).astype(BF)
    if len(out_ref.shape) == 2:
        for z, ref in enumerate(refs):
            out_ref[z * cut : (z + 1) * cut, :] = ref[:cut, :]
        out_ref[4 * cut :, :] = last
        return
    for k in range(out_ref.shape[0]):
        for z, ref in enumerate(refs):
            out_ref[k, z * cut : (z + 1) * cut, :] = ref[:cut, :]
        out_ref[k, 4 * cut :, :] = last


def plane_join(parts, cut, copies=()):
    rows, half = parts[0].shape
    return pl.pallas_call(
        functools.partial(plane_join_kernel, cut),
        in_specs=vmem_specs(4),
        out_specs=vmem_specs(1)[0],
        out_shape=jax.ShapeDtypeStruct((*copies, 3 * cut + rows, half), BF),
        compiler_params=params(8),
        cost_estimate=cost(10**8, 2 * 10**6),
        name="plane_join",
    )(*parts)


def plane_sum_kernel(x_ref, out_ref):
    out_ref[...] = sum(x_ref[k].astype(F32) for k in range(x_ref.shape[0])).astype(BF)


def plane_sum(parts):
    return pl.pallas_call(
        plane_sum_kernel,
        in_specs=vmem_specs(1),
        out_specs=vmem_specs(1)[0],
        out_shape=jax.ShapeDtypeStruct(parts.shape[1:], BF),
        compiler_params=params(8),
        cost_estimate=cost(8 * 10**11, 2 * 10**6),
        name="plane_sum",
    )(parts)


def finish_kernel(per_plane, width, a_ref, half_ref, back_ref,
                  gi_ref, go_ref, in_ref, keep_ref):
    seq = lax.axis_index("seq")
    plane = lax.div(seq, per_plane)
    blocks, pieces, cut, half = keep_ref.shape
    for k in range(pieces):
        for z in range(blocks):
            keep_ref[lax.bitwise_xor(plane, z), k] = a_ref[k, z * cut : (z + 1) * cut, :].astype(F32)
    outs = []
    for j in range(blocks):
        block = jnp.concatenate([keep_ref[j, k] for k in range(pieces)], axis=0)
        gi_ref[j, :, 0, :] = block[:width]
        gi_ref[j, :, 1, :] = block[width : 2 * width]
        outs.append(block[2 * width : 3 * width].T)
    go_ref[...] = jnp.concatenate(outs, axis=1)
    count = half_ref.shape[0]
    me = lax.axis_index("tp")
    in_ref[pl.ds(pl.multiple_of(me * count, count), count), :] = half_ref[...]
    in_ref[pl.ds(pl.multiple_of((1 - me) * count, count), count), :] = back_ref[...]


def finish(sums, half_rows, other_rows, per_plane, width):
    half = sums.shape[2]
    model = 4 * width
    return pl.pallas_call(
        functools.partial(finish_kernel, per_plane, width),
        in_specs=vmem_specs(3),
        out_specs=vmem_specs(3),
        out_shape=[
            jax.ShapeDtypeStruct((4, width, 2, half), F32),
            jax.ShapeDtypeStruct((half, model), F32),
            jax.ShapeDtypeStruct((2 * half_rows.shape[0], model), BF),
        ],
        scratch_shapes=[pltpu.VMEM((4, 4, 3 * width // 4, half), F32)],
        compiler_params=params(32),
        cost_estimate=cost(10**8, 6 * 10**6),
        name="finish",
    )(sums, half_rows, other_rows)


def out_unpack_kernel(mine_ref, theirs_ref, wo_ref):
    first = lax.axis_index("tp") == 0
    mine, theirs = mine_ref[...].astype(F32), theirs_ref[...].astype(F32)
    left, right = jnp.where(first, mine, theirs), jnp.where(first, theirs, mine)
    _, cut, lanes = left.shape
    for k in range(left.shape[0]):
        wo_ref[k * cut : (k + 1) * cut, :lanes] = left[k]
        wo_ref[k * cut : (k + 1) * cut, lanes:] = right[k]


def out_unpack(mine, theirs):
    count, rows, lanes = mine.shape
    return pl.pallas_call(
        out_unpack_kernel,
        in_specs=vmem_specs(2),
        out_specs=vmem_specs(1)[0],
        out_shape=jax.ShapeDtypeStruct((count * rows, 2 * lanes), F32),
        compiler_params=params(8),
        cost_estimate=cost(10**8, 10**6),
        name="out_unpack",
    )(mine, theirs)


def in_unpack_kernel(place, w_ref, gain_ref, *refs):
    tiles, (gi_ref, st_ref, gain_out, w1_ref, b1_ref, w2_ref, gain2_ref, keep_ref) = refs[:-8], refs[-8:]
    _, width, model = gi_ref.shape
    count, rows3, _ = keep_ref.shape
    small = None
    for k, ref in enumerate(tiles):
        half, z = divmod(k, 4)
        for inner in range(4):
            keep_ref[source_of(place, (half, inner), z)] = ref[inner * rows3 : (inner + 1) * rows3, :].astype(F32)
        part = ref[4 * rows3 :, :].astype(F32)
        small = part if small is None else small + part
    hidden = w2_ref.shape[0]
    more = small.shape[0]
    w2_ref[:more, :] = small[:, :LANES]
    w2_ref[more:, :] = small[: hidden - more, LANES:]
    rest = small[hidden - more : hidden - more + 8, LANES:]
    w1_ref[...] = rest[:5]
    b1_ref[...] = rest[5:6].reshape(-1)
    rest = small[hidden - more + 8 :, LANES:]
    for k in range(model // LANES):
        gain2_ref[k * LANES : (k + 1) * LANES] = rest[k : k + 1].reshape(-1)
    chans = rows3 // 3
    blocks = model // width
    per_block = count // blocks
    gains = []
    for j in range(blocks):
        acc = None
        for p in range(3):
            got = jnp.concatenate(
                [keep_ref[j * per_block + k, p * chans : (p + 1) * chans, :] for k in range(per_block)], axis=0
            )
            turned = got.T
            gi_ref[p, :, column(j, width)] = turned[:width]
            for k in range(3):
                st_ref[k, p : p + 1, column(j, width)] = turned[width + k : width + k + 1]
            part = turned[:width] * w_ref[p, :, column(j, width)].astype(F32)
            acc = part if acc is None else acc + part
        gains.append(jnp.sum(acc.T, axis=0, keepdims=True))
    gain_out[...] = (jnp.concatenate(gains, axis=1) / gain_ref[...].reshape(1, -1)).reshape(-1)


def in_unpack(tiles, place, w, gain):
    rows3 = (tiles[0].shape[0] - SMALL_ROWS) // 4
    hidden = LANES
    count = 4 * len(tiles)
    _, width, model = w.shape
    return pl.pallas_call(
        functools.partial(in_unpack_kernel, place),
        in_specs=vmem_specs(2 + len(tiles)),
        out_specs=vmem_specs(7),
        out_shape=[
            jax.ShapeDtypeStruct((3, width, model), F32),
            jax.ShapeDtypeStruct((3, 3, model), F32),
            jax.ShapeDtypeStruct((model,), F32),
            jax.ShapeDtypeStruct((5, hidden), F32),
            jax.ShapeDtypeStruct((hidden,), F32),
            jax.ShapeDtypeStruct((hidden, hidden), F32),
            jax.ShapeDtypeStruct((model,), F32),
        ],
        scratch_shapes=[pltpu.VMEM((count, rows3, 2 * LANES), F32)],
        compiler_params=params(24),
        cost_estimate=cost(10**8, 4 * 10**6),
        name="in_unpack",
    )(w, gain, *tiles)


def short_mix(proj_ref, taps_ref, p, rows):
    lead = proj_ref.shape[1] - rows
    proj = proj_ref[p].astype(F32)
    return (
        taps_ref[0, p : p + 1, :] * proj[lead:]
        + taps_ref[1, p : p + 1, :] * proj[lead - 1 : lead - 1 + rows]
        + taps_ref[2, p : p + 1, :] * proj[lead - 2 : lead - 2 + rows]
    )


def mixer_back_kernel(chans, seq_length, *refs):
    *grad_refs, third_ref, edge_ref, proj_ref, taps_ref, mid_ref, x_ref, gain_ref, w_ref, in_ref = refs
    rows, model = mid_ref.shape
    width = w_ref.shape[1]
    blocks = model // width
    if len(grad_refs) == 1:
        got = grad_refs[0][...].astype(F32)
        count = got.shape[0]
        main = got[:, :chans, :].reshape(count * chans, rows)
        tiles = []
        for k in range(count):
            tile = got[k, chans:, :]
            for a in range(chans // GROUP):
                tiles.append(pltpu.roll(tile, LANES - 2 * a, 1) if a else tile)
        tail = jnp.concatenate(tiles, axis=0)
    else:
        main, tail = grad_refs[0][...].astype(F32), grad_refs[1][...].astype(F32)
    back = jnp.concatenate([main.T, tail.T[:8]], axis=0)
    linear = lax.axis_index("seq") * 2 + lax.axis_index("tp")
    keep = jnp.where(lax.rem((linear + 1) * rows, seq_length) == 0, 0.0, 1.0)
    third = jnp.concatenate([third_ref[...], edge_ref[:8, :] * keep], axis=0)
    mixed = [
        jnp.concatenate([short_mix(proj_ref, taps_ref, p, rows), edge_ref[8 * p + 8 : 8 * p + 16, :]], axis=0)
        for p in range(2)
    ]
    total = [None] * blocks
    for p, sg in enumerate((back * mixed[1], back * mixed[0], third)):
        pg = (
            taps_ref[0, p : p + 1, :] * sg[:rows]
            + taps_ref[1, p : p + 1, :] * sg[1 : rows + 1]
            + taps_ref[2, p : p + 1, :] * sg[2 : rows + 2]
        ).astype(BF)
        for j in range(blocks):
            part = mm_nt(pg[:, column(j, width)], w_ref[p, :, column(j, width)])
            total[j] = part if total[j] is None else total[j] + part
    n1_grad = jnp.concatenate(total, axis=1)
    xhat, r = norm_stats(own_part(x_ref, rows).astype(F32))
    in_ref[...] = (mid_ref[...] + norm_backward(n1_grad, gain_ref[...].reshape(1, -1), xhat, r)).astype(BF)


def mixer_back(grads, third, edge, proj, taps, mid, x, gain, w, chans, seq_length):
    return pl.pallas_call(
        functools.partial(mixer_back_kernel, chans, seq_length),
        in_specs=vmem_specs(8 + len(grads)),
        out_specs=vmem_specs(1)[0],
        out_shape=jax.ShapeDtypeStruct(mid.shape, BF),
        compiler_params=params(BACK_MIB),
        cost_estimate=cost(3 * 10**9, 4 * 10**6),
        name="mixer_back",
    )(*grads, third, edge, proj, taps, mid, x, gain, w)


def after(x, *others):
    return lax.optimization_barrier((x,) + others)[0]


def permuted(x, axes, count, by):
    pairs = [(i, i + by) for i in range(count) if 0 <= i + by < count]
    return lax.ppermute(x, axes, pairs)


def swapped(x):
    return lax.ppermute(x, "tp", [(0, 1), (1, 0)])


def crossed(x, mask):
    devices = lax.axis_size("seq")
    return lax.ppermute(x, "seq", [(i, i ^ mask) for i in range(devices)])


def exchanged(x, axes, groups=None):
    return lax.all_to_all(x, axes, 0, 0, axis_index_groups=groups, tiled=True)


def gathered_over(x, count, groups=None):
    return exchanged(jnp.broadcast_to(x[None], (count,) + x.shape), "seq", groups)


def local(
    layer_input,
    mixer_gain,
    in_proj,
    short_taps,
    filter_w1,
    filter_b1,
    filter_w2,
    filter_w3,
    filter_decay,
    out_proj,
    glu_gain,
    glu_in,
    glu_out,
    out_grad,
):
    tok_rows, model = layer_input.shape
    width = in_proj.shape[0]
    blocks = model // width
    half = glu_out.shape[0]
    seq_devices = lax.axis_size("seq")
    tp_devices = lax.axis_size("tp")
    devices = seq_devices * tp_devices
    both = ("seq", "tp")
    rows = tok_rows // tp_devices
    seq_length = min(MIN_LEN, tok_rows * seq_devices)
    seqs = tok_rows * seq_devices // seq_length
    per_plane = seq_devices // blocks
    quick = per_plane == 4 and not SLOW_PATH
    place = (per_plane, quick)
    chans = model // devices
    chans_padded = -(-chans // GROUP) * GROUP
    spare = chans_padded - chans
    hidden = filter_w2.shape[0]
    tp_index = lax.axis_index("tp")
    linear = lax.axis_index("seq") * tp_devices + tp_index
    tables = transform_tables(seq_length)
    features = feature_table(seq_length)
    within = [[g * per_plane + r for r in range(per_plane)] for g in range(blocks)]

    halo = permuted(layer_input[tok_rows - 16 :], "seq", seq_devices, 1)

    w3t = filter_w3.T.reshape(tp_devices, chans, hidden)
    w3t = jnp.pad(w3t, ((0, 0), (0, spare), (0, 0))).reshape(tp_devices * chans_padded, hidden)
    decay = jnp.pad(filter_decay.reshape(tp_devices, chans), ((0, 0), (0, spare))).reshape(-1)
    lag_own, lag_other, *saved = filter_forward(features, filter_w1, filter_b1, filter_w2, w3t, decay)
    lag_back = swapped(lag_other)

    w_in = in_proj.transpose(1, 0, 2)
    conv_rows, sm2, proj_rows, start_rows, *sent = mixer_in(
        layer_input, after(halo, lag_own), mixer_gain, w_in, short_taps, out_grad, per_plane, seq_length
    )

    def to_channels(x):
        out = exchanged(x.reshape(devices, chans, rows), both)
        return jnp.pad(out, ((0, 0), (0, spare), (0, 0)))

    def to_tokens(x):
        return exchanged(x[:, :chans], both).reshape(model, rows)

    conv_channels = to_channels(conv_rows)
    early = [sent[0]] + [crossed(sent[d], d * per_plane) for d in range(1, blocks)]
    glu_own = after(glu_in, conv_rows).transpose(0, 2, 1, 3)
    down_own = after(glu_out, conv_rows)
    glu_other = swapped(glu_own)
    down_other = swapped(down_own)
    spectrum = filter_spectrum(after(lag_own, glu_own), lag_back, tables)
    conv_out, signal_spec = conv_forward(after(conv_channels, spectrum), spectrum, tables, seqs)
    conv_tokens = to_tokens(conv_out)

    early = [after(x, conv_out) for x in early]
    rows_in = jnp.stack([x[:width] for x in early])
    if quick:
        plane_tiles = [rows_in] + [crossed(rows_in, d) for d in range(1, per_plane)]
        turns = [[(0, d)] for d in range(per_plane)]
    else:
        plane_tiles = [gathered_over(rows_in, per_plane, within).reshape(per_plane * blocks, width, rows)]
        turns = [[(0, r) for r in range(per_plane)]]
    gated_grad, mid, layer_output, extra, extra_other, gain_sum, third, edge, *sent = middle_part(
        conv_tokens, sm2, start_rows, layer_input, out_grad, glu_gain, out_proj, glu_own, glu_other,
        down_own, down_other, per_plane
    )
    gated_channels = to_channels(gated_grad)
    across = lambda parts: [parts[0]] + [crossed(parts[d], d * per_plane) for d in range(1, blocks)]
    late = across(sent)
    extra_back = swapped(extra_other)
    edge = permuted(edge, both, devices, -1)
    plane_tiles = [after(x, gated_grad) for x in plane_tiles]
    tiles = plane_tiles + [swapped(x) for x in plane_tiles]
    turns = turns + [[(1, r) for _, r in t] for t in turns]
    turns = tuple(tuple(t) for t in turns)
    proj_channels, mixed_channels = channel_mixer(tiles, turns, place, w_in, short_taps, devices, seqs, chans)

    late = [after(x, proj_channels, gated_channels) for x in late]
    g_own, g_other = glu_grads(late, early, glu_own, glu_other, down_own, down_other, per_plane)
    g_back = swapped(g_other)
    if quick:
        to_sum = plane_add(g_own, g_back, extra, extra_back, per_plane)
        sums = exchanged(to_sum, "seq", within)
        gated_channels = after(gated_channels, to_sum)

    pg, cross, tap_sums, icg = conv_backward(
        after(gated_channels, g_own), mixed_channels, proj_channels, conv_out, signal_spec, short_taps, spectrum, tables,
        seqs, chans
    )
    icg_tokens = exchanged(after(icg, sums) if quick else icg, both)

    if quick:
        glu_piece = plane_sum(after(sums, pg))
        glu_parts = across([glu_piece] * blocks)
        tap_sums = after(tap_sums, glu_piece)
    cross_back = swapped(cross)
    in_piece, g3 = channel_grads(
        tiles, turns, place, pg, tap_sums, cross, cross_back, tables, features, filter_w2, w3t, decay, gain_sum, saved
    )
    g3_back = swapped(g3)
    if quick:
        in_parts = [in_piece] + [crossed(in_piece, d) for d in range(1, per_plane)]
        glu_parts = plane_join([after(x, in_piece) for x in glu_parts], 3 * width // per_plane, (per_plane,))
        icg_tokens = after(icg_tokens, glu_parts)
    if chans == chans_padded:
        grads = [icg_tokens]
    else:
        grads = [
            icg_tokens[:, :chans].reshape(model, rows),
            icg_tokens[:, chans_padded : chans_padded + chans].reshape(model, rows),
        ]
    input_half = mixer_back(
        grads, third, edge, proj_rows, short_taps, mid, layer_input, mixer_gain, w_in, chans, seq_length
    )
    input_other = swapped(input_half)

    if quick:
        in_parts = plane_join([after(x, input_half) for x in in_parts], 3 * chans_padded)
        in_full = across([in_parts] * blocks)
        glu_full = exchanged(after(glu_parts, in_parts), "seq", within)
        in_full = in_full + [swapped(x) for x in in_full]
        in_proj_grad, short_taps_grad, mixer_gain_grad, w1_grad, b1_grad, w2_grad, glu_gain_grad = in_unpack(
            in_full, place, w_in, mixer_gain
        )
        glu_full = after(glu_full, glu_gain_grad)
        out_mine = glu_full[:, 3 * width :, :]
        out_theirs = swapped(out_mine)
        glu_in_grad, glu_out_grad, input_grad = finish(
            after(glu_full, out_mine), input_half, input_other, per_plane, width
        )
        out_proj_grad = out_unpack(out_mine, after(out_theirs, glu_out_grad))
        in_proj_grad = in_proj_grad.transpose(1, 0, 2)
    else:
        total = (g_own + g_back.astype(F32)).astype(BF)
        piece = exchanged(total, "seq", within).reshape(per_plane, -1, half)
        piece = jnp.sum(piece.astype(F32), axis=0).astype(BF)
        full = gathered_over(piece, seq_devices).reshape(blocks, -1, half).astype(F32)
        glu_in_grad = full[:, : 2 * width].reshape(blocks, 2, width, half).transpose(0, 2, 1, 3)
        glu_out_grad = full[:, 2 * width :].transpose(2, 0, 1).reshape(half, model)
        total = (extra.astype(F32) + extra_back.astype(F32)).astype(BF)
        piece = exchanged(total.reshape(seq_devices, -1), "seq")
        piece = jnp.sum(piece.astype(F32), axis=0).astype(BF)
        mine = gathered_over(piece, seq_devices).reshape(width, model // 2).astype(F32)
        theirs = swapped(mine)
        out_proj_grad = jnp.where(
            tp_index == 0, jnp.concatenate([mine, theirs], axis=1), jnp.concatenate([theirs, mine], axis=1)
        )
        mine = gathered_over(in_piece, seq_devices)
        theirs = swapped(mine)
        pair = jnp.where(tp_index == 0, jnp.stack([mine, theirs], 1), jnp.stack([theirs, mine], 1)).astype(F32)
        pair = pair.reshape(devices, -1, 2 * LANES)
        small = jnp.sum(pair[:, 3 * chans_padded :], axis=0)
        small = jnp.concatenate([small[:, :LANES], small[:, LANES:]], axis=0)
        w1_grad, b1_grad, w2_grad = small[hidden : hidden + 5], small[hidden + 5], small[:hidden]
        glu_gain_grad = small[hidden + 8 : hidden + 8 + model // LANES].reshape(model)
        pair = pair[:, : 3 * chans_padded].reshape(devices, 3, chans_padded, 2 * LANES)[:, :, :chans]
        pair = pair.transpose(1, 0, 2, 3).reshape(3, model, 2 * LANES)
        in_proj_grad = pair[:, :, :width].transpose(2, 0, 1)
        short_taps_grad = pair[:, :, width : width + 3].transpose(2, 0, 1)
        products = in_proj_grad * in_proj.astype(F32)
        products = jnp.sum(products.reshape(width, 3, blocks, width), axis=(1, 3))
        mixer_gain_grad = products.T.reshape(model) / mixer_gain
        input_grad = jnp.where(
            tp_index == 0,
            jnp.concatenate([input_half, input_other], axis=0),
            jnp.concatenate([input_other, input_half], axis=0),
        )

    mine = g3[:chans] + g3_back[chans_padded : chans_padded + chans]
    theirs = g3[chans_padded : chans_padded + chans] + g3_back[:chans]
    g3_full = jnp.where(
        tp_index == 0, jnp.concatenate([mine, theirs], axis=0), jnp.concatenate([theirs, mine], axis=0)
    ).T
    return (
        layer_output,
        input_grad,
        mixer_gain_grad,
        in_proj_grad,
        short_taps_grad,
        w1_grad,
        b1_grad,
        w2_grad,
        g3_full,
        out_proj_grad,
        glu_gain_grad,
        glu_in_grad,
        glu_out_grad,
    )


def solution(mesh):
    placed = (
        P("seq", None),
        P(),
        P(),
        P(),
        P(),
        P(),
        P(),
        P(None, "seq"),
        P("seq"),
        P(),
        P(),
        P(None, None, None, "tp"),
        P("tp", None),
        P(("seq", "tp"), None),
    )
    return jax.shard_map(
        local,
        mesh=mesh,
        in_specs=placed,
        out_specs=(
            P(("seq", "tp"), None),
            P("seq", None),
            P(),
            P(),
            P(),
            P(),
            P(),
            P(),
            P(None, "seq"),
            P(),
            P(),
            P(None, None, None, "tp"),
            P("tp", None),
        ),
        check_vma=False,
    )
```

```python
import math
import functools

import jax
import jax.numpy as jnp
import ml_dtypes
import numpy as np
from jax import lax
from jax.experimental import pallas as pl
from jax.experimental.pallas import tpu as pltpu
from jax.sharding import PartitionSpec as P

MIN_LEN = 8192
SLOW_PATH = False
EPSILON = 1e-05
LANES = 128
GROUP = 8
FILTER_LANES = 4096
SMALL_ROWS = 72
BACK_MIB = 24
BF = jnp.bfloat16
F32 = jnp.float32

PI_HIGH = 3.140625
ROUNDER = 12582912.0
PI_LOW = 9.67653589793e-4
SIN_C = (1.0, -0.16666647791862488, 0.00833289884030819, -0.0001980081869987771, 2.590327312645968e-06)
COS_C = (0.9999999403953552, -0.4999990463256836, 0.041663575917482376, -0.0013853635173290968, 2.315232813998591e-05)


def vmem_specs(count):
    return [pl.BlockSpec(memory_space=pltpu.VMEM)] * count


def params(mib=60):
    return pltpu.CompilerParams(vmem_limit_bytes=mib * 1024 * 1024)


def cost(flops, bytes_accessed=0, transcendentals=0):
    return pl.CostEstimate(flops=flops // 20, bytes_accessed=bytes_accessed // 20, transcendentals=0)


def split_np(table):
    high = np.asarray(table, np.float32).astype(ml_dtypes.bfloat16)
    low = (np.asarray(table, np.float64) - high.astype(np.float64)).astype(ml_dtypes.bfloat16)
    return high, low


def split3_np(table):
    table = np.asarray(table, np.float64)
    high = table.astype(np.float32).astype(ml_dtypes.bfloat16)
    rest = table - high.astype(np.float64)
    mid = rest.astype(np.float32).astype(ml_dtypes.bfloat16)
    low = (rest - mid.astype(np.float64)).astype(np.float32).astype(ml_dtypes.bfloat16)
    return high, mid, low


@functools.lru_cache(maxsize=None)
def transform_tables(seq_length):
    period = 2 * seq_length
    first = period // LANES
    kept = first // 2 + 1
    padded = -(-kept // 8) * 8
    k = np.arange(padded)
    live = (k < kept).astype(np.float64)
    n = np.arange(first)
    angle = 2 * np.pi / first * ((k[:, None] * n[None, :]) % first)
    eye = np.eye(GROUP)
    stage = np.zeros((GROUP, 2, padded, first, GROUP))
    stage[:, 0] = np.einsum("kn,cd->cknd", np.cos(angle) * live[:, None], eye)
    stage[:, 1] = np.einsum("kn,cd->cknd", -np.sin(angle) * live[:, None], eye)
    forward = stage.reshape(GROUP * 2 * padded, first * GROUP)
    backward = forward.T
    m = np.arange(LANES)
    turn = 2 * np.pi / period * ((k[:, None] * m[None, :]) % period)
    weight = np.where((k == 0) | (k == first // 2), 1.0, 2.0) * live / period
    twiddle = np.stack(
        [np.cos(turn), np.sin(turn), np.cos(turn) * weight[:, None], np.sin(turn) * weight[:, None]]
    ).astype(np.float32)
    inner = 2 * np.pi / LANES * ((m[:, None] * m[None, :]) % LANES)
    c, s = np.cos(inner), np.sin(inner)
    second = np.block([[c, -s], [s, c]])
    return {
        "forward": split_np(forward),
        "backward": split_np(backward),
        "forward_used": split_np(forward[:, : first // 2 * GROUP]),
        "backward_used": split_np(backward[: first // 2 * GROUP]),
        "twiddle": twiddle,
        "second": split_np(second),
        "inverse": split_np(second.T),
        "first": first,
        "padded": padded,
    }


@functools.lru_cache(maxsize=None)
def feature_table(seq_length):
    period = 2 * seq_length
    index = np.arange(period)
    lag = np.where(index < seq_length, index, index - period)
    q = lag / seq_length
    rows = [q, np.cos(2 * np.pi * q), np.cos(4 * np.pi * q), np.sin(2 * np.pi * q), np.sin(4 * np.pi * q)]
    rows.append(np.ones_like(q))
    rows += [np.zeros_like(q)] * 2
    high, mid, low = split3_np(np.stack(rows))
    return np.concatenate([high, high, mid, high, mid, low], axis=0)


def split(values):
    high = values.astype(BF)
    low = (values - high.astype(F32)).astype(BF)
    return high, low


def first_weights(w1_ref, b1_ref):
    hidden = w1_ref.shape[1]
    rows = jnp.concatenate([w1_ref[...], b1_ref[...].reshape(1, hidden), jnp.zeros((2, hidden), F32)], axis=0)
    high = rows.astype(BF).astype(F32)
    mid = (rows - high).astype(BF).astype(F32)
    low = rows - high - mid
    return jnp.concatenate([high, mid, high, low, mid, high], axis=0).astype(BF)


def mm(a, b):
    return jnp.dot(a, b, preferred_element_type=F32)


def mm_nt(a, b):
    return lax.dot_general(a, b, (((1,), (1,)), ((), ())), preferred_element_type=F32)


def mm_tn(a, b):
    return lax.dot_general(a, b, (((0,), (0,)), ((), ())), preferred_element_type=F32)


def mm3(a, b):
    ah, al = a
    bh, bl = b
    return mm(ah, bh) + (mm(al, bh) + mm(ah, bl))


def mm3_tn(a, b):
    ah, al = a
    bh, bl = b
    return mm_tn(ah, bh) + (mm_tn(al, bh) + mm_tn(ah, bl))


def sine_cosine(x):
    n = (x * (0.5 / math.pi) + ROUNDER) - ROUNDER
    t = (x * 0.5 - n * PI_HIGH) - n * PI_LOW
    t2 = t * t
    s = SIN_C[4]
    for c in SIN_C[3::-1]:
        s = s * t2 + c
    s = s * t
    k = COS_C[4]
    for c in COS_C[3::-1]:
        k = k * t2 + c
    twice = s + s
    return twice * k, 1.0 - twice * s


def lag_decay(decay, start, width, seq_length):
    lane = lax.broadcasted_iota(jnp.int32, decay.shape[:1] + (width,), 1) + start
    lag = jnp.where(lane < seq_length, lane, 2 * seq_length - lane).astype(F32)
    return jnp.exp(lag * (decay[:, :1] * (-1.0 / seq_length)))


def stacked_weights(w):
    high, low = split(w)
    zero = jnp.zeros_like(high)
    return jnp.concatenate(
        [jnp.concatenate([high, high], axis=1), jnp.concatenate([low, zero], axis=1)], axis=0
    )


def stacked_product(weights, values):
    out = mm(weights, jnp.concatenate(split(values), axis=0))
    rows = out.shape[0] // 2
    return out[:rows] + out[rows:]


def decay_columns(ref):
    row = jnp.broadcast_to(ref[...].reshape(1, -1), (LANES, ref.shape[0]))
    rows = row.T
    half = ref.shape[0] // 2
    a, b = rows[:half], rows[half:]
    first = lax.axis_index("tp") == 0
    return jnp.concatenate([jnp.where(first, a, b), jnp.where(first, b, a)], axis=0)


def own_first(ref):
    half = ref.shape[0] // 2
    me = lax.axis_index("tp")
    return jnp.concatenate([ref[pl.ds(me * half, half), :], ref[pl.ds((1 - me) * half, half), :]], axis=0)


def filter_forward_kernel(feat_ref, w1_ref, b1_ref, w2_ref, w3_ref, decay_ref, own_ref, other_ref, a_ref, ac_ref, b_ref, bc_ref):
    length = own_ref.shape[1]
    channels = own_ref.shape[0]
    width = min(FILTER_LANES, length)
    begin = lax.axis_index("tp") * length
    w1 = first_weights(w1_ref, b1_ref)
    w2 = stacked_weights(w2_ref[...].T)
    w3 = stacked_weights(own_first(w3_ref))
    decay = decay_columns(decay_ref)
    for lo in range(0, length, width):
        lanes = slice(lo, lo + width)
        start = pl.multiple_of(begin + lo, LANES)
        s1, c1 = sine_cosine(mm_tn(w1, feat_ref[:, pl.ds(start, width)]))
        a_ref[:, lanes] = s1.astype(BF)
        ac_ref[:, lanes] = c1.astype(BF)
        s2, c2 = sine_cosine(stacked_product(w2, s1))
        b_ref[:, lanes] = s2.astype(BF)
        bc_ref[:, lanes] = c2.astype(BF)
        lag = stacked_product(w3, s2) * lag_decay(decay, start, width, length)
        own_ref[:, lanes] = lag[:channels]
        other_ref[:, lanes] = lag[channels:]


def filter_forward(features, w1, b1, w2, w3t, decay):
    hidden = w2.shape[0]
    channels = w3t.shape[0] // 2
    length = features.shape[1] // 2
    return pl.pallas_call(
        filter_forward_kernel,
        in_specs=vmem_specs(6),
        out_specs=vmem_specs(6),
        out_shape=[jax.ShapeDtypeStruct((channels, length), F32)] * 2
        + [jax.ShapeDtypeStruct((hidden, length), BF)] * 4,
        compiler_params=params(),
        cost_estimate=cost(8 * 10**9, 8 * 10**6),
        name="filter_forward",
    )(features, w1, b1, w2, w3t, decay)


def inner_spectrum(a, twiddle_ref, second, padded, columns):
    tc, ts = twiddle_ref[0], twiddle_ref[1]
    parts = []
    for col in range(columns):
        lanes = slice(col * LANES, (col + 1) * LANES)
        for c in range(GROUP):
            base = c * 2 * padded
            re = a[base : base + padded, lanes]
            im = a[base + padded : base + 2 * padded, lanes]
            parts.append(jnp.concatenate([re * tc + im * ts, im * tc - re * ts], axis=1))
    return mm3(split(jnp.concatenate(parts, axis=0)), second)


def signal_of(spec, inverse, twiddle_ref, back, padded, columns):
    b = mm3(split(spec), inverse)
    tc, ts = twiddle_ref[2], twiddle_ref[3]
    cols = []
    for col in range(columns):
        parts = []
        for c in range(GROUP):
            base = (col * GROUP + c) * padded
            re = b[base : base + padded, :LANES]
            im = b[base : base + padded, LANES:]
            parts.append(re * tc - im * ts)
            parts.append(im * tc + re * ts)
        cols.append(jnp.concatenate(parts, axis=0))
    z = split(jnp.concatenate(cols, axis=1))
    return [mm3(rows, z) for rows in back]


def gathered(x, seqs, rows, groups):
    cols = []
    for q in range(seqs):
        for g in range(groups):
            block = x[q * rows : (q + 1) * rows, g * GROUP : (g + 1) * GROUP, :]
            cols.append(block.reshape(rows * GROUP, LANES))
    return jnp.concatenate(cols, axis=1)


def scattered(y, seqs, rows, groups):
    out = []
    for q in range(seqs):
        cols = [
            y[:, (q * groups + g) * LANES : (q * groups + g + 1) * LANES].reshape(rows, GROUP, LANES)
            for g in range(groups)
        ]
        out.append(jnp.concatenate(cols, axis=1))
    return jnp.concatenate(out, axis=0)


def product(a, b, conjugate):
    ar, ai = a[:, :LANES], a[:, LANES:]
    br, bi = b[:, :LANES], b[:, LANES:]
    if conjugate:
        return jnp.concatenate([ar * br + ai * bi, ai * br - ar * bi], axis=1)
    return jnp.concatenate([ar * br - ai * bi, ar * bi + ai * br], axis=1)


def filter_spectrum_kernel(padded, own_ref, other_ref, fh, fl, tw, sh, sl, out_ref):
    groups = own_ref.shape[0] // GROUP
    rows = own_ref.shape[1] // LANES
    used = rows * GROUP
    me = lax.axis_index("tp")
    total = None
    for lag_ref, half in ((own_ref, me), (other_ref, 1 - me)):
        cols = []
        for g in range(groups):
            tiles = [lag_ref[g * GROUP : (g + 1) * GROUP, n * LANES : (n + 1) * LANES] for n in range(rows)]
            cols.append(jnp.concatenate(tiles, axis=0))
        begin = pl.multiple_of(half * used, LANES)
        table = (fh[:, pl.ds(begin, used)], fl[:, pl.ds(begin, used)])
        part = mm3(table, split(jnp.concatenate(cols, axis=1)))
        total = part if total is None else total + part
    out_ref[...] = inner_spectrum(total, tw, (sh[...], sl[...]), padded, groups)


def signal_spectrum(x, seqs, fh, fl, tw, sh, sl, padded):
    rows = x.shape[0] // seqs
    groups = x.shape[1] // GROUP
    used = rows * GROUP
    flat = gathered(x, seqs, rows, groups).astype(BF)
    a = mm(fh[:, :used], flat) + mm(fl[:, :used], flat)
    return inner_spectrum(a, tw, (sh[...], sl[...]), padded, seqs * groups)


def filtered(spec, h_ref, seqs, conjugate, tw, ih, il, bh, bl, padded, shape):
    rows = shape[0] // seqs
    groups = shape[1] // GROUP
    used = rows * GROUP
    prod = product(spec, jnp.concatenate([h_ref[...]] * seqs, axis=0), conjugate)
    (y,) = signal_of(prod, (ih[...], il[...]), tw, [(bh[:used, :], bl[:used, :])], padded, seqs * groups)
    return scattered(y, seqs, rows, groups)


def conv_forward_kernel(padded, seqs, x_ref, h_ref, fh, fl, tw, sh, sl, ih, il, bh, bl, y_ref, spec_ref):
    x = x_ref[...].astype(F32)
    spec = signal_spectrum(x, seqs, fh, fl, tw, sh, sl, padded)
    spec_ref[...] = spec
    y_ref[...] = filtered(spec, h_ref, seqs, False, tw, ih, il, bh, bl, padded, x.shape).astype(BF)


def conv_backward_kernel(padded, seqs, real, g_ref, sm_ref, p_ref, y_ref, saved_ref, taps_ref, h_ref, fh, fl, tw, sh, sl, ih, il, bh, bl,
                         pg_ref, cross_ref, st_ref, sent_ref, icg_ref):
    count, chans, _ = g_ref.shape
    gated = g_ref[...].astype(F32)
    conv_grad = gated * sm_ref[:, 2 * chans :, :]
    spec = signal_spectrum(conv_grad, seqs, fh, fl, tw, sh, sl, padded)
    cross = product(spec, saved_ref[...], True)
    height = cross_ref.shape[0]
    cross_ref[...] = sum(cross[q * height : (q + 1) * height] for q in range(seqs))
    icg = filtered(spec, h_ref, seqs, True, tw, ih, il, bh, bl, padded, g_ref.shape)
    icg_ref[...] = icg.astype(BF).astype(F32)
    per_seq = count // seqs
    taps = tap_columns(taps_ref, real)
    lane = lax.broadcasted_iota(jnp.int32, (3 * chans, LANES), 1)
    first_lanes = lane[:GROUP]

    def edge_of(back):
        out = jnp.zeros((GROUP, LANES), F32)
        for a in range(chans // GROUP):
            rows = back[a * GROUP : (a + 1) * GROUP]
            rows = pltpu.roll(rows, 2 * a, 1) if a else rows
            out = jnp.where((first_lanes >= 2 * a) & (first_lanes < 2 * a + 2), rows, out)
        return out

    def step(i, carry):
        next1, next2, acc0, acc1, acc2, next_edge = carry
        n = count - 1 - i
        keep = jnp.where(lax.rem(n + 1, per_seq) == 0, 0.0, 1.0)
        sm = sm_ref[n]
        back = icg_ref[n]
        sg = jnp.concatenate(
            [back * sm[chans : 2 * chans], back * sm[:chans], g_ref[n].astype(F32) * y_ref[n].astype(F32)], axis=0
        )
        r1 = pltpu.roll(sg, LANES - 1, 1)
        r2 = pltpu.roll(sg, LANES - 2, 1)
        s1 = jnp.where(lane < LANES - 1, r1, next1 * keep)
        s2 = jnp.where(lane < LANES - 2, r2, next2 * keep)
        pg_ref[n] = (taps[0] * sg + taps[1] * s1 + taps[2] * s2).astype(BF)
        sent_ref[n] = jnp.concatenate([back, next_edge * keep], axis=0).astype(BF)
        p = p_ref[n].astype(F32)
        return r1, r2, acc0 + sg * p, acc1 + s1 * p, acc2 + s2 * p, edge_of(back)

    zero = jnp.zeros((3 * chans, LANES), F32)
    _, _, acc0, acc1, acc2, _ = lax.fori_loop(0, count, step, (zero,) * 5 + (zero[:GROUP],), unroll=8)
    out = zero
    for k, acc in enumerate((acc0, acc1, acc2)):
        out = jnp.where(lane == k, jnp.sum(acc, axis=1, keepdims=True), out)
    st_ref[...] = out


def filter_spectrum(own, other, tables):
    padded = tables["padded"]
    return pl.pallas_call(
        functools.partial(filter_spectrum_kernel, padded),
        in_specs=vmem_specs(7),
        out_specs=vmem_specs(1)[0],
        out_shape=jax.ShapeDtypeStruct((own.shape[0] * padded, 2 * LANES), F32),
        compiler_params=params(),
        cost_estimate=cost(4 * 10**9, 4 * 10**6),
        name="filter_spectrum",
    )(own, other, *tables["forward"], tables["twiddle"], *tables["second"])


def transforms(tables):
    return (*tables["forward_used"], tables["twiddle"], *tables["second"], *tables["inverse"], *tables["backward_used"])


def conv_forward(x, spectrum, tables, seqs):
    padded = tables["padded"]
    return pl.pallas_call(
        functools.partial(conv_forward_kernel, padded, seqs),
        in_specs=vmem_specs(11),
        out_specs=vmem_specs(2),
        out_shape=[
            jax.ShapeDtypeStruct(x.shape, BF),
            jax.ShapeDtypeStruct((seqs * x.shape[1] * padded, 2 * LANES), F32),
        ],
        compiler_params=params(),
        cost_estimate=cost(5 * 10**9, 6 * 10**6),
        name="conv_forward",
    )(x, spectrum, *transforms(tables))


def conv_backward(gated, mixed, proj, conv_out, saved, taps, spectrum, tables, seqs, real):
    padded = tables["padded"]
    count, chans, _ = gated.shape
    return pl.pallas_call(
        functools.partial(conv_backward_kernel, padded, seqs, real),
        in_specs=vmem_specs(16),
        out_specs=vmem_specs(4),
        out_shape=[
            jax.ShapeDtypeStruct((count, 3 * chans, LANES), BF),
            jax.ShapeDtypeStruct((chans * padded, 2 * LANES), F32),
            jax.ShapeDtypeStruct((3 * chans, LANES), F32),
            jax.ShapeDtypeStruct((count, chans + GROUP, LANES), BF),
        ],
        scratch_shapes=[pltpu.VMEM(gated.shape, F32)],
        compiler_params=params(),
        cost_estimate=cost(7 * 10**9, 9 * 10**6),
        name="conv_backward",
    )(gated, mixed, proj, conv_out, saved, taps, spectrum, *transforms(tables))


def source_of(place, turn, group):
    per_plane, relative = place
    seq = lax.axis_index("seq")
    plane = lax.div(seq, per_plane)
    inside = lax.rem(seq, per_plane)
    half, index = turn
    inner = lax.bitwise_xor(inside, index) if relative else index
    return (lax.bitwise_xor(plane, group) * per_plane + inner) * 2 + lax.bitwise_xor(lax.axis_index("tp"), half)


def own_channels(ref, index, chans):
    model = ref.shape[-1]
    linear = lax.axis_index("seq") * 2 + lax.axis_index("tp")
    first = linear * chans
    window = jnp.minimum(lax.div(first, LANES) * LANES, model - 2 * LANES)
    part = ref[index, :, pl.ds(pl.multiple_of(window, LANES), 2 * LANES)].astype(F32)
    part = pltpu.roll(part, lax.rem(2 * LANES - (first - window), 2 * LANES), 1)
    turned = part[:, :LANES].T
    return turned[: -(-chans // GROUP) * GROUP]


def tap_columns(taps_ref, chans):
    out = []
    for k in range(3):
        cols = own_channels(taps_ref, k, chans)
        out.append(jnp.concatenate([jnp.broadcast_to(cols[:, p : p + 1], (cols.shape[0], LANES)) for p in range(3)], axis=0))
    return out


def channel_mixer_kernel(place, turns, seqs, chans, w_ref, taps_ref, *refs):
    tiles, (p_ref, sm_ref) = refs[:-2], refs[-2:]
    count, rows3, _ = p_ref.shape
    wc = jnp.concatenate([own_channels(w_ref, p, chans) for p in range(3)], axis=0).astype(BF)
    for ref, turn_list in zip(tiles, turns):
        for q, turn in enumerate(turn_list):
            x = jnp.concatenate([ref[4 * q + z] for z in range(4)], axis=1)
            p = mm(wc, x).astype(BF)
            for z in range(4):
                p_ref[source_of(place, turn, z)] = p[:, z * LANES : (z + 1) * LANES]
    per_seq = count // seqs
    taps = tap_columns(taps_ref, chans)
    lane = lax.broadcasted_iota(jnp.int32, (rows3, LANES), 1)

    def step(n, carry):
        last1, last2 = carry
        keep = jnp.where(lax.rem(n, per_seq) == 0, 0.0, 1.0)
        p = p_ref[n].astype(F32)
        r1 = pltpu.roll(p, 1, 1)
        r2 = pltpu.roll(p, 2, 1)
        s1 = jnp.where(lane < 1, last1 * keep, r1)
        s2 = jnp.where(lane < 2, last2 * keep, r2)
        sm_ref[n] = taps[0] * p + taps[1] * s1 + taps[2] * s2
        return r1, r2

    zero = jnp.zeros((rows3, LANES), F32)
    lax.fori_loop(0, count, step, (zero, zero), unroll=8)


def channel_mixer(tiles, turns, place, w, taps, count, seqs, chans):
    rows3 = 3 * (-(-chans // GROUP) * GROUP)
    return pl.pallas_call(
        functools.partial(channel_mixer_kernel, place, turns, seqs, chans),
        in_specs=vmem_specs(2 + len(tiles)),
        out_specs=vmem_specs(2),
        out_shape=[
            jax.ShapeDtypeStruct((count, rows3, LANES), BF),
            jax.ShapeDtypeStruct((count, rows3, LANES), F32),
        ],
        compiler_params=params(),
        cost_estimate=cost(3 * 10**9, 6 * 10**6),
        name="channel_mixer",
    )(w, taps, *tiles)


def channel_grads_kernel(place, turns, padded, count, pg_ref, st_ref, own_ref, other_ref, tw, ih, il, bh, bl, feat_ref, w2_ref,
                         w3_ref, decay_ref, gain_ref, a_ref, ac_ref, b_ref, bc_ref, *refs):
    tiles, (out_ref, g3_ref, keep_ref, lag_ref) = refs[:count], refs[count:]
    total = None
    for ref, turn_list in zip(tiles, turns):
        for q, turn in enumerate(turn_list):
            x = jnp.concatenate([ref[4 * q + z] for z in range(4)], axis=1)
            g = jnp.concatenate([pg_ref[source_of(place, turn, z)] for z in range(4)], axis=1)
            part = mm_nt(g, x)
            total = part if total is None else total + part
    rows3, width = total.shape
    keep_ref[...] = jnp.zeros_like(keep_ref)
    keep_ref[:rows3, :width] = total
    keep_ref[:rows3, width : width + 3] = st_ref[:, :3]

    length = lag_ref.shape[1]
    rows = length // LANES
    used = rows * GROUP
    channels = lag_ref.shape[0] // 2
    groups = channels // GROUP
    begin = pl.multiple_of(lax.axis_index("tp") * used, LANES)
    back = (bh[pl.ds(begin, used), :], bl[pl.ds(begin, used), :])
    for half, ref in enumerate((own_ref, other_ref)):
        (y,) = signal_of(ref[...], (ih[...], il[...]), tw, [back], padded, groups)
        for g in range(groups):
            base = half * channels + g * GROUP
            for n in range(rows):
                lag_ref[base : base + GROUP, n * LANES : (n + 1) * LANES] = y[
                    n * GROUP : (n + 1) * GROUP, g * LANES : (g + 1) * LANES
                ]

    span = min(FILTER_LANES, length)
    begin = lax.axis_index("tp") * length
    w2 = stacked_weights(w2_ref[...])
    w3 = split(own_first(w3_ref))
    decay = decay_columns(decay_ref)
    g1 = g2 = g3 = 0.0
    for lo in range(0, length, span):
        lanes = slice(lo, lo + span)
        start = pl.multiple_of(begin + lo, LANES)
        wh, wl = split(lag_ref[:, lanes] * lag_decay(decay, start, span, length))
        second = b_ref[:, lanes]
        g3 += mm_nt(wh, second) + mm_nt(wl, second)
        pre2 = mm3_tn(w3, (wh, wl)) * bc_ref[:, lanes].astype(F32)
        g2 += mm_nt(a_ref[:, lanes], pre2.astype(BF))
        pre1 = stacked_product(w2, pre2) * ac_ref[:, lanes].astype(F32)
        g1 += mm_nt(feat_ref[:8, pl.ds(start, span)], pre1.astype(BF))
    g3_ref[...] = g3
    more = out_ref.shape[0] - rows3
    gains = [gain_ref[k * LANES : (k + 1) * LANES].reshape(1, LANES) for k in range(gain_ref.shape[0] // LANES)]
    gains += [jnp.zeros((8 - len(gains), LANES), F32)]
    keep_ref[rows3:, :LANES] = g2[:more]
    keep_ref[rows3:, LANES:] = jnp.concatenate([g2[more:], g1] + gains, axis=0)
    out_ref[...] = keep_ref[...].astype(BF)


def channel_grads(tiles, turns, place, pg, st, own, other, tables, features, w2, w3t, decay, gain, saved):
    rows3 = pg.shape[1]
    hidden = w2.shape[0]
    length = features.shape[1] // 2
    return pl.pallas_call(
        functools.partial(channel_grads_kernel, place, turns, tables["padded"], len(tiles)),
        in_specs=vmem_specs(18 + len(tiles)),
        out_specs=vmem_specs(2),
        out_shape=[
            jax.ShapeDtypeStruct((rows3 + SMALL_ROWS, 2 * LANES), BF),
            jax.ShapeDtypeStruct((w3t.shape[0], hidden), F32),
        ],
        scratch_shapes=[
            pltpu.VMEM((rows3 + SMALL_ROWS, 2 * LANES), F32),
            pltpu.VMEM((w3t.shape[0], length), F32),
        ],
        compiler_params=params(),
        cost_estimate=cost(8 * 10**9, 8 * 10**6),
        name="channel_grads",
    )(pg, st, own, other, tables["twiddle"], *tables["inverse"], *tables["backward"], features, w2, w3t, decay, gain,
      *saved, *tiles)


def erf_parts(g):
    x = jnp.abs(g) * (1.0 / math.sqrt(2.0))
    t = 1.0 / (1.0 + 0.3275911 * x)
    e = jnp.exp(-x * x)
    poly = t * (0.254829592 + t * (-0.284496736 + t * (1.421413741 + t * (-1.453152027 + t * 1.061405429))))
    tail = 0.5 * poly * e
    return jnp.where(g < 0, tail, 1.0 - tail), e


def norm_stats(v):
    centered = v - jnp.mean(v, axis=-1, keepdims=True)
    variance = jnp.mean(centered * centered, axis=-1, keepdims=True)
    r = lax.rsqrt(variance + EPSILON)
    return centered * r, r


def norm_backward(w, gain, xhat, r):
    a = w * gain
    return r * (a - jnp.mean(a, axis=-1, keepdims=True) - xhat * jnp.mean(a * xhat, axis=-1, keepdims=True))


def column(j, width):
    return slice(j * width, (j + 1) * width)


def own_part(ref, rows):
    return ref[pl.ds(pl.multiple_of(lax.axis_index("tp") * rows, rows), rows), :]


def mixer_in_kernel(per_plane, seq_length, x_ref, halo_ref, gain_ref, w_ref, taps_ref, og_ref, conv_ref, sm2_ref, proj_ref, start_ref,
                    z0, z1, z2, z3, keep_ref):
    rows = sm2_ref.shape[0]
    width = w_ref.shape[1]
    blocks = w_ref.shape[2] // width
    lead = halo_ref.shape[0]
    linear = lax.axis_index("seq") * 2 + lax.axis_index("tp")
    keep = jnp.where(lax.rem(linear * rows, seq_length) == 0, 0.0, 1.0)
    inner = x_ref[rows - lead : rows, :].astype(F32)
    halo = jnp.where(lax.axis_index("tp") == 0, halo_ref[...].astype(F32), inner) * keep
    x = jnp.concatenate([halo, own_part(x_ref, rows).astype(F32)], axis=0)
    xhat, _ = norm_stats(x)
    normed = xhat * gain_ref[...].reshape(1, -1)
    n1 = normed.astype(BF)
    mixed = []
    for p in range(3):
        proj = jnp.concatenate(
            [mm(n1[:, column(j, width)], w_ref[p, :, column(j, width)]) for j in range(blocks)], axis=1
        )
        low = proj.astype(BF)
        if p < 2:
            proj_ref[p] = low
        proj = low.astype(F32)
        mixed.append(
            taps_ref[0, p : p + 1, :] * proj[lead : lead + rows]
            + taps_ref[1, p : p + 1, :] * proj[lead - 1 : lead - 1 + rows]
            + taps_ref[2, p : p + 1, :] * proj[lead - 2 : lead - 2 + rows]
        )
    sm2_ref[...] = mixed[2]
    start_ref[:8, :] = mixed[0][:8]
    start_ref[8:, :] = mixed[1][:8]
    conv_ref[...] = (mixed[0] * mixed[1]).T.astype(BF)
    nt = normed[lead : lead + rows].T.astype(BF)
    ot = og_ref[...].astype(F32).T.astype(BF)
    for j in range(blocks):
        keep_ref[j, :width, :] = nt[column(j, width)]
        keep_ref[j, width:, :] = ot[column(j, width)]
    plane = lax.div(lax.axis_index("seq"), per_plane)
    for d, out in enumerate((z0, z1, z2, z3)):
        out[...] = keep_ref[lax.bitwise_xor(plane, d)]


def mixer_in(x, halo, gain, w, taps, og, per_plane, seq_length):
    rows, model = og.shape
    width = w.shape[1]
    return pl.pallas_call(
        functools.partial(mixer_in_kernel, per_plane, seq_length),
        in_specs=vmem_specs(6),
        out_specs=vmem_specs(8),
        out_shape=[
            jax.ShapeDtypeStruct((model, rows), BF),
            jax.ShapeDtypeStruct((rows, model), F32),
            jax.ShapeDtypeStruct((2, rows + halo.shape[0], model), BF),
            jax.ShapeDtypeStruct((16, model), F32),
        ]
        + [jax.ShapeDtypeStruct((2 * width, rows), BF)] * 4,
        scratch_shapes=[pltpu.VMEM((model // width, 2 * width, rows), BF)],
        compiler_params=params(24),
        cost_estimate=cost(4 * 10**9, 4 * 10**6),
        name="mixer_in",
    )(x, halo, gain, w, taps, og)


def glu_block(x, og, w_pairs, d_pairs):
    down = None
    back = None
    for (wg, wu), wd in zip(w_pairs, d_pairs):
        gate = mm(x, wg)
        up = mm(x, wu)
        phi, e = erf_parts(gate)
        act = gate * phi
        hidden = (act * up).astype(BF)
        hg = mm_nt(og, wd)
        slope = phi + gate * (e * (1.0 / math.sqrt(2.0 * math.pi)))
        gg = (hg * up * slope).astype(BF)
        ug = (hg * act).astype(BF)
        down_part = mm(hidden, wd)
        back_part = mm_nt(gg, wg) + mm_nt(ug, wu)
        down = down_part if down is None else down + down_part
        back = back_part if back is None else back + back_part
    return down, back


def middle_kernel(per_plane, conv_ref, sm2_ref, start_ref, x_ref, og_ref, gain_ref, wo_ref, ga_ref, gb_ref, da_ref, db_ref,
                  gg_ref, mid_ref, out_ref, wo_own, wo_other, gain_out, third_ref, edge_ref, z0, z1, z2, z3, keep_ref):
    width = wo_ref.shape[0]
    blocks = wo_ref.shape[1] // width
    conv = conv_ref[...].astype(F32).T
    gated = sm2_ref[...] * conv
    gated_low = gated.astype(BF)
    branch = jnp.concatenate(
        [mm(gated_low[:, column(j, width)], wo_ref[:, column(j, width)]) for j in range(blocks)], axis=1
    )
    middle = own_part(x_ref, conv.shape[0]).astype(F32) + branch
    gain = gain_ref[...].reshape(1, -1)
    xhat, r = norm_stats(middle)
    normed = xhat * gain
    n2 = normed.astype(BF)
    og = og_ref[...]
    downs, backs = [], []
    for j in range(blocks):
        down, back = glu_block(
            n2[:, column(j, width)],
            og[:, column(j, width)],
            [(ga_ref[j, 0], ga_ref[j, 1]), (gb_ref[j, 0], gb_ref[j, 1])],
            [da_ref[:, column(j, width)], db_ref[:, column(j, width)]],
        )
        downs.append(down)
        backs.append(back)
    out_ref[...] = (middle + jnp.concatenate(downs, axis=1)).astype(BF)
    n2_grad = jnp.concatenate(backs, axis=1)
    mid_grad = og.astype(F32) + norm_backward(n2_grad, gain, xhat, r)
    mid_ref[...] = mid_grad
    bg = mid_grad.astype(BF)
    gated_grad = jnp.concatenate(
        [mm_nt(bg[:, column(j, width)], wo_ref[:, column(j, width)]) for j in range(blocks)], axis=1
    )
    gg_ref[...] = gated_grad.T.astype(BF)
    third = gated_grad * conv
    third_ref[...] = third
    edge_ref[:8, :] = third[:8]
    edge_ref[8:, :] = start_ref[...]
    gain_out[...] = jnp.sum(n2_grad * xhat, axis=0, keepdims=True).reshape(-1)
    weight = jnp.concatenate(
        [mm_tn(gated_low[:, column(j, width)], bg[:, column(j, width)]) for j in range(blocks)], axis=1
    )
    lanes = wo_own.shape[1]
    first = lax.axis_index("tp") == 0
    wo_own[...] = jnp.where(first, weight[:, :lanes], weight[:, lanes:]).astype(BF)
    wo_other[...] = jnp.where(first, weight[:, lanes:], weight[:, :lanes]).astype(BF)
    turned = normed.T.astype(BF)
    for j in range(blocks):
        keep_ref[j] = turned[column(j, width)]
    plane = lax.div(lax.axis_index("seq"), per_plane)
    for d, out in enumerate((z0, z1, z2, z3)):
        out[...] = keep_ref[lax.bitwise_xor(plane, d)]


def middle_part(conv, sm2, start, x, og, gain, wo, ga, gb, da, db, per_plane):
    rows, model = og.shape
    width = wo.shape[0]
    return pl.pallas_call(
        functools.partial(middle_kernel, per_plane),
        in_specs=vmem_specs(11),
        out_specs=vmem_specs(12),
        out_shape=[
            jax.ShapeDtypeStruct((model, rows), BF),
            jax.ShapeDtypeStruct((rows, model), F32),
            jax.ShapeDtypeStruct((rows, model), BF),
            jax.ShapeDtypeStruct((width, model // 2), BF),
            jax.ShapeDtypeStruct((width, model // 2), BF),
            jax.ShapeDtypeStruct((model,), F32),
            jax.ShapeDtypeStruct((rows, model), F32),
            jax.ShapeDtypeStruct((24, model), F32),
        ]
        + [jax.ShapeDtypeStruct((width, rows), BF)] * 4,
        scratch_shapes=[pltpu.VMEM((model // width, width, rows), BF)],
        compiler_params=params(),
        cost_estimate=cost(9 * 10**9, 6 * 10**6),
        name="middle_part",
    )(conv, sm2, start, x, og, gain, wo, ga, gb, da, db)


def glu_grad_kernel(per_plane, za, zb, zc, zd, oa, ob, oc, od, ga_ref, gb_ref, da_ref, db_ref, own_ref, other_ref):
    j = lax.div(lax.axis_index("seq"), per_plane)
    width = ga_ref.shape[2]
    xt = jnp.concatenate([ref[...] for ref in (za, zb, zc, zd)], axis=1)
    ot = jnp.concatenate([ref[width:, :] for ref in (oa, ob, oc, od)], axis=1)
    x = xt.astype(F32).T.astype(BF)
    og = ot.astype(F32).T.astype(BF)
    for g_ref, d_ref, out_ref in ((gb_ref, db_ref, other_ref), (ga_ref, da_ref, own_ref)):
        wg, wu = g_ref[j, 0], g_ref[j, 1]
        wd = d_ref[:, :width]
        for k in range(1, d_ref.shape[1] // width):
            wd = jnp.where(j == k, d_ref[:, column(k, width)], wd)
        gate = mm(x, wg)
        up = mm(x, wu)
        phi, e = erf_parts(gate)
        act = gate * phi
        hidden = (act * up).astype(BF)
        hg = mm_nt(og, wd)
        slope = phi + gate * (e * (1.0 / math.sqrt(2.0 * math.pi)))
        out_ref[0:width, :] = mm(xt, (hg * up * slope).astype(BF)).astype(out_ref.dtype)
        out_ref[width : 2 * width, :] = mm(xt, (hg * act).astype(BF)).astype(out_ref.dtype)
        out_ref[2 * width : 3 * width, :] = mm(ot, hidden).astype(out_ref.dtype)


def glu_grads(z_parts, o_parts, ga, gb, da, db, per_plane):
    width, half = ga.shape[2:]
    return pl.pallas_call(
        functools.partial(glu_grad_kernel, per_plane),
        in_specs=vmem_specs(12),
        out_specs=vmem_specs(2),
        out_shape=[
            jax.ShapeDtypeStruct((3 * width, half), F32),
            jax.ShapeDtypeStruct((3 * width, half), BF),
        ],
        compiler_params=params(40),
        cost_estimate=cost(9 * 10**9, 4 * 10**6),
        name="glu_grads",
    )(*z_parts, *o_parts, ga, gb, da, db)


def plane_add_kernel(own_ref, other_ref, mine_ref, theirs_ref, out_ref):
    total = (own_ref[...] + other_ref[...].astype(F32)).astype(BF)
    extra = (mine_ref[...].astype(F32) + theirs_ref[...].astype(F32)).astype(BF)
    count = out_ref.shape[0]
    rows, more = total.shape[0] // count, extra.shape[0] // count
    for k in range(count):
        out_ref[k, :rows, :] = total[k * rows : (k + 1) * rows]
        out_ref[k, rows:, :] = extra[k * more : (k + 1) * more]


def plane_add(own, other, mine, theirs, count):
    half = own.shape[1]
    rows = (own.shape[0] + mine.shape[0]) // count
    return pl.pallas_call(
        plane_add_kernel,
        in_specs=vmem_specs(4),
        out_specs=vmem_specs(1)[0],
        out_shape=jax.ShapeDtypeStruct((count, rows, half), BF),
        compiler_params=params(8),
        cost_estimate=cost(10**8, 2 * 10**6),
        name="plane_add",
    )(own, other, mine, theirs)


def plane_join_kernel(cut, a0, a1, a2, a3, out_ref):
    refs = (a0, a1, a2, a3)
    last = sum(ref[cut:, :].astype(F32) for ref in refs).astype(BF)
    if len(out_ref.shape) == 2:
        for z, ref in enumerate(refs):
            out_ref[z * cut : (z + 1) * cut, :] = ref[:cut, :]
        out_ref[4 * cut :, :] = last
        return
    for k in range(out_ref.shape[0]):
        for z, ref in enumerate(refs):
            out_ref[k, z * cut : (z + 1) * cut, :] = ref[:cut, :]
        out_ref[k, 4 * cut :, :] = last


def plane_join(parts, cut, copies=()):
    rows, half = parts[0].shape
    return pl.pallas_call(
        functools.partial(plane_join_kernel, cut),
        in_specs=vmem_specs(4),
        out_specs=vmem_specs(1)[0],
        out_shape=jax.ShapeDtypeStruct((*copies, 3 * cut + rows, half), BF),
        compiler_params=params(8),
        cost_estimate=cost(10**8, 2 * 10**6),
        name="plane_join",
    )(*parts)


def plane_sum_kernel(x_ref, out_ref):
    out_ref[...] = sum(x_ref[k].astype(F32) for k in range(x_ref.shape[0])).astype(BF)


def plane_sum(parts):
    return pl.pallas_call(
        plane_sum_kernel,
        in_specs=vmem_specs(1),
        out_specs=vmem_specs(1)[0],
        out_shape=jax.ShapeDtypeStruct(parts.shape[1:], BF),
        compiler_params=params(8),
        cost_estimate=cost(8 * 10**11, 2 * 10**6),
        name="plane_sum",
    )(parts)


def finish_kernel(per_plane, width, a_ref, half_ref, back_ref,
                  gi_ref, go_ref, in_ref, keep_ref):
    seq = lax.axis_index("seq")
    plane = lax.div(seq, per_plane)
    blocks, pieces, cut, half = keep_ref.shape
    for k in range(pieces):
        for z in range(blocks):
            keep_ref[lax.bitwise_xor(plane, z), k] = a_ref[k, z * cut : (z + 1) * cut, :].astype(F32)
    outs = []
    for j in range(blocks):
        block = jnp.concatenate([keep_ref[j, k] for k in range(pieces)], axis=0)
        gi_ref[j, :, 0, :] = block[:width]
        gi_ref[j, :, 1, :] = block[width : 2 * width]
        outs.append(block[2 * width : 3 * width].T)
    go_ref[...] = jnp.concatenate(outs, axis=1)
    count = half_ref.shape[0]
    me = lax.axis_index("tp")
    in_ref[pl.ds(pl.multiple_of(me * count, count), count), :] = half_ref[...]
    in_ref[pl.ds(pl.multiple_of((1 - me) * count, count), count), :] = back_ref[...]


def finish(sums, half_rows, other_rows, per_plane, width):
    half = sums.shape[2]
    model = 4 * width
    return pl.pallas_call(
        functools.partial(finish_kernel, per_plane, width),
        in_specs=vmem_specs(3),
        out_specs=vmem_specs(3),
        out_shape=[
            jax.ShapeDtypeStruct((4, width, 2, half), F32),
            jax.ShapeDtypeStruct((half, model), F32),
            jax.ShapeDtypeStruct((2 * half_rows.shape[0], model), BF),
        ],
        scratch_shapes=[pltpu.VMEM((4, 4, 3 * width // 4, half), F32)],
        compiler_params=params(32),
        cost_estimate=cost(10**8, 6 * 10**6),
        name="finish",
    )(sums, half_rows, other_rows)


def out_unpack_kernel(mine_ref, theirs_ref, wo_ref):
    first = lax.axis_index("tp") == 0
    mine, theirs = mine_ref[...].astype(F32), theirs_ref[...].astype(F32)
    left, right = jnp.where(first, mine, theirs), jnp.where(first, theirs, mine)
    _, cut, lanes = left.shape
    for k in range(left.shape[0]):
        wo_ref[k * cut : (k + 1) * cut, :lanes] = left[k]
        wo_ref[k * cut : (k + 1) * cut, lanes:] = right[k]


def out_unpack(mine, theirs):
    count, rows, lanes = mine.shape
    return pl.pallas_call(
        out_unpack_kernel,
        in_specs=vmem_specs(2),
        out_specs=vmem_specs(1)[0],
        out_shape=jax.ShapeDtypeStruct((count * rows, 2 * lanes), F32),
        compiler_params=params(8),
        cost_estimate=cost(10**8, 10**6),
        name="out_unpack",
    )(mine, theirs)


def in_unpack_kernel(place, w_ref, gain_ref, *refs):
    tiles, (gi_ref, st_ref, gain_out, w1_ref, b1_ref, w2_ref, gain2_ref, keep_ref) = refs[:-8], refs[-8:]
    _, width, model = gi_ref.shape
    count, rows3, _ = keep_ref.shape
    small = None
    for k, ref in enumerate(tiles):
        half, z = divmod(k, 4)
        for inner in range(4):
            keep_ref[source_of(place, (half, inner), z)] = ref[inner * rows3 : (inner + 1) * rows3, :].astype(F32)
        part = ref[4 * rows3 :, :].astype(F32)
        small = part if small is None else small + part
    hidden = w2_ref.shape[0]
    more = small.shape[0]
    w2_ref[:more, :] = small[:, :LANES]
    w2_ref[more:, :] = small[: hidden - more, LANES:]
    rest = small[hidden - more : hidden - more + 8, LANES:]
    w1_ref[...] = rest[:5]
    b1_ref[...] = rest[5:6].reshape(-1)
    rest = small[hidden - more + 8 :, LANES:]
    for k in range(model // LANES):
        gain2_ref[k * LANES : (k + 1) * LANES] = rest[k : k + 1].reshape(-1)
    chans = rows3 // 3
    blocks = model // width
    per_block = count // blocks
    gains = []
    for j in range(blocks):
        acc = None
        for p in range(3):
            got = jnp.concatenate(
                [keep_ref[j * per_block + k, p * chans : (p + 1) * chans, :] for k in range(per_block)], axis=0
            )
            turned = got.T
            gi_ref[p, :, column(j, width)] = turned[:width]
            for k in range(3):
                st_ref[k, p : p + 1, column(j, width)] = turned[width + k : width + k + 1]
            part = turned[:width] * w_ref[p, :, column(j, width)].astype(F32)
            acc = part if acc is None else acc + part
        gains.append(jnp.sum(acc.T, axis=0, keepdims=True))
    gain_out[...] = (jnp.concatenate(gains, axis=1) / gain_ref[...].reshape(1, -1)).reshape(-1)


def in_unpack(tiles, place, w, gain):
    rows3 = (tiles[0].shape[0] - SMALL_ROWS) // 4
    hidden = LANES
    count = 4 * len(tiles)
    _, width, model = w.shape
    return pl.pallas_call(
        functools.partial(in_unpack_kernel, place),
        in_specs=vmem_specs(2 + len(tiles)),
        out_specs=vmem_specs(7),
        out_shape=[
            jax.ShapeDtypeStruct((3, width, model), F32),
            jax.ShapeDtypeStruct((3, 3, model), F32),
            jax.ShapeDtypeStruct((model,), F32),
            jax.ShapeDtypeStruct((5, hidden), F32),
            jax.ShapeDtypeStruct((hidden,), F32),
            jax.ShapeDtypeStruct((hidden, hidden), F32),
            jax.ShapeDtypeStruct((model,), F32),
        ],
        scratch_shapes=[pltpu.VMEM((count, rows3, 2 * LANES), F32)],
        compiler_params=params(24),
        cost_estimate=cost(10**8, 4 * 10**6),
        name="in_unpack",
    )(w, gain, *tiles)


def short_mix(proj_ref, taps_ref, p, rows):
    lead = proj_ref.shape[1] - rows
    proj = proj_ref[p].astype(F32)
    return (
        taps_ref[0, p : p + 1, :] * proj[lead:]
        + taps_ref[1, p : p + 1, :] * proj[lead - 1 : lead - 1 + rows]
        + taps_ref[2, p : p + 1, :] * proj[lead - 2 : lead - 2 + rows]
    )


def mixer_back_kernel(chans, seq_length, *refs):
    *grad_refs, third_ref, edge_ref, proj_ref, taps_ref, mid_ref, x_ref, gain_ref, w_ref, in_ref = refs
    rows, model = mid_ref.shape
    width = w_ref.shape[1]
    blocks = model // width
    if len(grad_refs) == 1:
        got = grad_refs[0][...].astype(F32)
        count = got.shape[0]
        main = got[:, :chans, :].reshape(count * chans, rows)
        tiles = []
        for k in range(count):
            tile = got[k, chans:, :]
            for a in range(chans // GROUP):
                tiles.append(pltpu.roll(tile, LANES - 2 * a, 1) if a else tile)
        tail = jnp.concatenate(tiles, axis=0)
    else:
        main, tail = grad_refs[0][...].astype(F32), grad_refs[1][...].astype(F32)
    back = jnp.concatenate([main.T, tail.T[:8]], axis=0)
    linear = lax.axis_index("seq") * 2 + lax.axis_index("tp")
    keep = jnp.where(lax.rem((linear + 1) * rows, seq_length) == 0, 0.0, 1.0)
    third = jnp.concatenate([third_ref[...], edge_ref[:8, :] * keep], axis=0)
    mixed = [
        jnp.concatenate([short_mix(proj_ref, taps_ref, p, rows), edge_ref[8 * p + 8 : 8 * p + 16, :]], axis=0)
        for p in range(2)
    ]
    total = [None] * blocks
    for p, sg in enumerate((back * mixed[1], back * mixed[0], third)):
        pg = (
            taps_ref[0, p : p + 1, :] * sg[:rows]
            + taps_ref[1, p : p + 1, :] * sg[1 : rows + 1]
            + taps_ref[2, p : p + 1, :] * sg[2 : rows + 2]
        ).astype(BF)
        for j in range(blocks):
            part = mm_nt(pg[:, column(j, width)], w_ref[p, :, column(j, width)])
            total[j] = part if total[j] is None else total[j] + part
    n1_grad = jnp.concatenate(total, axis=1)
    xhat, r = norm_stats(own_part(x_ref, rows).astype(F32))
    in_ref[...] = (mid_ref[...] + norm_backward(n1_grad, gain_ref[...].reshape(1, -1), xhat, r)).astype(BF)


def mixer_back(grads, third, edge, proj, taps, mid, x, gain, w, chans, seq_length):
    return pl.pallas_call(
        functools.partial(mixer_back_kernel, chans, seq_length),
        in_specs=vmem_specs(8 + len(grads)),
        out_specs=vmem_specs(1)[0],
        out_shape=jax.ShapeDtypeStruct(mid.shape, BF),
        compiler_params=params(BACK_MIB),
        cost_estimate=cost(3 * 10**9, 4 * 10**6),
        name="mixer_back",
    )(*grads, third, edge, proj, taps, mid, x, gain, w)


def after(x, *others):
    return lax.optimization_barrier((x,) + others)[0]


def permuted(x, axes, count, by):
    pairs = [(i, i + by) for i in range(count) if 0 <= i + by < count]
    return lax.ppermute(x, axes, pairs)


def swapped(x):
    return lax.ppermute(x, "tp", [(0, 1), (1, 0)])


def crossed(x, mask):
    devices = lax.axis_size("seq")
    return lax.ppermute(x, "seq", [(i, i ^ mask) for i in range(devices)])


def exchanged(x, axes, groups=None):
    return lax.all_to_all(x, axes, 0, 0, axis_index_groups=groups, tiled=True)


def gathered_over(x, count, groups=None):
    return exchanged(jnp.broadcast_to(x[None], (count,) + x.shape), "seq", groups)


def local(
    layer_input,
    mixer_gain,
    in_proj,
    short_taps,
    filter_w1,
    filter_b1,
    filter_w2,
    filter_w3,
    filter_decay,
    out_proj,
    glu_gain,
    glu_in,
    glu_out,
    out_grad,
):
    tok_rows, model = layer_input.shape
    width = in_proj.shape[0]
    blocks = model // width
    half = glu_out.shape[0]
    seq_devices = lax.axis_size("seq")
    tp_devices = lax.axis_size("tp")
    devices = seq_devices * tp_devices
    both = ("seq", "tp")
    rows = tok_rows // tp_devices
    seq_length = min(MIN_LEN, tok_rows * seq_devices)
    seqs = tok_rows * seq_devices // seq_length
    per_plane = seq_devices // blocks
    quick = per_plane == 4 and not SLOW_PATH
    place = (per_plane, quick)
    chans = model // devices
    chans_padded = -(-chans // GROUP) * GROUP
    spare = chans_padded - chans
    hidden = filter_w2.shape[0]
    tp_index = lax.axis_index("tp")
    linear = lax.axis_index("seq") * tp_devices + tp_index
    tables = transform_tables(seq_length)
    features = feature_table(seq_length)
    within = [[g * per_plane + r for r in range(per_plane)] for g in range(blocks)]

    halo = permuted(layer_input[tok_rows - 16 :], "seq", seq_devices, 1)

    w3t = filter_w3.T.reshape(tp_devices, chans, hidden)
    w3t = jnp.pad(w3t, ((0, 0), (0, spare), (0, 0))).reshape(tp_devices * chans_padded, hidden)
    decay = jnp.pad(filter_decay.reshape(tp_devices, chans), ((0, 0), (0, spare))).reshape(-1)
    lag_own, lag_other, *saved = filter_forward(features, filter_w1, filter_b1, filter_w2, w3t, decay)
    lag_back = swapped(lag_other)

    w_in = in_proj.transpose(1, 0, 2)
    conv_rows, sm2, proj_rows, start_rows, *sent = mixer_in(
        layer_input, after(halo, lag_own), mixer_gain, w_in, short_taps, out_grad, per_plane, seq_length
    )

    def to_channels(x):
        out = exchanged(x.reshape(devices, chans, rows), both)
        return jnp.pad(out, ((0, 0), (0, spare), (0, 0)))

    def to_tokens(x):
        return exchanged(x[:, :chans], both).reshape(model, rows)

    conv_channels = to_channels(conv_rows)
    early = [sent[0]] + [crossed(sent[d], d * per_plane) for d in range(1, blocks)]
    glu_own = after(glu_in, conv_rows).transpose(0, 2, 1, 3)
    down_own = after(glu_out, conv_rows)
    glu_other = swapped(glu_own)
    down_other = swapped(down_own)
    spectrum = filter_spectrum(after(lag_own, glu_own), lag_back, tables)
    conv_out, signal_spec = conv_forward(after(conv_channels, spectrum), spectrum, tables, seqs)
    conv_tokens = to_tokens(conv_out)

    early = [after(x, conv_out) for x in early]
    rows_in = jnp.stack([x[:width] for x in early])
    if quick:
        plane_tiles = [rows_in] + [crossed(rows_in, d) for d in range(1, per_plane)]
        turns = [[(0, d)] for d in range(per_plane)]
    else:
        plane_tiles = [gathered_over(rows_in, per_plane, within).reshape(per_plane * blocks, width, rows)]
        turns = [[(0, r) for r in range(per_plane)]]
    gated_grad, mid, layer_output, extra, extra_other, gain_sum, third, edge, *sent = middle_part(
        conv_tokens, sm2, start_rows, layer_input, out_grad, glu_gain, out_proj, glu_own, glu_other,
        down_own, down_other, per_plane
    )
    gated_channels = to_channels(gated_grad)
    across = lambda parts: [parts[0]] + [crossed(parts[d], d * per_plane) for d in range(1, blocks)]
    late = across(sent)
    extra_back = swapped(extra_other)
    edge = permuted(edge, both, devices, -1)
    plane_tiles = [after(x, gated_grad) for x in plane_tiles]
    tiles = plane_tiles + [swapped(x) for x in plane_tiles]
    turns = turns + [[(1, r) for _, r in t] for t in turns]
    turns = tuple(tuple(t) for t in turns)
    proj_channels, mixed_channels = channel_mixer(tiles, turns, place, w_in, short_taps, devices, seqs, chans)

    late = [after(x, proj_channels, gated_channels) for x in late]
    g_own, g_other = glu_grads(late, early, glu_own, glu_other, down_own, down_other, per_plane)
    g_back = swapped(g_other)
    if quick:
        to_sum = plane_add(g_own, g_back, extra, extra_back, per_plane)
        sums = exchanged(to_sum, "seq", within)
        gated_channels = after(gated_channels, to_sum)

    pg, cross, tap_sums, icg = conv_backward(
        after(gated_channels, g_own), mixed_channels, proj_channels, conv_out, signal_spec, short_taps, spectrum, tables,
        seqs, chans
    )
    icg_tokens = exchanged(after(icg, sums) if quick else icg, both)

    if quick:
        glu_piece = plane_sum(after(sums, pg))
        glu_parts = across([glu_piece] * blocks)
        tap_sums = after(tap_sums, glu_piece)
    cross_back = swapped(cross)
    in_piece, g3 = channel_grads(
        tiles, turns, place, pg, tap_sums, cross, cross_back, tables, features, filter_w2, w3t, decay, gain_sum, saved
    )
    g3_back = swapped(g3)
    if quick:
        in_parts = [in_piece] + [crossed(in_piece, d) for d in range(1, per_plane)]
        glu_parts = plane_join([after(x, in_piece) for x in glu_parts], 3 * width // per_plane, (per_plane,))
        icg_tokens = after(icg_tokens, glu_parts)
    if chans == chans_padded:
        grads = [icg_tokens]
    else:
        grads = [
            icg_tokens[:, :chans].reshape(model, rows),
            icg_tokens[:, chans_padded : chans_padded + chans].reshape(model, rows),
        ]
    input_half = mixer_back(
        grads, third, edge, proj_rows, short_taps, mid, layer_input, mixer_gain, w_in, chans, seq_length
    )
    input_other = swapped(input_half)

    if quick:
        in_parts = plane_join([after(x, input_half) for x in in_parts], 3 * chans_padded)
        in_full = across([in_parts] * blocks)
        glu_full = exchanged(after(glu_parts, in_parts), "seq", within)
        in_full = in_full + [swapped(x) for x in in_full]
        in_proj_grad, short_taps_grad, mixer_gain_grad, w1_grad, b1_grad, w2_grad, glu_gain_grad = in_unpack(
            in_full, place, w_in, mixer_gain
        )
        glu_full = after(glu_full, glu_gain_grad)
        out_mine = glu_full[:, 3 * width :, :]
        out_theirs = swapped(out_mine)
        glu_in_grad, glu_out_grad, input_grad = finish(
            after(glu_full, out_mine), input_half, input_other, per_plane, width
        )
        out_proj_grad = out_unpack(out_mine, after(out_theirs, glu_out_grad))
        in_proj_grad = in_proj_grad.transpose(1, 0, 2)
    else:
        total = (g_own + g_back.astype(F32)).astype(BF)
        piece = exchanged(total, "seq", within).reshape(per_plane, -1, half)
        piece = jnp.sum(piece.astype(F32), axis=0).astype(BF)
        full = gathered_over(piece, seq_devices).reshape(blocks, -1, half).astype(F32)
        glu_in_grad = full[:, : 2 * width].reshape(blocks, 2, width, half).transpose(0, 2, 1, 3)
        glu_out_grad = full[:, 2 * width :].transpose(2, 0, 1).reshape(half, model)
        total = (extra.astype(F32) + extra_back.astype(F32)).astype(BF)
        piece = exchanged(total.reshape(seq_devices, -1), "seq")
        piece = jnp.sum(piece.astype(F32), axis=0).astype(BF)
        mine = gathered_over(piece, seq_devices).reshape(width, model // 2).astype(F32)
        theirs = swapped(mine)
        out_proj_grad = jnp.where(
            tp_index == 0, jnp.concatenate([mine, theirs], axis=1), jnp.concatenate([theirs, mine], axis=1)
        )
        mine = gathered_over(in_piece, seq_devices)
        theirs = swapped(mine)
        pair = jnp.where(tp_index == 0, jnp.stack([mine, theirs], 1), jnp.stack([theirs, mine], 1)).astype(F32)
        pair = pair.reshape(devices, -1, 2 * LANES)
        small = jnp.sum(pair[:, 3 * chans_padded :], axis=0)
        small = jnp.concatenate([small[:, :LANES], small[:, LANES:]], axis=0)
        w1_grad, b1_grad, w2_grad = small[hidden : hidden + 5], small[hidden + 5], small[:hidden]
        glu_gain_grad = small[hidden + 8 : hidden + 8 + model // LANES].reshape(model)
        pair = pair[:, : 3 * chans_padded].reshape(devices, 3, chans_padded, 2 * LANES)[:, :, :chans]
        pair = pair.transpose(1, 0, 2, 3).reshape(3, model, 2 * LANES)
        in_proj_grad = pair[:, :, :width].transpose(2, 0, 1)
        short_taps_grad = pair[:, :, width : width + 3].transpose(2, 0, 1)
        products = in_proj_grad * in_proj.astype(F32)
        products = jnp.sum(products.reshape(width, 3, blocks, width), axis=(1, 3))
        mixer_gain_grad = products.T.reshape(model) / mixer_gain
        input_grad = jnp.where(
            tp_index == 0,
            jnp.concatenate([input_half, input_other], axis=0),
            jnp.concatenate([input_other, input_half], axis=0),
        )

    mine = g3[:chans] + g3_back[chans_padded : chans_padded + chans]
    theirs = g3[chans_padded : chans_padded + chans] + g3_back[:chans]
    g3_full = jnp.where(
        tp_index == 0, jnp.concatenate([mine, theirs], axis=0), jnp.concatenate([theirs, mine], axis=0)
    ).T
    return (
        layer_output,
        input_grad,
        mixer_gain_grad,
        in_proj_grad,
        short_taps_grad,
        w1_grad,
        b1_grad,
        w2_grad,
        g3_full,
        out_proj_grad,
        glu_gain_grad,
        glu_in_grad,
        glu_out_grad,
    )


def solution(mesh):
    placed = (
        P("seq", None),
        P(),
        P(),
        P(),
        P(),
        P(),
        P(),
        P(None, "seq"),
        P("seq"),
        P(),
        P(),
        P(None, None, None, "tp"),
        P("tp", None),
        P(("seq", "tp"), None),
    )
    return jax.shard_map(
        local,
        mesh=mesh,
        in_specs=placed,
        out_specs=(
            P(("seq", "tp"), None),
            P("seq", None),
            P(),
            P(),
            P(),
            P(),
            P(),
            P(),
            P(None, "seq"),
            P(),
            P(),
            P(None, None, None, "tp"),
            P("tp", None),
        ),
        check_vma=False,
    )
```
